32 devices in a mesh: wide: 8 (over y, x, core), tp: 4 (over z).
Axes of the slice: x: 2, y: 2, z: 4, core: 2. Of those that a mesh axis runs over, the one named last changes fastest.
Arguments:
- tokens: bfloat16 [17408, 2048], P(('wide', 'tp')), may hold values from -6 to 6
- out_grad: bfloat16 [17408, 2048], P(('wide', 'tp')), may hold values from -6 to 6
- seg_ids: int32 [17408], P('wide'), may hold values from 0 to 71, as said below
- parent_table: int32 [72], P('wide'), may hold values from 0 to 71, as said below
- path_pos: int32 [17408], P('wide'), may hold values from 0 to 1407, as said below
- attn_gain: bfloat16 [2048], P('wide'), may hold values from 0.099609375 to 1.8984375
- w_query: bfloat16 [2048, 2048], P('wide', 'tp'), may hold values from -0.125 to 0.125
- w_key: bfloat16 [2048, 1024], P('wide', 'tp'), may hold values from -0.125 to 0.125
- w_value: bfloat16 [2048, 1024], P('wide', 'tp'), may hold values from -0.125 to 0.125
- w_out: bfloat16 [2048, 2048], P('tp', 'wide'), may hold values from -2 to 2
- q_gain: bfloat16 [128], P('wide'), may hold values from 0.099609375 to 1.8984375
- k_gain: bfloat16 [128], P('wide'), may hold values from 0.099609375 to 1.8984375
- ffn_gain: bfloat16 [2048], P('wide'), may hold values from 0.099609375 to 1.8984375
- w_gate: bfloat16 [2048, 6144], P('wide', 'tp'), may hold values from -0.125 to 0.125
- w_up: bfloat16 [2048, 6144], P('wide', 'tp'), may hold values from -0.125 to 0.125
- w_down: bfloat16 [6144, 2048], P('tp', 'wide'), may hold values from -0.078125 to 0.078125
Outputs:
- mixed: bfloat16 [17408, 2048], P(('wide', 'tp'))
- tokens_grad: bfloat16 [17408, 2048], P(('wide', 'tp'))
- attn_gain_grad: float32 [2048], P('wide')
- w_query_grad: float32 [2048, 2048], P('wide', 'tp')
- w_key_grad: float32 [2048, 1024], P('wide', 'tp')
- w_value_grad: float32 [2048, 1024], P('wide', 'tp')
- w_out_grad: float32 [2048, 2048], P('tp', 'wide')
- q_gain_grad: float32 [128], P('wide')
- k_gain_grad: float32 [128], P('wide')
- ffn_gain_grad: float32 [2048], P('wide')
- w_gate_grad: float32 [2048, 6144], P('wide', 'tp')
- w_up_grad: float32 [2048, 6144], P('wide', 'tp')
- w_down_grad: float32 [6144, 2048], P('tp', 'wide')
The draws below stay inside these ranges and needn't reach their ends.
Inputs may be any that keep to these rules, and one draw needn't show every extreme that they name: `seg_ids`: tokens come as whole trees of 2176: first a trunk of 1152 tokens (segment tree * 9), then 2 * 4 blocks of 128 tokens, each a segment of its own with an id of tree * 9 + 1 to tree * 9 + 2 * 4, in drawn order. `parent_table`: A trunk is its own parent; 4 blocks of each tree are branches whose parent is the trunk, the others are leaves, one under each branch. The segment tree * 9 + 2 * 4 is a branch. `path_pos`: the trunk's t-th token is at t, a branch's t-th at 1152 + t, a leaf's t-th at 1280 + t.
All inputs are finite; a program needn't handle non-finite values.
Results may differ from the reference program's by a relative error of at most 0.025.
Values may be sent and summed in bfloat16 or wider, within the bound.
A program may use at most 320 MiB of HBM per device.

```python
import jax
import jax.numpy as jnp
from jax import lax

D = 2048
HEADS = 16
KV_HEADS = 8
HEAD_DIM = 128
FF = 6144
TRUNK = 1152
BRANCH_LEN = 128
FORKS = 4
NSEGS = 9
TREE_TOK = 2176
TREES = 8
TOKENS = 17408


def tree_layout(key):
    role_keys = jax.random.split(jax.random.fold_in(key, 11), TREES)
    name_keys = jax.random.split(jax.random.fold_in(key, 13), TREES)

    def shuffled(single):
        return jax.random.permutation(single, 2 * FORKS).astype(jnp.int32)
    block_roles = jax.vmap(shuffled)(role_keys)
    drawn_names = jax.vmap(shuffled)(name_keys)
    block_range = jnp.arange(2 * FORKS, dtype=jnp.int32)
    first_owner = jnp.sum(jnp.where(block_roles == 0, block_range[None, :], 0), axis=1).astype(jnp.int32)
    owner_name = jnp.take_along_axis(drawn_names, first_owner[:, None], axis=1)
    is_owner = block_range[None, :] == first_owner[:, None]
    top_name = 2 * FORKS - 1
    block_names = jnp.where(is_owner, top_name, jnp.where(drawn_names == top_name, owner_name, drawn_names)).astype(jnp.int32)
    return (block_roles, block_names)


def token_blocks():
    token_index = jnp.arange(TREE_TOK, dtype=jnp.int32)
    in_trunk = token_index < TRUNK
    block_of = jnp.clip((token_index - TRUNK) // BRANCH_LEN, 0, 2 * FORKS - 1).astype(jnp.int32)
    return (token_index, in_trunk, block_of)


def draw_seg_ids(key, part):
    block_roles, block_names = tree_layout(key)
    token_index, in_trunk, block_of = token_blocks()
    local_ids = jnp.where(in_trunk[None, :], 0, 1 + block_names[:, block_of])
    tree_base = jnp.arange(TREES, dtype=jnp.int32)[:, None] * NSEGS
    return (tree_base + local_ids).reshape(-1).astype(jnp.int32)


def draw_path_pos(key, part):
    block_roles, block_names = tree_layout(key)
    token_index, in_trunk, block_of = token_blocks()
    role_of_token = block_roles[:, block_of]
    offset = jnp.where(role_of_token < FORKS, TRUNK, TRUNK + BRANCH_LEN)
    within = token_index - TRUNK - block_of * BRANCH_LEN
    path_values = jnp.where(in_trunk[None, :], token_index[None, :], offset + within[None, :])
    return path_values.reshape(-1).astype(jnp.int32)


def draw_parent_table(key, part):
    block_roles, block_names = tree_layout(key)
    block_range = jnp.arange(2 * FORKS, dtype=jnp.int32)
    owners = jnp.sum(jnp.where(block_roles[:, None, :] == block_range[None, :, None], block_range[None, None, :], 0), axis=2).astype(jnp.int32)
    branch_role = jnp.clip(block_roles - FORKS, 0, FORKS - 1).astype(jnp.int32)
    branch_block = jnp.take_along_axis(owners, branch_role, axis=1)
    branch_name = jnp.take_along_axis(block_names, branch_block, axis=1)
    parent_local = jnp.where(block_roles < FORKS, 0, 1 + branch_name)
    by_name = jnp.sum(jnp.where(block_names[:, :, None] == block_range[None, None, :], parent_local[:, :, None], 0), axis=1)
    table = jnp.concatenate([jnp.zeros((TREES, 1), jnp.int32), by_name.astype(jnp.int32)], axis=1)
    tree_base = jnp.arange(TREES, dtype=jnp.int32)[:, None] * NSEGS
    return (table + tree_base).reshape(-1).astype(jnp.int32)


def level_of(own_key, dims, cuts, smallest, top_value):
    loudness = 1.0
    for position, blocks in cuts:
        heights = jax.random.uniform(jax.random.fold_in(jax.random.fold_in(own_key, 6), position), (blocks,), jnp.float32, smallest / len(cuts), top_value / len(cuts))
        loudness = loudness * jnp.repeat(jnp.exp(heights), dims[position] // blocks).reshape((-1,) + (1,) * (len(dims) - 1 - position))
    return loudness


def bell_draw(key, shape, scale, most, cuts=(), kind=jnp.bfloat16):
    array = jax.random.normal(key, shape, jnp.float32) * scale
    if len(cuts) > 0:
        array = level_of(key, shape, cuts, -0.22, 0.18) * array
    return jnp.clip(array, min=-most, max=most).astype(kind)


def setup_inputs(seed: int = 0) -> dict:
    keys = jax.random.split(jax.random.key(seed), 17)
    tokens = bell_draw(keys[0], (TOKENS, D), 1.0, 6.0, ((0, 32),))
    out_grad = bell_draw(keys[1], (TOKENS, D), 1.0, 6.0, ((0, 32),))
    seg_ids = draw_seg_ids(jax.random.fold_in(keys[16], 71), 0)
    parent_table = draw_parent_table(jax.random.fold_in(keys[16], 71), 0)
    path_pos = draw_path_pos(jax.random.fold_in(keys[16], 71), 0)
    attn_gain = jnp.clip(1.0 + 0.18 * jax.random.normal(keys[5], (D,), jnp.float32), 0.099609375, 1.8984375).astype(jnp.bfloat16)
    w_query = bell_draw(keys[6], (D, HEADS * HEAD_DIM), D ** -0.5, 0.125, ((0, 8), (1, 4)))
    w_key = bell_draw(keys[7], (D, KV_HEADS * HEAD_DIM), D ** -0.5, 0.125, ((0, 8), (1, 4)))
    w_value = bell_draw(keys[8], (D, KV_HEADS * HEAD_DIM), D ** -0.5, 0.125, ((0, 8), (1, 4)))
    w_out = bell_draw(keys[9], (HEADS * HEAD_DIM, D), (max(HEADS * HEAD_DIM * 8 // TREE_TOK, 4)) ** -0.5, 2.0, ((0, 4), (1, 8)))
    q_gain = jnp.clip(1.0 + 0.18 * jax.random.normal(keys[10], (HEAD_DIM,), jnp.float32), 0.099609375, 1.8984375).astype(jnp.bfloat16)
    k_gain = jnp.clip(1.0 + 0.18 * jax.random.normal(keys[11], (HEAD_DIM,), jnp.float32), 0.099609375, 1.8984375).astype(jnp.bfloat16)
    ffn_gain = jnp.clip(1.0 + 0.18 * jax.random.normal(keys[12], (D,), jnp.float32), 0.099609375, 1.8984375).astype(jnp.bfloat16)
    w_gate = bell_draw(keys[13], (D, FF), D ** -0.5, 0.125, ((0, 8), (1, 4)))
    w_up = bell_draw(keys[14], (D, FF), D ** -0.5, 0.125, ((0, 8), (1, 4)))
    w_down = bell_draw(keys[15], (FF, D), FF ** -0.5, 0.078125, ((0, 4), (1, 8)))
    return {"tokens": tokens, "out_grad": out_grad, "seg_ids": seg_ids, "parent_table": parent_table, "path_pos": path_pos, "attn_gain": attn_gain, "w_query": w_query, "w_key": w_key, "w_value": w_value, "w_out": w_out, "q_gain": q_gain, "k_gain": k_gain, "ffn_gain": ffn_gain, "w_gate": w_gate, "w_up": w_up, "w_down": w_down}


@jax.custom_vjp
def low(v):
    return lax.optimization_barrier(v.astype(jnp.bfloat16)).astype(jnp.float32)

@jax.custom_vjp
def low_back(v):
    return v

def low_keep(v):
    return (low(v), None)

def low_pass(kept, grad):
    return (grad,)

def back_keep(v):
    return (v, None)

def back_low(kept, grad):
    return (low(grad),)
low.defvjp(low_keep, low_pass)
low_back.defvjp(back_keep, back_low)
norm_eps = 1e-06
rope_base = 1000000.0
masked_score = -1e+30

def exact_dot(left, right):
    return jnp.dot(left, right, precision=lax.Precision.HIGHEST, preferred_element_type=jnp.float32)

def rms_normed(values, gain):
    inverse = lax.rsqrt(lax.optimization_barrier(jnp.mean(values * values, axis=-1, keepdims=True)) + norm_eps)
    return values * inverse * gain

def rotary_tables(positions):
    half_width = HEAD_DIM // 2
    frequency = rope_base ** (-(jnp.arange(half_width, dtype=jnp.float32) * 2.0) / HEAD_DIM)
    angles = positions.astype(jnp.float32)[:, None] * frequency[None, :]
    cosine = jnp.cos(angles)
    sine_table = jnp.sin(angles)
    return (jnp.concatenate([cosine, cosine], axis=-1), jnp.concatenate([sine_table, sine_table], axis=-1))

def rotate(values, cosine, sine_table):
    half_width = values.shape[-1] // 2
    turned = jnp.concatenate([-values[..., half_width:], values[..., :half_width]], axis=-1)
    return values * cosine[:, None, :] + turned * sine_table[:, None, :]

def allowed(row_seg, row_parent, row_grand, row_pos, col_seg, col_pos):
    related = (col_seg[None, :] == row_seg[:, None]) | (col_seg[None, :] == row_parent[:, None]) | (col_seg[None, :] == row_grand[:, None])
    return related & (col_pos[None, :] <= row_pos[:, None])

def attention(queries, key_rows, value_rows, tree_seg, tree_parent, tree_grand, tree_pos):
    group_size = HEADS // KV_HEADS
    key_all = jnp.repeat(key_rows, group_size, axis=1)
    value_all = jnp.repeat(value_rows, group_size, axis=1)
    block_rows = TREE_TOK // 4
    score_scale = HEAD_DIM ** (-0.5)

    def one_block(block_item):
        query_block, row_seg, row_parent, row_grand, row_pos = block_item
        pair_mask = allowed(row_seg, row_parent, row_grand, row_pos, tree_seg, tree_pos)
        scores = low_back(score_scale * jnp.einsum('qhd,khd->hqk', query_block, key_all, precision=lax.Precision.HIGHEST))
        scores = jnp.where(pair_mask[None], scores, masked_score)
        row_peak = lax.optimization_barrier(jnp.max(scores, axis=-1, keepdims=True))
        exponent = jnp.exp(scores - row_peak)
        probabilities = low(exponent / lax.optimization_barrier(jnp.sum(exponent, axis=-1, keepdims=True)))
        return jnp.einsum('hqk,khd->qhd', probabilities, value_all, precision=lax.Precision.HIGHEST)
    block_items = (queries.reshape(4, block_rows, HEADS, HEAD_DIM), tree_seg.reshape(4, block_rows), tree_parent.reshape(4, block_rows), tree_grand.reshape(4, block_rows), tree_pos.reshape(4, block_rows))
    return lax.map(jax.checkpoint(one_block), block_items).reshape(TREE_TOK, HEADS, HEAD_DIM)

def tree_layer(stream, parameters, tree_seg, tree_parent, tree_grand, tree_pos):
    gain_one, wq_full, wk_full, wv_full, wo_full, gain_query, gain_key, gain_two, wg_full, wu_full, wd_full = parameters
    normed_one = low(rms_normed(stream, gain_one))
    query_raw = low_back(exact_dot(normed_one, wq_full)).reshape(TREE_TOK, HEADS, HEAD_DIM)
    key_raw = low_back(exact_dot(normed_one, wk_full)).reshape(TREE_TOK, KV_HEADS, HEAD_DIM)
    value_rows = low_back(low(exact_dot(normed_one, wv_full))).reshape(TREE_TOK, KV_HEADS, HEAD_DIM)
    cosine, sine_table = rotary_tables(tree_pos)
    queries = low(rotate(rms_normed(query_raw, gain_query), cosine, sine_table))
    key_rows = low(rotate(rms_normed(key_raw, gain_key), cosine, sine_table))
    attended = attention(queries, key_rows, value_rows, tree_seg, tree_parent, tree_grand, tree_pos)
    attended = low_back(low(attended.reshape(TREE_TOK, HEADS * HEAD_DIM)))
    after_attn = stream + low_back(exact_dot(attended, wo_full))
    normed_two = low(rms_normed(after_attn, gain_two))
    gate_act = low_back(exact_dot(normed_two, wg_full))
    up_act = low_back(exact_dot(normed_two, wu_full))
    hidden = low(jax.nn.silu(gate_act) * up_act)
    return after_attn + low_back(exact_dot(hidden, wd_full))

def reference(tokens, out_grad, seg_ids, parent_table, path_pos, attn_gain, w_query, w_key, w_value, w_out, q_gain, k_gain, ffn_gain, w_gate, w_up, w_down):
    weights = tuple((entry.astype(jnp.float32) for entry in (attn_gain, w_query, w_key, w_value, w_out, q_gain, k_gain, ffn_gain, w_gate, w_up, w_down)))
    parent_ids = parent_table[seg_ids].astype(jnp.int32)
    grand_ids = parent_table[parent_ids].astype(jnp.int32)
    inputs = tokens.astype(jnp.float32).reshape(TREES, TREE_TOK, D)
    cotangents = out_grad.astype(jnp.float32).reshape(TREES, TREE_TOK, D)

    def per_tree(totals, tree_item):
        tree_rows, cotangent, tree_seg, tree_parent, tree_grand, tree_pos = tree_item

        def forward(values, parameters):
            return tree_layer(values, parameters, tree_seg, tree_parent, tree_grand, tree_pos)
        result, pullback = jax.vjp(forward, tree_rows, weights)
        rows_grad, params_grad = pullback(cotangent)
        return (jax.tree.map(jnp.add, totals, params_grad), (result, rows_grad))
    zero_grads = jax.tree.map(jnp.zeros_like, weights)
    tree_items = (inputs, cotangents, seg_ids.reshape(TREES, TREE_TOK), parent_ids.reshape(TREES, TREE_TOK), grand_ids.reshape(TREES, TREE_TOK), path_pos.reshape(TREES, TREE_TOK))
    totals, (results, input_grads) = lax.scan(per_tree, zero_grads, tree_items)
    mixed = results.reshape(TOKENS, D).astype(jnp.bfloat16)
    tokens_grad = input_grads.reshape(TOKENS, D).astype(jnp.bfloat16)
    return (mixed, tokens_grad, totals[0], totals[1], totals[2], totals[3], totals[4], totals[5], totals[6], totals[7], totals[8], totals[9], totals[10])
```

```python
import functools
import math

import jax
import jax.numpy as jnp
from jax import lax
from jax.experimental import pallas as pl
from jax.experimental.pallas import tpu as pltpu
from jax.sharding import PartitionSpec as P

HEAD_DIM = 128
TRUNK = 1152
BRANCH = 128
FORKS2 = 8
TREE_TOK = 2176
GROUP = 2

norm_eps = 1e-06
rope_base = 1000000.0
score_scale = HEAD_DIM ** (-0.5)
key_scale = score_scale * math.log2(math.e)
LN2 = math.log(2.0)
VMEM = 52 * 1024 * 1024

f32 = jnp.float32
bf16 = jnp.bfloat16


def dot_nn(a, b):
    return lax.dot_general(a, b, (((1,), (0,)), ((), ())), preferred_element_type=f32)


def dot_nt(a, b):
    return lax.dot_general(a, b, (((1,), (1,)), ((), ())), preferred_element_type=f32)


def contract_rows(a, b):
    return lax.dot_general(a, b, (((0,), (0,)), ((), ())), preferred_element_type=f32)


def params():
    return pltpu.CompilerParams(vmem_limit_bytes=VMEM)


def cost(flops, nbytes):
    return pl.CostEstimate(flops=int(flops), bytes_accessed=int(nbytes), transcendentals=0)


def nbytes(arrays):
    return sum(a.size * a.dtype.itemsize for a in arrays)


def offsets(pieces):
    offs, at = [], 0
    for piece in pieces:
        offs.append((at, piece.shape[0]))
        at += piece.shape[0]
    return offs


class Tiles:
    def __init__(self, first, rest, quarters, parts, base, per, width):
        self.first, self.rest = list(first), list(rest) if quarters > 1 else []
        self.quarters, self.parts, self.base, self.per, self.width = quarters, parts, base, per, width
        self.offs = offsets(self.first)
        self.steps = quarters * parts

    def arrays(self):
        return self.first + self.rest

    def scratch(self):
        depth = sum(r for _, r in self.offs)
        return [
            pltpu.VMEM((2, depth, self.width), bf16),
            pltpu.SemaphoreType.DMA((2, len(self.offs))),
        ]

    def fetch(self, refs, buf, sems, step):
        first, rest = refs[: len(self.first)], refs[len(self.first) :]
        slot = lax.rem(step, 2)
        quarter = lax.div(step, self.parts)
        part = step - quarter * self.parts

        def begin(group, tile):
            col = pl.multiple_of(tile * self.width, 128)
            for k, (at, r) in enumerate(self.offs):
                pltpu.make_async_copy(
                    group[k].at[:, pl.ds(col, self.width)],
                    buf.at[slot, pl.ds(at, r), :],
                    sems.at[slot, k],
                ).start()

        if not rest:
            begin(first, self.base + part)
        else:

            @pl.when(quarter == 0)
            def _():
                begin(first, self.base + part)

            @pl.when(quarter > 0)
            def _():
                begin(rest, (quarter - 1) * self.per + self.base + part)

    def wait(self, refs, buf, sems, step):
        slot = lax.rem(step, 2)
        for k, (at, r) in enumerate(self.offs):
            pltpu.make_async_copy(
                refs[k].at[:, pl.ds(0, self.width)], buf.at[slot, pl.ds(at, r), :], sems.at[slot, k]
            ).wait()
        return slot


def tiled_call(body, sets, ins, in_specs, out_shape, out_specs, scratch, flops):
    steps = sets[0].steps
    counts = [len(s.arrays()) for s in sets]
    n_in, n_out = len(ins), len(out_shape)

    def kernel(*refs):
        at = 0
        piece_refs = []
        for c in counts:
            piece_refs.append(refs[at : at + c])
            at += c
        in_refs = refs[at : at + n_in]
        at += n_in
        out_refs = refs[at : at + n_out]
        at += n_out
        bufs = [(refs[at + 2 * i], refs[at + 2 * i + 1]) for i in range(len(sets))]
        own = refs[at + 2 * len(sets) :]
        step = pl.program_id(0)

        @pl.when(step == 0)
        def _():
            for s, p, (buf, sems) in zip(sets, piece_refs, bufs):
                s.fetch(p, buf, sems, step)

        @pl.when(step + 1 < steps)
        def _():
            for s, p, (buf, sems) in zip(sets, piece_refs, bufs):
                s.fetch(p, buf, sems, step + 1)

        tiles = []
        for s, p, (buf, sems) in zip(sets, piece_refs, bufs):
            slot = s.wait(p, buf, sems, step)
            tiles.append(buf.at[slot])
        body(step, tiles, in_refs, out_refs, own)

    weights = [a for s in sets for a in s.arrays()]
    return pl.pallas_call(
        kernel,
        grid=(steps,),
        in_specs=[pl.BlockSpec(memory_space=pl.ANY)] * len(weights) + in_specs,
        out_specs=out_specs,
        out_shape=out_shape,
        scratch_shapes=[x for s in sets for x in s.scratch()] + scratch,
        compiler_params=params(),
        cost_estimate=cost(flops, nbytes(weights) + nbytes(ins) + nbytes(out_shape)),
    )(*weights, *ins)


def whole(array):
    return pl.BlockSpec(array.shape, lambda t: (0,) * len(array.shape))


def head_slices(width):
    return [slice(h * HEAD_DIM, (h + 1) * HEAD_DIM) for h in range(width // HEAD_DIM)]


def project_qkv(normed, tiles, cosine, sine, q_gain, k_gain):
    rows, tw = normed.shape[0], tiles.width

    def body(step, weights, ins, outs, own):
        a, cos_ref, sin_ref, qg, kg = ins
        hat, raw = outs
        acc = dot_nn(a[...], weights[0][...])

        def turned(x, gain):
            inverse = lax.rsqrt(jnp.mean(x * x, axis=-1, keepdims=True) + norm_eps)
            u = x * inverse * gain
            return u * cos_ref[...] + pltpu.roll(u, HEAD_DIM // 2, 1) * sin_ref[...]

        @pl.when(step == 0)
        def _():
            for cut in head_slices(tw):
                hat[:, cut] = turned(acc[:, cut], qg[...]).astype(bf16)
            raw[...] = acc.astype(bf16)

        @pl.when(step == 1)
        def _():
            for cut in head_slices(tw // 2):
                hat[:, cut] = (turned(acc[:, cut], kg[...]) * key_scale).astype(bf16)
            hat[:, tw // 2 :] = acc[:, tw // 2 :].astype(bf16)
            raw[...] = acc.astype(bf16)

    ins = [normed, cosine, sine, q_gain, k_gain]
    shape = jax.ShapeDtypeStruct((rows, 2 * tw), bf16)
    return tiled_call(
        body,
        [tiles],
        ins,
        [whole(x) for x in ins],
        [shape, shape],
        [pl.BlockSpec((rows, tw), lambda t: (0, t))] * 2,
        [],
        4 * rows * normed.shape[1] * tw,
    )


def project_rows(a, tiles, out_dtype=bf16):
    rows, tw = a.shape[0], tiles.width

    def body(step, weights, ins, outs, own):
        outs[0][...] = dot_nn(ins[0][...], weights[0][...]).astype(out_dtype)

    return tiled_call(
        body,
        [tiles],
        [a],
        [whole(a)],
        [jax.ShapeDtypeStruct((rows, tiles.steps * tw), out_dtype)],
        [pl.BlockSpec((rows, tw), lambda t: (0, t))],
        [],
        2 * rows * a.shape[1] * tw * tiles.steps,
    )[0]


def project_columns(lefts, sets, depth, out_dtype):
    rows, tw, steps = lefts[0].shape[0], sets[0].width, sets[0].steps

    def body(step, weights, ins, outs, own):
        acc = own[0]
        total = dot_nt(ins[0][...], weights[0][...])
        for left, weight in zip(ins[1:], weights[1:]):
            total = total + dot_nt(left[...], weight[...])

        @pl.when(step == 0)
        def _():
            acc[...] = total

        @pl.when(step > 0)
        def _():
            acc[...] += total

        @pl.when(step == steps - 1)
        def _():
            outs[0][...] = acc[...].astype(out_dtype)

    return tiled_call(
        body,
        sets,
        list(lefts),
        [pl.BlockSpec((rows, tw), lambda t: (0, t))] * len(lefts),
        [jax.ShapeDtypeStruct((rows, depth), out_dtype)],
        [pl.BlockSpec((rows, depth), lambda t: (0, 0))],
        [pltpu.VMEM((rows, depth), f32)],
        2 * rows * depth * tw * steps * len(sets),
    )[0]


def feed_forward(normed, gate_tiles, up_tiles):
    rows, tw = normed.shape[0], gate_tiles.width

    def body(step, weights, ins, outs, own):
        a = ins[0][...]
        gate = dot_nn(a, weights[0][...])
        up = dot_nn(a, weights[1][...])
        outs[0][...] = (gate * jax.nn.sigmoid(gate) * up).astype(bf16)
        outs[1][...] = gate.astype(bf16)
        outs[2][...] = up.astype(bf16)

    shape = jax.ShapeDtypeStruct((rows, gate_tiles.steps * tw), bf16)
    return tiled_call(
        body,
        [gate_tiles, up_tiles],
        [normed],
        [whole(normed)],
        [shape] * 3,
        [pl.BlockSpec((rows, tw), lambda t: (0, t))] * 3,
        [],
        4 * rows * normed.shape[1] * tw * gate_tiles.steps,
    )


def feed_back(cotangent, gate, up, down_tiles):
    rows, tw = cotangent.shape[0], down_tiles.width

    def body(step, weights, ins, outs, own):
        grad = dot_nn(ins[0][...], weights[0][...])
        g = ins[1][...].astype(f32)
        u = ins[2][...].astype(f32)
        s = jax.nn.sigmoid(g)
        outs[0][...] = (grad * u * s * (1.0 + g * (1.0 - s))).astype(bf16)
        outs[1][...] = (grad * (g * s)).astype(bf16)

    shape = jax.ShapeDtypeStruct(gate.shape, bf16)
    tile = pl.BlockSpec((rows, tw), lambda t: (0, t))
    return tiled_call(
        body,
        [down_tiles],
        [cotangent, gate, up],
        [whole(cotangent), tile, tile],
        [shape] * 2,
        [tile] * 2,
        [],
        2 * rows * cotangent.shape[1] * tw * down_tiles.steps,
    )


def qkv_back(grad_hat, raw, cosine, sine, q_gain, k_gain):
    rows, width = grad_hat.shape
    tw = width // 2

    def kernel(g_ref, r_ref, cos_ref, sin_ref, qg, kg, out, qsum, ksum):
        def back(cut, gain, total):
            w = g_ref[:, cut].astype(f32)
            w = w * cos_ref[...] + pltpu.roll(w * sin_ref[...], HEAD_DIM // 2, 1)
            x = r_ref[:, cut].astype(f32)
            inverse = lax.rsqrt(jnp.mean(x * x, axis=-1, keepdims=True) + norm_eps)
            u = x * inverse
            wu = w * u
            scaled = w * gain
            out[:, cut] = (
                inverse * (scaled - u * jnp.mean(wu * gain, axis=-1, keepdims=True))
            ).astype(bf16)
            return total + jnp.sum(wu, axis=0, keepdims=True)

        total = jnp.zeros((1, HEAD_DIM), f32)
        cuts = head_slices(width)
        n_query, n_key = tw // HEAD_DIM, tw // HEAD_DIM // 2
        for cut in cuts[:n_query]:
            total = back(cut, qg[...], total)
        qsum[...] = total
        total = jnp.zeros((1, HEAD_DIM), f32)
        for cut in cuts[n_query : n_query + n_key]:
            total = back(cut, kg[...], total)
        ksum[...] = total
        out[:, tw + tw // 2 :] = g_ref[:, tw + tw // 2 :]

    ins = [grad_hat, raw, cosine, sine, q_gain, k_gain]
    gain_shape = jax.ShapeDtypeStruct((1, HEAD_DIM), f32)
    out_shape = [jax.ShapeDtypeStruct((rows, width), bf16), gain_shape, gain_shape]
    return pl.pallas_call(
        kernel,
        out_shape=out_shape,
        compiler_params=params(),
        cost_estimate=cost(40 * rows * width, nbytes(ins) + nbytes(out_shape)),
    )(*ins)


def attention_specs(kv):
    q = pl.BlockSpec((TREE_TOK, GROUP * HEAD_DIM), lambda n, s: (0, n))
    k = pl.BlockSpec((TREE_TOK, HEAD_DIM), lambda n, s: (0, GROUP * kv + n))
    v = pl.BlockSpec((TREE_TOK, HEAD_DIM), lambda n, s: (0, (GROUP + 1) * kv + n))
    return q, k, v


def stacked(ref, start):
    rows = pl.ds(start, BRANCH)
    return jnp.concatenate(
        [ref[rows, h * HEAD_DIM : (h + 1) * HEAD_DIM] for h in range(GROUP)], axis=0
    )


def causal():
    key = lax.broadcasted_iota(jnp.int32, (BRANCH, GROUP * BRANCH), 0)
    query = lax.rem(lax.broadcasted_iota(jnp.int32, (BRANCH, GROUP * BRANCH), 1), BRANCH)
    return key <= query


TRUNK_BLOCKS = TRUNK // BRANCH
BLOCKS = TREE_TOK // BRANCH


def attention_forward(qkv, parents, kv):
    def kernel(parent_ref, q_ref, k_ref, v_ref, out_ref, log_ref, vt):
        vt[...] = v_ref[...].T
        mask = causal()

        def part(q, start, size, rule):
            score = dot_nt(k_ref[pl.ds(start, size), :], q)
            weight = jnp.exp2(score)
            if rule is not None:
                weight = rule(weight)
            out = dot_nn(vt[:, pl.ds(start, size)], weight.astype(bf16))
            return out, jnp.sum(weight, axis=0, keepdims=True)

        def finish(block, start, pieces):
            out = sum(p[0] for p in pieces)
            total = sum(p[1] for p in pieces)
            out = (out / total).T.astype(bf16)
            for h in range(GROUP):
                out_ref[pl.ds(start, BRANCH), h * HEAD_DIM : (h + 1) * HEAD_DIM] = out[
                    h * BRANCH : (h + 1) * BRANCH
                ]
            log_ref[0, pl.ds(block, 1), :] = jnp.log2(total)

        diagonal = lambda w: jnp.where(mask, w, 0.0)
        for block in range(TRUNK_BLOCKS):
            q = stacked(q_ref, block * BRANCH)
            pieces = [part(q, block * BRANCH, BRANCH, diagonal)]
            if block > 0:
                pieces.append(part(q, 0, block * BRANCH, None))
            finish(block, block * BRANCH, pieces)

        def branch(i, carry):
            block = TRUNK_BLOCKS + i
            start = pl.multiple_of(block * BRANCH, BRANCH)
            q = stacked(q_ref, start)
            parent = parent_ref[i]
            has = (parent != block).astype(f32)
            pieces = [
                part(q, start, BRANCH, diagonal),
                part(q, pl.multiple_of(parent * BRANCH, BRANCH), BRANCH, lambda w: w * has),
                part(q, 0, TRUNK, None),
            ]
            finish(block, start, pieces)
            return carry

        lax.fori_loop(0, FORKS2, branch, 0)

    q, k, v = attention_specs(kv)
    out_shape = [
        jax.ShapeDtypeStruct((TREE_TOK, GROUP * kv * HEAD_DIM), bf16),
        jax.ShapeDtypeStruct((kv, BLOCKS, GROUP * BRANCH), f32),
    ]
    return pl.pallas_call(
        kernel,
        grid_spec=pltpu.PrefetchScalarGridSpec(
            num_scalar_prefetch=1,
            grid=(kv,),
            in_specs=[q, k, v],
            out_specs=[
                q,
                pl.BlockSpec((1, BLOCKS, GROUP * BRANCH), lambda n, s: (n, 0, 0)),
            ],
            scratch_shapes=[pltpu.VMEM((HEAD_DIM, TREE_TOK), bf16)],
        ),
        out_shape=out_shape,
        compiler_params=params(),
        cost_estimate=cost(kv * 2.2e6 * 2 * GROUP * 256 * 2, nbytes([qkv]) + nbytes(out_shape)),
    )(parents, qkv, qkv, qkv)


def attention_backward(qkv, attended, grads, logs, parents, kv):
    def kernel(
        parent_ref, q_ref, k_ref, v_ref, o_ref, do_ref, log_ref, dq_ref, dk_ref, dv_ref, kt, dk, dv
    ):
        kt[...] = k_ref[...].T
        dk[...] = jnp.zeros_like(dk)
        dv[...] = jnp.zeros_like(dv)
        mask = causal()

        def part(q, do, log, delta, start, size, rule):
            rows = pl.ds(start, size)
            prob = jnp.exp2(dot_nt(k_ref[rows, :], q) - log)
            if rule is not None:
                prob = rule(prob)
            grad = dot_nt(v_ref[rows, :], do)
            score_grad = (prob * (grad - delta)).astype(bf16)
            dk[rows, :] += dot_nn(score_grad, q)
            dv[rows, :] += dot_nn(prob.astype(bf16), do)
            return dot_nn(kt[:, rows], score_grad)

        def one(block, start, ranges):
            q = stacked(q_ref, start)
            do = stacked(do_ref, start)
            o = stacked(o_ref, start)
            delta = jnp.sum((do.astype(f32) * o.astype(f32)).T, axis=0, keepdims=True)
            log = log_ref[0, pl.ds(block, 1), :]
            total = sum(part(q, do, log, delta, *r) for r in ranges)
            out = (total * LN2).T.astype(bf16)
            for h in range(GROUP):
                dq_ref[pl.ds(start, BRANCH), h * HEAD_DIM : (h + 1) * HEAD_DIM] = out[
                    h * BRANCH : (h + 1) * BRANCH
                ]

        diagonal = lambda p: jnp.where(mask, p, 0.0)
        for block in range(TRUNK_BLOCKS):
            ranges = [(block * BRANCH, BRANCH, diagonal)]
            if block > 0:
                ranges.append((0, block * BRANCH, None))
            one(block, block * BRANCH, ranges)

        def branch(i, carry):
            block = TRUNK_BLOCKS + i
            start = pl.multiple_of(block * BRANCH, BRANCH)
            parent = parent_ref[i]
            has = (parent != block).astype(f32)
            one(
                block,
                start,
                [
                    (start, BRANCH, diagonal),
                    (pl.multiple_of(parent * BRANCH, BRANCH), BRANCH, lambda p: p * has),
                    (0, TRUNK, None),
                ],
            )
            return carry

        lax.fori_loop(0, FORKS2, branch, 0)
        dk_ref[...] = (dk[...] * score_scale).astype(bf16)
        dv_ref[...] = dv[...].astype(bf16)

    q, k, v = attention_specs(kv)
    single = pl.BlockSpec((TREE_TOK, HEAD_DIM), lambda n, s: (0, n))
    out_shape = [
        jax.ShapeDtypeStruct((TREE_TOK, GROUP * kv * HEAD_DIM), bf16),
        jax.ShapeDtypeStruct((TREE_TOK, kv * HEAD_DIM), bf16),
        jax.ShapeDtypeStruct((TREE_TOK, kv * HEAD_DIM), bf16),
    ]
    return pl.pallas_call(
        kernel,
        grid_spec=pltpu.PrefetchScalarGridSpec(
            num_scalar_prefetch=1,
            grid=(kv,),
            in_specs=[
                q,
                k,
                v,
                q,
                q,
                pl.BlockSpec((1, BLOCKS, GROUP * BRANCH), lambda n, s: (n, 0, 0)),
            ],
            out_specs=[q, single, single],
            scratch_shapes=[
                pltpu.VMEM((HEAD_DIM, TREE_TOK), bf16),
                pltpu.VMEM((TREE_TOK, HEAD_DIM), f32),
                pltpu.VMEM((TREE_TOK, HEAD_DIM), f32),
            ],
        ),
        out_shape=out_shape,
        compiler_params=params(),
        cost_estimate=cost(
            kv * 2.2e6 * 2 * GROUP * 640 * 2, nbytes([qkv, attended, grads]) + nbytes(out_shape)
        ),
    )(parents, qkv, qkv, qkv, attended, grads, logs)


def shuffle_columns(a, order):
    rows, count = a.shape[0], order.shape[0]
    width = a.shape[1] // count

    def kernel(order_ref, in_ref, out_ref):
        out_ref[...] = in_ref[...]

    return pl.pallas_call(
        kernel,
        grid_spec=pltpu.PrefetchScalarGridSpec(
            num_scalar_prefetch=1,
            grid=(count,),
            in_specs=[pl.BlockSpec((rows, width), lambda k, s: (0, s[k]))],
            out_specs=pl.BlockSpec((rows, width), lambda k, s: (0, k)),
        ),
        out_shape=jax.ShapeDtypeStruct(a.shape, a.dtype),
        cost_estimate=cost(0, 2 * nbytes([a])),
    )(order, a)


def place_rows(pieces, order):
    rows, width = pieces[0].shape
    count = len(pieces)

    def kernel(order_ref, *refs):
        ins, out, sems = refs[:count], refs[count], refs[count + 1]
        copies = [
            pltpu.make_async_copy(
                ins[e], out.at[pl.ds(pl.multiple_of(order_ref[e] * rows, 16), rows), :], sems.at[e]
            )
            for e in range(count)
        ]
        for c in copies:
            c.start()
        for c in copies:
            c.wait()

    return pl.pallas_call(
        kernel,
        grid_spec=pltpu.PrefetchScalarGridSpec(
            num_scalar_prefetch=1,
            grid=(),
            in_specs=[pl.BlockSpec(memory_space=pl.ANY)] * count,
            out_specs=pl.BlockSpec(memory_space=pl.ANY),
            scratch_shapes=[pltpu.SemaphoreType.DMA((count,))],
        ),
        out_shape=jax.ShapeDtypeStruct((rows * count, width), pieces[0].dtype),
        cost_estimate=cost(0, 2 * nbytes(pieces)),
    )(order, *pieces)


def inverse_rms(values):
    return lax.rsqrt(jnp.mean(values * values, axis=-1, keepdims=True) + norm_eps)


def norm_back(grads, unit_values, inverse, gain):
    scaled = grads * gain
    return inverse * (scaled - unit_values * jnp.mean(scaled * unit_values, axis=-1, keepdims=True))


def local(
    m,
    n,
    tokens,
    out_grad,
    seg_ids,
    parent_table,
    path_pos,
    attn_gain,
    w_query,
    w_key,
    w_value,
    w_out,
    q_gain,
    k_gain,
    ffn_gain,
    w_gate,
    w_up,
    w_down,
):
    rows, depth = tokens.shape
    block = depth // m
    order = [0, 2, 4, 6, 1, 3, 5, 7] if m == 8 else list(range(m))
    where = lax.axis_index("wide").astype(jnp.int32)
    seat = lax.axis_index("tp").astype(jnp.int32)
    relative = jnp.asarray(order, jnp.int32) ^ where
    inverse_order = [order.index(k) for k in range(m)]
    absolute = jnp.take(jnp.asarray(inverse_order, jnp.int32), jnp.arange(m, dtype=jnp.int32) ^ where)
    seats = jnp.arange(n, dtype=jnp.int32) ^ seat

    def over(axis, a, mask):
        size = m if axis == "wide" else n
        return lax.ppermute(a, axis, [(i, i ^ mask) for i in range(size)])

    def gather(a):
        if m == 8:
            half = a.shape[0] // 2
            along_x = over("wide", a, 2)
            along_y = over("wide", a, 4)
            top = over("wide", along_y[:half], 2)
            low = over("wide", along_x[half:], 4)
            mine = [a, along_x, along_y, top, low]
            return mine + [over("wide", p, 1) for p in mine]
        return [a] + [over("wide", a, k) for k in range(1, m)]

    def scatter(mine, other):
        if m == 8:
            half = block // 2
            total = mine.astype(f32) + over("wide", other, 1).astype(f32)
            top = over("wide", total[3 * block : 3 * block + half].astype(bf16), 2)
            low = over("wide", total[3 * block + half :].astype(bf16), 4)
            for_x = jnp.concatenate(
                [
                    total[block : block + half],
                    total[block + half : 2 * block] + low.astype(f32),
                ]
            ).astype(bf16)
            for_y = jnp.concatenate(
                [
                    total[2 * block : 2 * block + half] + top.astype(f32),
                    total[2 * block + half : 3 * block],
                ]
            ).astype(bf16)
            return (
                total[:block]
                + over("wide", for_x, 2).astype(f32)
                + over("wide", for_y, 4).astype(f32)
            )
        both = jnp.concatenate([mine, other])
        total = both[:block].astype(f32)
        for k in range(1, m):
            total = total + over("wide", both[k * block : (k + 1) * block], k).astype(f32)
        return total

    def gradient(left, right):
        half = depth // 2
        return (
            contract_rows(left[:, :half], right).astype(bf16),
            contract_rows(left[:, half:], right).astype(bf16),
        )

    attn_block = jnp.concatenate([w_query, w_key, w_value, w_out.T], axis=1)
    ffn_block = jnp.concatenate([w_gate, w_up, w_down.T], axis=1)
    attn_first = gather(attn_block)
    attn_rest = gather(
        jnp.concatenate([over("tp", attn_block, e) for e in range(1, n)], axis=1)
    )
    ffn_first = gather(ffn_block)
    ffn_rest = gather(
        jnp.concatenate([over("tp", ffn_block, 2 * e) for e in range(1, n // 2)], axis=1)
    )
    aw = w_query.shape[1]
    kv = w_key.shape[1] // HEAD_DIM
    fcols = w_gate.shape[1]
    fw = fcols // 3

    def attn_tiles(parts, base):
        return Tiles(attn_first, attn_rest, n, parts, base, 3, aw)

    def ffn_tiles(base):
        return Tiles(ffn_first, ffn_rest, n // 2, 3, base, 9, fw)

    gains = lax.all_gather(
        jnp.concatenate([attn_gain, ffn_gain, q_gain, k_gain]), "wide", axis=0, tiled=False
    ).astype(f32)
    gain_one = jnp.take(gains[:, :block], relative, axis=0).reshape(1, depth)
    gain_two = jnp.take(gains[:, block : 2 * block], relative, axis=0).reshape(1, depth)
    small = q_gain.shape[0]
    gain_q = gains[:, 2 * block : 2 * block + small].reshape(1, HEAD_DIM)
    gain_k = gains[:, 2 * block + small :].reshape(1, HEAD_DIM)

    base = where * parent_table.shape[0]
    block_segs = seg_ids[TRUNK::BRANCH] - base
    hit = block_segs[:, None] == jnp.arange(parent_table.shape[0], dtype=jnp.int32)[None, :]
    block_parents = jnp.sum(jnp.where(hit, parent_table[None, :] - base, 0), axis=1)
    match = block_parents[:, None] == block_segs[None, :]
    number = TRUNK_BLOCKS + jnp.arange(FORKS2, dtype=jnp.int32)
    parents = jnp.where(
        jnp.any(match, axis=1), jnp.sum(jnp.where(match, number[None, :], 0), axis=1), number
    ).astype(jnp.int32)

    own_pos = lax.dynamic_slice_in_dim(path_pos, seat * rows, rows, 0).astype(f32)
    frequency = rope_base ** (-(jnp.arange(HEAD_DIM // 2, dtype=f32) * 2.0) / HEAD_DIM)
    angles = own_pos[:, None] * frequency[None, :]
    cosine, sine = jnp.cos(angles), jnp.sin(angles)
    cosine = jnp.concatenate([cosine, cosine], axis=-1)
    sine = jnp.concatenate([-sine, sine], axis=-1)

    stream = shuffle_columns(tokens, relative).astype(f32)
    cotangent = shuffle_columns(out_grad, relative)
    cotangent_next = over("tp", cotangent, 1)
    inverse_one = inverse_rms(stream)
    unit_one = stream * inverse_one
    normed_one = (unit_one * gain_one).astype(bf16)
    hats, raws = [None] * n, [None] * n
    for e in list(range(1, n)) + [0]:
        tiles = (
            Tiles(attn_first, [], 1, 2, 0, 3, aw)
            if e == 0
            else Tiles(attn_rest, [], 1, 2, 3 * (e - 1), 3, aw)
        )
        hats[e], raws[e] = project_qkv(normed_one, tiles, cosine, sine, gain_q, gain_k)

    def exchange(parts):
        return [parts[0]] + [over("tp", parts[e], e) for e in range(1, n)]

    def rows_for(a, e):
        return lax.dynamic_slice_in_dim(a, seats[e] * rows, rows, 0)

    qkv = place_rows(exchange(hats), seats)
    attended_heads, logs = attention_forward(qkv, parents, kv)
    attended = jnp.concatenate(
        exchange([rows_for(attended_heads, e) for e in range(n)]), axis=1
    )
    after_attn = stream + project_columns([attended], [attn_tiles(1, 2)], depth, f32)

    inverse_two = inverse_rms(after_attn)
    unit_two = after_attn * inverse_two
    normed_two = (unit_two * gain_two).astype(bf16)
    normed_two_next = over("tp", normed_two, 1)
    hidden, gate, up = feed_forward(normed_two, ffn_tiles(0), ffn_tiles(3))
    hidden_next, gate_next, up_next = feed_forward(normed_two_next, ffn_tiles(0), ffn_tiles(3))
    down_next = over("tp", project_columns([hidden_next], [ffn_tiles(6)], depth, bf16), 1)
    down = project_columns([hidden], [ffn_tiles(6)], depth, f32)
    mixed = (after_attn + down + down_next.astype(f32)).astype(bf16)
    mixed = shuffle_columns(mixed, absolute)

    gate_grad_next, up_grad_next = feed_back(cotangent_next, gate_next, up_next, ffn_tiles(6))
    back_next = over(
        "tp",
        project_columns([gate_grad_next, up_grad_next], [ffn_tiles(0), ffn_tiles(3)], depth, bf16),
        1,
    )
    gate_grad, up_grad = feed_back(cotangent, gate, up, ffn_tiles(6))
    back = project_columns([gate_grad, up_grad], [ffn_tiles(0), ffn_tiles(3)], depth, f32)
    normed_two_grad = back + back_next.astype(f32)

    cotangent_pair = jnp.concatenate([cotangent, cotangent_next])
    normed_two_pair = jnp.concatenate([normed_two, normed_two_next])

    def ffn_share(left, right):
        total = scatter(*gradient(left, right))
        shares = total[:, :fcols]
        for e in range(1, n // 2):
            shares = shares + over(
                "tp", total[:, e * fcols : (e + 1) * fcols].astype(bf16), 2 * e
            ).astype(f32)
        return shares

    down_share = ffn_share(cotangent_pair, jnp.concatenate([hidden, hidden_next])).T
    gate_share = ffn_share(normed_two_pair, jnp.concatenate([gate_grad, gate_grad_next]))
    up_share = ffn_share(normed_two_pair, jnp.concatenate([up_grad, up_grad_next]))

    ffn_gain_part = jnp.sum(normed_two_grad * unit_two, axis=0)
    stream_grad = cotangent.astype(f32) + norm_back(
        normed_two_grad, unit_two, inverse_two, gain_two
    )
    grad_low = stream_grad.astype(bf16)
    attended_grad = project_rows(grad_low, attn_tiles(1, 2))
    grad_heads = place_rows(
        exchange([attended_grad[:, e * aw : (e + 1) * aw] for e in range(n)]), seats
    )
    dq, dk, dv = attention_backward(qkv, attended_heads, grad_heads, logs, parents, kv)
    back_hats = exchange(
        [
            jnp.concatenate([rows_for(dq, e), rows_for(dk, e), rows_for(dv, e)], axis=1)
            for e in range(n)
        ]
    )
    raw_grads, q_parts, k_parts = zip(
        *[
            qkv_back(back_hats[e], raws[e], cosine, sine, gain_q, gain_k)
            for e in range(n)
        ]
    )
    raw_grads = jnp.concatenate(raw_grads, axis=1)
    normed_one_grad = project_columns([raw_grads], [attn_tiles(2, 0)], depth, f32)

    def attn_share(left, right, width):
        total = scatter(*gradient(left, right))
        shares = total[:, :width]
        for e in range(1, n):
            shares = shares + over(
                "tp", total[:, e * width : (e + 1) * width].astype(bf16), e
            ).astype(f32)
        return shares

    out_share = attn_share(grad_low, attended, aw).T
    qkv_share = attn_share(normed_one, raw_grads, 2 * aw)

    attn_gain_part = jnp.sum(normed_one_grad * unit_one, axis=0)
    tokens_grad = (
        stream_grad + norm_back(normed_one_grad, unit_one, inverse_one, gain_one)
    ).astype(bf16)
    tokens_grad = shuffle_columns(tokens_grad, absolute)

    parts = jnp.concatenate(
        [
            jnp.take(attn_gain_part.reshape(m, block), absolute, axis=0),
            jnp.take(ffn_gain_part.reshape(m, block), absolute, axis=0),
            sum(q_parts).reshape(m, small),
            sum(k_parts).reshape(m, small),
        ],
        axis=1,
    )
    sums = lax.dynamic_index_in_dim(lax.psum(parts, ("wide", "tp")), where, 0, False)
    return (
        mixed,
        tokens_grad,
        sums[:block],
        qkv_share[:, :aw],
        qkv_share[:, aw : aw + aw // 2],
        qkv_share[:, aw + aw // 2 :],
        out_share,
        sums[2 * block : 2 * block + small],
        sums[2 * block + small :],
        sums[block : 2 * block],
        gate_share,
        up_share,
        down_share,
    )


def solution(mesh):
    both = P(("wide", "tp"), None)
    w, wt, tw = P("wide"), P("wide", "tp"), P("tp", "wide")
    return jax.shard_map(
        functools.partial(local, mesh.shape["wide"], mesh.shape["tp"]),
        mesh=mesh,
        in_specs=(both, both, w, w, w, w, wt, wt, wt, tw, w, w, w, wt, wt, tw),
        out_specs=(both, both, w, wt, wt, wt, tw, w, w, w, wt, wt, tw),
        check_vma=False,
    )
```

```python
import functools
import math

import jax
import jax.numpy as jnp
from jax import lax
from jax.experimental import pallas as pl
from jax.experimental.pallas import tpu as pltpu
from jax.sharding import PartitionSpec as P

HEAD_DIM = 128
TRUNK = 1152
BRANCH = 128
FORKS2 = 8
TREE_TOK = 2176
GROUP = 2

norm_eps = 1e-06
rope_base = 1000000.0
score_scale = HEAD_DIM ** (-0.5)
key_scale = score_scale * math.log2(math.e)
LN2 = math.log(2.0)
VMEM = 52 * 1024 * 1024
COST = 0.01

f32 = jnp.float32
bf16 = jnp.bfloat16


def dot_nn(a, b):
    return lax.dot_general(a, b, (((1,), (0,)), ((), ())), preferred_element_type=f32)


def dot_nt(a, b):
    return lax.dot_general(a, b, (((1,), (1,)), ((), ())), preferred_element_type=f32)


def contract_rows(a, b):
    return lax.dot_general(a, b, (((0,), (0,)), ((), ())), preferred_element_type=f32)


def params():
    return pltpu.CompilerParams(vmem_limit_bytes=VMEM)


def cost(flops, nbytes):
    return pl.CostEstimate(flops=int(flops * COST), bytes_accessed=int(nbytes * COST), transcendentals=0)


def nbytes(arrays):
    return sum(a.size * a.dtype.itemsize for a in arrays)


class Tiles:
    def __init__(self, arrays, parts, base, width):
        self.list = list(arrays)
        self.quarters = sum(a.shape[0] for a in self.list)
        self.depth = self.list[0].shape[1]
        self.parts, self.base, self.width = parts, base, width
        self.steps = self.quarters * parts

    def arrays(self):
        return self.list

    def scratch(self):
        return [pltpu.VMEM((2, self.depth, self.width), bf16), pltpu.SemaphoreType.DMA((2,))]

    def fetch(self, refs, buf, sems, step):
        slot = lax.rem(step, 2)
        quarter = lax.div(step, self.parts)
        part = step - quarter * self.parts
        col = pl.multiple_of((self.base + part) * self.width, 128)

        def begin(ref, at):
            pltpu.make_async_copy(
                ref.at[at, :, pl.ds(col, self.width)], buf.at[slot], sems.at[slot]
            ).start()

        split = self.list[0].shape[0]
        if len(refs) == 1:
            begin(refs[0], quarter)
        else:

            @pl.when(quarter < split)
            def _():
                begin(refs[0], quarter)

            @pl.when(quarter >= split)
            def _():
                begin(refs[1], quarter - split)

    def wait(self, refs, buf, sems, step):
        slot = lax.rem(step, 2)
        pltpu.make_async_copy(
            refs[0].at[0, :, pl.ds(0, self.width)], buf.at[slot], sems.at[slot]
        ).wait()
        return slot


def tiled_call(body, sets, seats, ins, in_specs, out_shape, out_specs, scratch, flops):
    steps = sets[0].steps
    counts = [len(s.arrays()) for s in sets]
    n_in, n_out = len(ins), len(out_shape)

    def kernel(seat_ref, *refs):
        at = 0
        piece_refs = []
        for c in counts:
            piece_refs.append(refs[at : at + c])
            at += c
        in_refs = refs[at : at + n_in]
        at += n_in
        out_refs = refs[at : at + n_out]
        at += n_out
        bufs = [(refs[at + 2 * i], refs[at + 2 * i + 1]) for i in range(len(sets))]
        own = refs[at + 2 * len(sets) :]
        step = pl.program_id(0)

        @pl.when(step == 0)
        def _():
            for s, p, (buf, sems) in zip(sets, piece_refs, bufs):
                s.fetch(p, buf, sems, step)

        @pl.when(step + 1 < steps)
        def _():
            for s, p, (buf, sems) in zip(sets, piece_refs, bufs):
                s.fetch(p, buf, sems, step + 1)

        tiles = []
        for s, p, (buf, sems) in zip(sets, piece_refs, bufs):
            slot = s.wait(p, buf, sems, step)
            tiles.append(buf.at[slot])
        body(step, tiles, in_refs, out_refs, own)

    weights = [a for s in sets for a in s.arrays()]
    return pl.pallas_call(
        kernel,
        grid_spec=pltpu.PrefetchScalarGridSpec(
            num_scalar_prefetch=1,
            grid=(steps,),
            in_specs=[pl.BlockSpec(memory_space=pl.ANY)] * len(weights) + in_specs,
            out_specs=out_specs,
            scratch_shapes=[x for s in sets for x in s.scratch()] + scratch,
        ),
        out_shape=out_shape,
        compiler_params=params(),
        cost_estimate=cost(flops, nbytes(weights) + nbytes(ins) + nbytes(out_shape)),
    )(seats, *weights, *ins)


def whole(array):
    return pl.BlockSpec(array.shape, lambda t, s: (0,) * len(array.shape))


def seated(rows, width, parts):
    return pl.BlockSpec(
        (None, rows, width),
        lambda t, s: (s[lax.div(t, parts)], 0, lax.rem(t, parts)),
    )


def head_slices(width):
    return [slice(h * HEAD_DIM, (h + 1) * HEAD_DIM) for h in range(width // HEAD_DIM)]


def project_qkv(normed, tiles, seats, cosine, sine, q_gain, k_gain):
    rows, tw = normed.shape[0], tiles.width

    def body(step, weights, ins, outs, own):
        a, cos_ref, sin_ref, qg, kg = ins
        hat, raw = outs
        acc = dot_nn(a[...], weights[0][...])
        part = lax.rem(step, 2)

        def turned(x, gain):
            inverse = lax.rsqrt(jnp.mean(x * x, axis=-1, keepdims=True) + norm_eps)
            u = x * inverse * gain
            return u * cos_ref[...] + pltpu.roll(u, HEAD_DIM // 2, 1) * sin_ref[...]

        @pl.when(part == 0)
        def _():
            for cut in head_slices(tw):
                hat[:, cut] = turned(acc[:, cut], qg[...]).astype(bf16)
            raw[...] = acc.astype(bf16)

        @pl.when(part == 1)
        def _():
            for cut in head_slices(tw // 2):
                hat[:, cut] = (turned(acc[:, cut], kg[...]) * key_scale).astype(bf16)
            hat[:, tw // 2 :] = acc[:, tw // 2 :].astype(bf16)
            raw[...] = acc.astype(bf16)

    ins = [normed, cosine, sine, q_gain, k_gain]
    shape = jax.ShapeDtypeStruct((tiles.quarters, rows, 2 * tw), bf16)
    return tiled_call(
        body,
        [tiles],
        seats,
        ins,
        [whole(x) for x in ins],
        [shape, shape],
        [seated(rows, tw, 2)] * 2,
        [],
        4 * rows * normed.shape[1] * tw * tiles.quarters,
    )


def project_rows(a, tiles, seats):
    rows, tw = a.shape[0], tiles.width

    def body(step, weights, ins, outs, own):
        outs[0][...] = dot_nn(ins[0][...], weights[0][...]).astype(bf16)

    return tiled_call(
        body,
        [tiles],
        seats,
        [a],
        [whole(a)],
        [jax.ShapeDtypeStruct((tiles.quarters, rows, tiles.parts * tw), bf16)],
        [seated(rows, tw, tiles.parts)],
        [],
        2 * rows * a.shape[1] * tw * tiles.steps,
    )[0]


def project_columns(lefts, sets, seats, depth, out_dtype):
    rows, tw, steps = lefts[0].shape[1], sets[0].width, sets[0].steps

    def body(step, weights, ins, outs, own):
        acc = own[0]
        total = dot_nt(ins[0][...], weights[0][...])
        for left, weight in zip(ins[1:], weights[1:]):
            total = total + dot_nt(left[...], weight[...])

        @pl.when(step == 0)
        def _():
            acc[...] = total

        @pl.when(step > 0)
        def _():
            acc[...] += total

        @pl.when(step == steps - 1)
        def _():
            outs[0][...] = acc[...].astype(out_dtype)

    return tiled_call(
        body,
        sets,
        seats,
        list(lefts),
        [seated(rows, tw, s.parts) for s in sets],
        [jax.ShapeDtypeStruct((rows, depth), out_dtype)],
        [pl.BlockSpec((rows, depth), lambda t, s: (0, 0))],
        [pltpu.VMEM((rows, depth), f32)],
        2 * rows * depth * tw * steps * len(sets),
    )[0]


def feed_forward(normed, gate_tiles, up_tiles, seats):
    rows, tw = normed.shape[0], gate_tiles.width

    def body(step, weights, ins, outs, own):
        a = ins[0][...]
        gate = dot_nn(a, weights[0][...])
        up = dot_nn(a, weights[1][...])
        outs[0][...] = (gate * jax.nn.sigmoid(gate) * up).astype(bf16)
        outs[1][...] = gate.astype(bf16)
        outs[2][...] = up.astype(bf16)

    shape = jax.ShapeDtypeStruct((gate_tiles.quarters, rows, gate_tiles.parts * tw), bf16)
    return tiled_call(
        body,
        [gate_tiles, up_tiles],
        seats,
        [normed],
        [whole(normed)],
        [shape] * 3,
        [seated(rows, tw, gate_tiles.parts)] * 3,
        [],
        4 * rows * normed.shape[1] * tw * gate_tiles.steps,
    )


def feed_back(cotangent, gate, up, down_tiles, seats):
    rows, tw = cotangent.shape[0], down_tiles.width

    def body(step, weights, ins, outs, own):
        grad = dot_nn(ins[0][...], weights[0][...])
        g = ins[1][...].astype(f32)
        u = ins[2][...].astype(f32)
        s = jax.nn.sigmoid(g)
        outs[0][...] = (grad * u * s * (1.0 + g * (1.0 - s))).astype(bf16)
        outs[1][...] = (grad * (g * s)).astype(bf16)

    shape = jax.ShapeDtypeStruct(gate.shape, bf16)
    tile = seated(rows, tw, down_tiles.parts)
    return tiled_call(
        body,
        [down_tiles],
        seats,
        [cotangent, gate, up],
        [whole(cotangent), tile, tile],
        [shape] * 2,
        [tile] * 2,
        [],
        2 * rows * cotangent.shape[1] * tw * down_tiles.steps,
    )


def qkv_back(grad_hat, raw, cosine, sine, q_gain, k_gain):
    quarters, rows, width = grad_hat.shape
    tw = width // 2

    def kernel(g_ref, r_ref, cos_ref, sin_ref, qg, kg, out, qsum, ksum):
        @pl.when(pl.program_id(0) == 0)
        def _():
            qsum[...] = jnp.zeros_like(qsum)
            ksum[...] = jnp.zeros_like(ksum)

        def back(cut, gain, total):
            w = g_ref[:, cut].astype(f32)
            w = w * cos_ref[...] + pltpu.roll(w * sin_ref[...], HEAD_DIM // 2, 1)
            x = r_ref[:, cut].astype(f32)
            inverse = lax.rsqrt(jnp.mean(x * x, axis=-1, keepdims=True) + norm_eps)
            u = x * inverse
            wu = w * u
            scaled = w * gain
            out[:, cut] = (
                inverse * (scaled - u * jnp.mean(wu * gain, axis=-1, keepdims=True))
            ).astype(bf16)
            return total + jnp.sum(wu, axis=0, keepdims=True)

        total = jnp.zeros((1, HEAD_DIM), f32)
        cuts = head_slices(width)
        n_query, n_key = tw // HEAD_DIM, tw // HEAD_DIM // 2
        for cut in cuts[:n_query]:
            total = back(cut, qg[...], total)
        qsum[...] += total
        total = jnp.zeros((1, HEAD_DIM), f32)
        for cut in cuts[n_query : n_query + n_key]:
            total = back(cut, kg[...], total)
        ksum[...] += total
        out[:, tw + tw // 2 :] = g_ref[:, tw + tw // 2 :]

    ins = [grad_hat, raw, cosine, sine, q_gain, k_gain]
    gain_shape = jax.ShapeDtypeStruct((1, HEAD_DIM), f32)
    out_shape = [jax.ShapeDtypeStruct(grad_hat.shape, bf16), gain_shape, gain_shape]
    tile = pl.BlockSpec((None, rows, width), lambda e: (e, 0, 0))
    fixed = lambda x: pl.BlockSpec(x.shape, lambda e: (0, 0))
    return pl.pallas_call(
        kernel,
        grid=(quarters,),
        in_specs=[tile, tile] + [fixed(x) for x in ins[2:]],
        out_specs=[tile, fixed(gain_shape), fixed(gain_shape)],
        out_shape=out_shape,
        compiler_params=params(),
        cost_estimate=cost(40 * quarters * rows * width, nbytes(ins) + nbytes(out_shape)),
    )(*ins)


def attention_specs(kv):
    q = pl.BlockSpec((TREE_TOK, GROUP * HEAD_DIM), lambda n, s: (0, n))
    k = pl.BlockSpec((TREE_TOK, HEAD_DIM), lambda n, s: (0, GROUP * kv + n))
    v = pl.BlockSpec((TREE_TOK, HEAD_DIM), lambda n, s: (0, (GROUP + 1) * kv + n))
    return q, k, v


def stacked(ref, start):
    rows = pl.ds(start, BRANCH)
    return jnp.concatenate(
        [ref[rows, h * HEAD_DIM : (h + 1) * HEAD_DIM] for h in range(GROUP)], axis=0
    )


def causal():
    key = lax.broadcasted_iota(jnp.int32, (BRANCH, GROUP * BRANCH), 0)
    query = lax.rem(lax.broadcasted_iota(jnp.int32, (BRANCH, GROUP * BRANCH), 1), BRANCH)
    return key <= query


TRUNK_BLOCKS = TRUNK // BRANCH
BLOCKS = TREE_TOK // BRANCH


def attention_forward(qkv, parents, kv):
    def kernel(parent_ref, q_ref, k_ref, v_ref, out_ref, log_ref, vt):
        vt[...] = v_ref[...].T
        mask = causal()

        def part(q, start, size, rule):
            score = dot_nt(k_ref[pl.ds(start, size), :], q)
            weight = jnp.exp2(score)
            if rule is not None:
                weight = rule(weight)
            out = dot_nn(vt[:, pl.ds(start, size)], weight.astype(bf16))
            return out, jnp.sum(weight, axis=0, keepdims=True)

        def finish(block, start, pieces):
            out = sum(p[0] for p in pieces)
            total = sum(p[1] for p in pieces)
            out = (out / total).T.astype(bf16)
            for h in range(GROUP):
                out_ref[pl.ds(start, BRANCH), h * HEAD_DIM : (h + 1) * HEAD_DIM] = out[
                    h * BRANCH : (h + 1) * BRANCH
                ]
            log_ref[0, pl.ds(block, 1), :] = jnp.log2(total)

        diagonal = lambda w: jnp.where(mask, w, 0.0)
        for block in range(TRUNK_BLOCKS):
            q = stacked(q_ref, block * BRANCH)
            pieces = [part(q, block * BRANCH, BRANCH, diagonal)]
            if block > 0:
                pieces.append(part(q, 0, block * BRANCH, None))
            finish(block, block * BRANCH, pieces)

        def branch(i, carry):
            block = TRUNK_BLOCKS + i
            start = pl.multiple_of(block * BRANCH, BRANCH)
            q = stacked(q_ref, start)
            parent = parent_ref[i]
            has = (parent != block).astype(f32)
            pieces = [
                part(q, start, BRANCH, diagonal),
                part(q, pl.multiple_of(parent * BRANCH, BRANCH), BRANCH, lambda w: w * has),
                part(q, 0, TRUNK, None),
            ]
            finish(block, start, pieces)
            return carry

        lax.fori_loop(0, FORKS2, branch, 0)

    q, k, v = attention_specs(kv)
    out_shape = [
        jax.ShapeDtypeStruct((TREE_TOK, GROUP * kv * HEAD_DIM), bf16),
        jax.ShapeDtypeStruct((kv, BLOCKS, GROUP * BRANCH), f32),
    ]
    return pl.pallas_call(
        kernel,
        grid_spec=pltpu.PrefetchScalarGridSpec(
            num_scalar_prefetch=1,
            grid=(kv,),
            in_specs=[q, k, v],
            out_specs=[
                q,
                pl.BlockSpec((1, BLOCKS, GROUP * BRANCH), lambda n, s: (n, 0, 0)),
            ],
            scratch_shapes=[pltpu.VMEM((HEAD_DIM, TREE_TOK), bf16)],
        ),
        out_shape=out_shape,
        compiler_params=params(),
        cost_estimate=cost(kv * 2.2e6 * 2 * GROUP * 256 * 2, nbytes([qkv]) + nbytes(out_shape)),
    )(parents, qkv, qkv, qkv)


def attention_backward(qkv, attended, grads, logs, parents, kv):
    width = qkv.shape[1]

    def kernel(
        parent_ref, q_ref, k_ref, v_ref, o_ref, do_ref, log_ref, out_ref, kt, dk, dv, dq_ref
    ):
        kt[...] = k_ref[...].T
        dk[...] = jnp.zeros_like(dk)
        dv[...] = jnp.zeros_like(dv)
        mask = causal()

        def part(q, do, log, delta, start, size, rule):
            rows = pl.ds(start, size)
            prob = jnp.exp2(dot_nt(k_ref[rows, :], q) - log)
            if rule is not None:
                prob = rule(prob)
            grad = dot_nt(v_ref[rows, :], do)
            score_grad = (prob * (grad - delta)).astype(bf16)
            dk[rows, :] += dot_nn(score_grad, q)
            dv[rows, :] += dot_nn(prob.astype(bf16), do)
            return dot_nn(kt[:, rows], score_grad)

        def one(block, start, ranges):
            q = stacked(q_ref, start)
            do = stacked(do_ref, start)
            o = stacked(o_ref, start)
            delta = jnp.sum((do.astype(f32) * o.astype(f32)).T, axis=0, keepdims=True)
            log = log_ref[0, pl.ds(block, 1), :]
            total = sum(part(q, do, log, delta, *r) for r in ranges)
            out = (total * LN2).T.astype(bf16)
            for h in range(GROUP):
                dq_ref[pl.ds(start, BRANCH), h * HEAD_DIM : (h + 1) * HEAD_DIM] = out[
                    h * BRANCH : (h + 1) * BRANCH
                ]

        diagonal = lambda p: jnp.where(mask, p, 0.0)
        for block in range(TRUNK_BLOCKS):
            ranges = [(block * BRANCH, BRANCH, diagonal)]
            if block > 0:
                ranges.append((0, block * BRANCH, None))
            one(block, block * BRANCH, ranges)

        def branch(i, carry):
            block = TRUNK_BLOCKS + i
            start = pl.multiple_of(block * BRANCH, BRANCH)
            parent = parent_ref[i]
            has = (parent != block).astype(f32)
            one(
                block,
                start,
                [
                    (start, BRANCH, diagonal),
                    (pl.multiple_of(parent * BRANCH, BRANCH), BRANCH, lambda p: p * has),
                    (0, TRUNK, None),
                ],
            )
            return carry

        lax.fori_loop(0, FORKS2, branch, 0)
        for head in range(kv):

            @pl.when(pl.program_id(0) == head)
            def _(head=head):
                wide = GROUP * HEAD_DIM
                out_ref[:, head * wide : (head + 1) * wide] = dq_ref[...]
                at = kv * wide + head * HEAD_DIM
                out_ref[:, at : at + HEAD_DIM] = (dk[...] * score_scale).astype(bf16)
                at += kv * HEAD_DIM
                out_ref[:, at : at + HEAD_DIM] = dv[...].astype(bf16)

    q, k, v = attention_specs(kv)
    out_shape = jax.ShapeDtypeStruct((TREE_TOK, width), bf16)
    return pl.pallas_call(
        kernel,
        grid_spec=pltpu.PrefetchScalarGridSpec(
            num_scalar_prefetch=1,
            grid=(kv,),
            in_specs=[
                q,
                k,
                v,
                q,
                q,
                pl.BlockSpec((1, BLOCKS, GROUP * BRANCH), lambda n, s: (n, 0, 0)),
            ],
            out_specs=pl.BlockSpec((TREE_TOK, width), lambda n, s: (0, 0)),
            scratch_shapes=[
                pltpu.VMEM((HEAD_DIM, TREE_TOK), bf16),
                pltpu.VMEM((TREE_TOK, HEAD_DIM), f32),
                pltpu.VMEM((TREE_TOK, HEAD_DIM), f32),
                pltpu.VMEM((TREE_TOK, GROUP * HEAD_DIM), bf16),
            ],
        ),
        out_shape=out_shape,
        compiler_params=params(),
        cost_estimate=cost(
            kv * 2.2e6 * 2 * GROUP * 640 * 2, nbytes([qkv, attended, grads, qkv])
        ),
    )(parents, qkv, qkv, qkv, attended, grads, logs)


def weight_gradient(lefts, rights, half, cut=None):
    pairs = len(lefts)
    rows, depth = lefts[0].shape
    quarters, _, width = rights[0].shape
    size = depth // 2
    if cut is None:
        tw = width // 2 if width > 1024 else width
        parts, first = width // tw, 0
    else:
        width = tw = width // 2
        parts, first = 1, cut

    def kernel(*refs):
        left_refs, right_refs = refs[:pairs], refs[pairs : 2 * pairs]
        out_ref, left_s, right_s = refs[2 * pairs :]

        @pl.when(pl.program_id(0) == 0)
        def _():
            for i, ref in enumerate(left_refs):
                left_s[i * rows : (i + 1) * rows] = ref[...]

        for i, ref in enumerate(right_refs):
            right_s[i * rows : (i + 1) * rows] = ref[...]
        out_ref[...] = contract_rows(left_s[...], right_s[...]).astype(bf16)

    out_shape = jax.ShapeDtypeStruct((size, quarters * width), bf16)
    arrays = list(lefts) + list(rights)
    return pl.pallas_call(
        kernel,
        grid=(quarters * parts,),
        in_specs=[pl.BlockSpec((rows, size), lambda t: (0, half))] * pairs
        + [pl.BlockSpec((None, rows, tw), lambda t: (t // parts, 0, first + t % parts))] * pairs,
        out_specs=pl.BlockSpec((size, tw), lambda t: (0, t)),
        out_shape=out_shape,
        scratch_shapes=[
            pltpu.VMEM((pairs * rows, size), bf16),
            pltpu.VMEM((pairs * rows, tw), bf16),
        ],
        compiler_params=params(),
        cost_estimate=cost(
            2 * pairs * rows * size * quarters * width, nbytes(arrays) + nbytes([out_shape])
        ),
    )(*arrays)


def flipped(index, mask):
    bit = 1
    while bit <= mask:
        if mask & bit:
            index = index + bit * (1 - 2 * lax.rem(lax.div(index, bit), 2))
        bit *= 2
    return index


def transfer_call(
    program, m, n, ins, outs, scratch, count, locals_, number, vmem_ins=(), aliases=None
):
    n_in, n_out, n_scratch = len(ins), len(outs), len(scratch)

    class Mover:
        def __init__(self, send, recv, own):
            self.send, self.recv, self.own = send, recv, own
            self.made, self.local = [], []

        def start(self, source, target, axis, mask):
            k = len(self.made)
            place = flipped(lax.axis_index(axis), mask)
            copy = pltpu.make_async_remote_copy(
                src_ref=source,
                dst_ref=target,
                send_sem=self.send.at[k],
                recv_sem=self.recv.at[k],
                device_id={axis: place},
                device_id_type=pl.DeviceIdType.MESH,
            )
            copy.start()
            self.made.append(copy)
            return copy

        def keep(self, source, target):
            copy = pltpu.make_async_copy(source, target, self.own.at[len(self.local)])
            copy.start()
            self.local.append(copy)
            return copy

    def kernel(*refs):
        in_refs, out_refs = refs[:n_in], refs[n_in : n_in + n_out]
        rest = refs[n_in + n_out :]
        mover = Mover(*rest[n_scratch:])
        barrier = pltpu.get_barrier_semaphore()
        partners = [("wide", k) for k in range(1, m)] if m != 8 else [
            ("wide", k) for k in (1, 2, 4)
        ]
        partners += [("tp", e) for e in range(1, n)]
        for axis, mask in partners:
            pl.semaphore_signal(
                barrier,
                inc=1,
                device_id={axis: flipped(lax.axis_index(axis), mask)},
                device_id_type=pl.DeviceIdType.MESH,
            )
        pl.semaphore_wait(barrier, len(partners))
        program(mover, in_refs, out_refs, rest[:n_scratch])
        for copy in mover.made:
            copy.wait_send()

    return pl.pallas_call(
        kernel,
        in_specs=[
            pl.BlockSpec(memory_space=pltpu.VMEM if i in vmem_ins else pl.ANY) for i in range(n_in)
        ],
        out_specs=[pl.BlockSpec(memory_space=pl.ANY)] * n_out,
        out_shape=outs,
        scratch_shapes=list(scratch)
        + [
            pltpu.SemaphoreType.DMA((count,)),
            pltpu.SemaphoreType.DMA((count,)),
            pltpu.SemaphoreType.DMA((locals_,)),
        ],
        input_output_aliases=aliases or {},
        compiler_params=pltpu.CompilerParams(
            collective_id=number, has_side_effects=True, vmem_limit_bytes=VMEM
        ),
        cost_estimate=cost(0, 1e6),
    )(*ins)


class Spread:
    def __init__(self, mover, m, source, target, block):
        self.mover, self.m, self.source, self.block = mover, m, source, block
        self.at = lambda start, size: target(pl.ds(start, size))

    def first(self):
        go, block, source = self.mover.start, self.block, self.source
        if self.m != 8:
            self.all = [
                go(source, self.at(k * block, block), "wide", k) for k in range(1, self.m)
            ]
            return
        self.x = go(source, self.at(block, block), "wide", 2)
        self.y = go(source, self.at(2 * block, block), "wide", 4)
        self.cores = [go(source, self.at(4 * block, block), "wide", 1)]

    def second(self):
        if self.m != 8:
            return
        go, block = self.mover.start, self.block
        half = block // 2
        self.x.wait_recv()
        low = self.at(block + half, half)
        self.low = go(low, self.at(3 * block + half, half), "wide", 4)
        self.cores.append(go(self.at(block, block), self.at(5 * block, block), "wide", 1))
        self.y.wait_recv()
        top = self.at(2 * block, half)
        self.top = go(top, self.at(3 * block, half), "wide", 2)
        self.cores.append(go(self.at(2 * block, block), self.at(6 * block, block), "wide", 1))

    def third(self):
        if self.m != 8:
            return
        go, block = self.mover.start, self.block
        self.low.wait_recv()
        self.top.wait_recv()
        self.cores.append(go(self.at(3 * block, block), self.at(7 * block, block), "wide", 1))

    def last(self):
        for copy in self.all if self.m != 8 else self.cores:
            copy.wait_recv()


def struct(*shape):
    return jax.ShapeDtypeStruct(shape, bf16)


def gather_front(m, n, qkv_block, in_block, down_block):
    block, qw = qkv_block.shape
    fw, dw = in_block.shape[1], down_block.shape[1]
    depth = block * m
    pairs = n // 2

    def program(mover, ins, outs, _):
        qkv, inner, down = ins
        weights, in_own, in_rest, down_rest = outs
        rows = pl.ds(0, block)
        waves = [mover.start(qkv, weights.at[e, rows], "tp", e) for e in range(1, n)]
        kept = [mover.keep(qkv, weights.at[0, rows]), mover.keep(inner, in_own.at[0, rows])]
        spreads = [
            Spread(
                mover,
                m,
                qkv if q == 0 else weights.at[q, rows],
                lambda r, q=q: weights.at[q, r],
                block,
            )
            for q in range(n)
        ]
        spreads[0].first()
        spreads[0].second()
        spreads[0].third()
        for q in range(1, n):
            waves[q - 1].wait_recv()
            spreads[q].first()
        late = []
        for e in range(1, pairs):
            late.append(mover.start(inner, in_rest.at[e - 1, rows], "tp", 2 * e))
            late.append(mover.start(down, down_rest.at[e - 1, rows], "tp", 2 * e))
        for q in range(1, n):
            spreads[q].second()
        own = Spread(mover, m, inner, lambda r: in_own.at[0, r], block)
        own.first()
        for q in range(1, n):
            spreads[q].third()
        own.second()
        own.third()
        for spread in spreads:
            spread.last()
        own.last()
        for copy in late:
            copy.wait_recv()
        for copy in kept:
            copy.wait()

    per = 8 if m == 8 else m - 1
    return transfer_call(
        program,
        m,
        n,
        [qkv_block, in_block, down_block],
        [
            struct(n, depth, qw),
            struct(1, depth, fw),
            struct(pairs - 1, depth, fw),
            struct(pairs - 1, depth, dw),
        ],
        [],
        (n - 1) + per * (n + 1) + 2 * (pairs - 1),
        2,
        1,
        vmem_ins=(0, 1, 2),
    )


def swap_heads(mover, n, mine, source, target):
    seat = lax.axis_index("tp")
    load = mover.keep(source.at[seat], mine)
    sends = [
        mover.start(source.at[flipped(seat, e)], target.at[seat], "tp", e) for e in range(1, n)
    ]
    load.wait()
    return sends, mover.keep(mine, target.at[seat])


def gather_middle(m, n, hats, in_rest, out_block, down_block):
    quarters, rows, width = hats.shape
    pairs, depth, fw = in_rest.shape
    block, ow = out_block.shape
    dw = down_block.shape[1]

    def program(mover, ins, outs, scratch):
        hat, _, out, down = ins
        heads, rest, weights, down_own = outs
        first = pl.ds(0, block)
        kept = [mover.keep(out, weights.at[0, first]), mover.keep(down, down_own.at[0, first])]
        waves = [mover.start(out, weights.at[e, first], "tp", e) for e in range(1, n)]
        spreads = [
            Spread(mover, m, rest.at[p, first], lambda r, p=p: rest.at[p, r], block)
            for p in range(pairs)
        ]
        for spread in spreads:
            spread.first()
        for copy in waves:
            copy.wait_recv()
        sends, own_row = swap_heads(mover, n, scratch[0], hat, heads)
        kept[0].wait()
        for spread in spreads:
            spread.second()
        quarter = Spread(mover, m, weights.at[:, first], lambda r: weights.at[:, r], block)
        quarter.first()
        for spread in spreads:
            spread.third()
        quarter.second()
        own = Spread(mover, m, down, lambda r: down_own.at[0, r], block)
        own.first()
        quarter.third()
        own.second()
        own.third()
        for spread in spreads + [own, quarter]:
            spread.last()
        for copy in sends:
            copy.wait_recv()
        kept[1].wait()
        own_row.wait()

    per = 8 if m == 8 else m - 1
    return transfer_call(
        program,
        m,
        n,
        [hats, in_rest, out_block, down_block],
        [
            struct(n, rows, width),
            struct(pairs, depth, fw),
            struct(n, depth, ow),
            struct(1, depth, dw),
        ],
        [pltpu.VMEM((rows, width), bf16)],
        2 * (n - 1) + per * (pairs + 2),
        4,
        2,
        vmem_ins=(2, 3),
        aliases={1: 1},
    )


def gather_late(m, n, heads, down_rest):
    quarters, rows, width = heads.shape
    pairs, depth, dw = down_rest.shape
    block = depth // m

    def program(mover, ins, outs, scratch):
        source, _ = ins
        target, rest = outs
        first = pl.ds(0, block)
        sends, own_row = swap_heads(mover, n, scratch[0], source, target)
        spreads = [
            Spread(mover, m, rest.at[p, first], lambda r, p=p: rest.at[p, r], block)
            for p in range(pairs)
        ]
        for stage in ("first", "second", "third", "last"):
            for spread in spreads:
                getattr(spread, stage)()
        for copy in sends:
            copy.wait_recv()
        own_row.wait()

    per = 8 if m == 8 else m - 1
    return transfer_call(
        program,
        m,
        n,
        [heads, down_rest],
        [struct(n, rows, width), struct(pairs, depth, dw)],
        [pltpu.VMEM((rows, width), bf16)],
        (n - 1) + per * pairs,
        2,
        3,
        aliases={1: 1},
    )


def shuffle_columns(a, order):
    rows, count = a.shape[0], order.shape[0]
    width = a.shape[1] // count

    def kernel(order_ref, in_ref, out_ref):
        out_ref[...] = in_ref[...]

    return pl.pallas_call(
        kernel,
        grid_spec=pltpu.PrefetchScalarGridSpec(
            num_scalar_prefetch=1,
            grid=(count,),
            in_specs=[pl.BlockSpec((rows, width), lambda k, s: (0, s[k]))],
            out_specs=pl.BlockSpec((rows, width), lambda k, s: (0, k)),
        ),
        out_shape=jax.ShapeDtypeStruct(a.shape, a.dtype),
        cost_estimate=cost(0, 2 * nbytes([a])),
    )(order, a)


def inverse_rms(values):
    return lax.rsqrt(jnp.mean(values * values, axis=-1, keepdims=True) + norm_eps)


def norm_back(grads, unit_values, inverse, gain):
    scaled = grads * gain
    return inverse * (scaled - unit_values * jnp.mean(scaled * unit_values, axis=-1, keepdims=True))


def after(values, *conditions):
    return lax.optimization_barrier((values, conditions))[0]


class Job:
    def __init__(self, stages):
        self.stages = stages
        self.result = None
        self.started, self.pending = next(stages)

    def advance(self, came):
        try:
            self.started, self.pending = self.stages.send(came)
        except StopIteration as stop:
            self.result = stop.value
            self.pending = None

    def finish(self):
        while self.result is None:
            self.advance(self.pending)
        return self.result


def tick(values, *jobs):
    jobs = [j for j in jobs if j.result is None]
    values, came = lax.optimization_barrier((values, [j.pending for j in jobs]))
    for j, c in zip(jobs, came):
        j.advance(c)
    return values


def local(
    m,
    n,
    tokens,
    out_grad,
    seg_ids,
    parent_table,
    path_pos,
    attn_gain,
    w_query,
    w_key,
    w_value,
    w_out,
    q_gain,
    k_gain,
    ffn_gain,
    w_gate,
    w_up,
    w_down,
):
    rows, depth = tokens.shape
    block = depth // m
    order = [0, 2, 4, 6, 1, 3, 5, 7] if m == 8 else list(range(m))
    where = lax.axis_index("wide").astype(jnp.int32)
    seat = lax.axis_index("tp").astype(jnp.int32)
    relative = jnp.asarray(order, jnp.int32) ^ where
    inverse_order = [order.index(k) for k in range(m)]
    absolute = jnp.take(jnp.asarray(inverse_order, jnp.int32), jnp.arange(m, dtype=jnp.int32) ^ where)
    seats = jnp.arange(n, dtype=jnp.int32) ^ seat
    plain = jnp.arange(n, dtype=jnp.int32)

    def over(axis, a, mask):
        size = m if axis == "wide" else n
        return lax.ppermute(a, axis, [(i, i ^ mask) for i in range(size)])

    def scatter(mine, other):
        if m != 8:
            both = jnp.concatenate([mine, other])
            got = yield both, [over("wide", both[k * block : (k + 1) * block], k) for k in range(1, m)]
            return sum((g.astype(f32) for g in got), both[:block].astype(f32))
        half = block // 2
        (came,) = yield (mine, other), [over("wide", other, 1)]

        def total(start, size):
            cut = slice(start, start + size)
            return mine[cut].astype(f32) + came[cut].astype(f32)

        sources = [
            total(3 * block, half).astype(bf16),
            total(3 * block + half, half).astype(bf16),
        ]
        top, low = yield sources, [over("wide", sources[0], 2), over("wide", sources[1], 4)]
        for_x = jnp.concatenate(
            [
                total(block, half).astype(bf16),
                (total(block + half, half) + low.astype(f32)).astype(bf16),
            ]
        )
        for_y = jnp.concatenate(
            [
                (total(2 * block, half) + top.astype(f32)).astype(bf16),
                total(2 * block + half, half).astype(bf16),
            ]
        )
        from_x, from_y = yield [for_x, for_y], [over("wide", for_x, 2), over("wide", for_y, 4)]
        return total(0, block) + from_x.astype(f32) + from_y.astype(f32)

    def wide_products(left, rights, cut=None):
        other = weight_gradient(left, rights, 1, cut)
        return weight_gradient(after(left, other), rights, 0, cut), other

    cotangent = shuffle_columns(out_grad, relative)

    def ffn_share(left, rights):
        total = yield from scatter(*wide_products(left, rights))
        parts = [total[:, e * fcols : (e + 1) * fcols].astype(bf16) for e in range(1, n // 2)]
        sent = yield parts, [over("tp", p, 2 * (e + 1)) for e, p in enumerate(parts)]
        return sum((x.astype(f32) for x in sent), total[:, :fcols])

    def swap(a):
        return lax.all_to_all(a, "tp", split_axis=0, concat_axis=0, tiled=True)

    def attn_share(left, right, cut=None):
        total = yield from scatter(*wide_products([left], [right], cut))
        parts = total.astype(bf16).reshape(block, n, -1).transpose(1, 0, 2)
        (came,) = yield parts, [swap(parts)]
        return jnp.sum(came.astype(f32), axis=0)

    def gather_small(a):
        stack = a[None]
        size = 1
        while size < m:
            stack = jnp.concatenate([stack, over("wide", stack, order[size])])
            size *= 2
        return stack

    qkv_block = jnp.concatenate([w_query, w_key, w_value], axis=1)
    out_block = w_out.T
    in_block = jnp.concatenate([w_gate, w_up], axis=1)
    down_block = w_down.T
    aw = w_query.shape[1]
    kv = w_key.shape[1] // HEAD_DIM
    fcols = w_gate.shape[1]
    fw = fcols // 3

    gains = gather_small(jnp.concatenate([attn_gain, ffn_gain, q_gain, k_gain])[None])[:, 0]
    gains = gains.astype(f32)
    small = q_gain.shape[0]
    gain_one = gains[:, :block].reshape(1, depth)
    gain_two = gains[:, block : 2 * block].reshape(1, depth)
    head_gains = jnp.take(gains[:, 2 * block :], absolute, axis=0)
    gain_q = head_gains[:, :small].reshape(1, HEAD_DIM)
    gain_k = head_gains[:, small:].reshape(1, HEAD_DIM)

    base = where * parent_table.shape[0]
    block_segs = seg_ids[TRUNK::BRANCH] - base
    hit = block_segs[:, None] == jnp.arange(parent_table.shape[0], dtype=jnp.int32)[None, :]
    block_parents = jnp.sum(jnp.where(hit, parent_table[None, :] - base, 0), axis=1)
    match = block_parents[:, None] == block_segs[None, :]
    number = TRUNK_BLOCKS + jnp.arange(FORKS2, dtype=jnp.int32)
    parents = jnp.where(
        jnp.any(match, axis=1), jnp.sum(jnp.where(match, number[None, :], 0), axis=1), number
    ).astype(jnp.int32)

    own_pos = lax.dynamic_slice_in_dim(path_pos, seat * rows, rows, 0).astype(f32)
    frequency = rope_base ** (-(jnp.arange(HEAD_DIM // 2, dtype=f32) * 2.0) / HEAD_DIM)
    angles = own_pos[:, None] * frequency[None, :]
    cosine, sine = jnp.cos(angles), jnp.sin(angles)
    cosine = jnp.concatenate([cosine, cosine], axis=-1)
    sine = jnp.concatenate([-sine, sine], axis=-1)

    stream = shuffle_columns(tokens, relative).astype(f32)
    inverse_one = inverse_rms(stream)
    unit_one = stream * inverse_one
    normed_one = (unit_one * gain_one).astype(bf16)

    qkv_all, in_own, in_rest, down_rest = gather_front(m, n, qkv_block, in_block, down_block)
    qkv_tiles = Tiles([qkv_all], 2, 0, aw)
    hats, raws = project_qkv(normed_one, qkv_tiles, seats, cosine, sine, gain_q, gain_k)
    qkv, in_rest, out_all, down_own = gather_middle(m, n, hats, in_rest, out_block, down_block)
    qkv = qkv.reshape(n * rows, -1)
    attended_heads, logs = attention_forward(qkv, parents, kv)
    attended, down_rest = gather_late(m, n, attended_heads.reshape(n, rows, -1), down_rest)
    out_tiles = Tiles([out_all], 1, 0, aw)
    after_attn = stream + project_columns([attended], [out_tiles], seats, depth, f32)

    inverse_two = inverse_rms(after_attn)
    unit_two = after_attn * inverse_two
    normed_two = (unit_two * gain_two).astype(bf16)
    normed_two_next = over("tp", normed_two, 1)

    gate_tiles = Tiles([in_own, in_rest], 3, 0, fw)
    up_tiles = Tiles([in_own, in_rest], 3, 3, fw)
    down_tiles = Tiles([down_own, down_rest], 3, 0, fw)

    hidden, gate, up = feed_forward(normed_two, gate_tiles, up_tiles, plain)
    down = project_columns([hidden], [down_tiles], plain, depth, f32)
    normed_two_next, cotangent_sent = after((normed_two_next, cotangent), (down, normed_two_next))
    cotangent_next = over("tp", cotangent_sent, 1)
    hidden_next, gate_next, up_next = feed_forward(normed_two_next, gate_tiles, up_tiles, plain)
    down_part = project_columns([hidden_next], [down_tiles], plain, depth, bf16)
    cotangent_next, hidden_late = after((cotangent_next, hidden), down_part)
    down_job = Job(ffn_share([cotangent, cotangent_next], [hidden_late, hidden_next]))
    cotangent_next = after(cotangent_next, down_job.started)
    gate_grad_next, up_grad_next = feed_back(
        cotangent_next, gate_next, up_next, down_tiles, plain
    )
    back_part = project_columns(
        [gate_grad_next, up_grad_next], [gate_tiles, up_tiles], plain, depth, bf16
    )
    back_next = over("tp", back_part, 1)
    own_grad = tick(after(cotangent, back_part), down_job)
    own_grad = after(own_grad, down_job.started)
    gate_grad, up_grad = feed_back(own_grad, gate, up, down_tiles, plain)
    gate_job = Job(ffn_share([normed_two, normed_two_next], [gate_grad, gate_grad_next]))
    gate_late, up_late = after((gate_grad, up_grad), gate_job.started)
    gate_late, up_late = tick((gate_late, up_late), down_job, gate_job)
    gate_late, up_late = after((gate_late, up_late), down_job.started, gate_job.started)
    back = project_columns([gate_late, up_late], [gate_tiles, up_tiles], plain, depth, f32)
    back, back_next = after((back, back_next), back)
    back = tick(back, down_job, gate_job)
    back = after(back, down_job.started, gate_job.started)
    normed_two_grad = back + back_next.astype(f32)

    ffn_gain_part = jnp.sum(normed_two_grad * unit_two, axis=0)
    stream_grad = cotangent.astype(f32) + norm_back(
        normed_two_grad, unit_two, inverse_two, gain_two
    )
    grad_low = stream_grad.astype(bf16)
    attended_grad = project_rows(grad_low, out_tiles, seats)
    grad_heads = swap(attended_grad).reshape(n * rows, -1)
    grad_heads = tick(grad_heads, gate_job)
    grad_heads = after(grad_heads, gate_job.started)
    down_next = over("tp", after(down_part, grad_heads), 1)
    back_hats = attention_backward(qkv, attended_heads, grad_heads, logs, parents, kv)
    back_hats_own = swap(back_hats.reshape(n, rows, -1))
    lefts, up_grads, grad_low, down_next, after_attn = after(
        (
            [normed_two, normed_two_next],
            [up_grad, up_grad_next],
            grad_low,
            down_next,
            after_attn,
        ),
        back_hats,
    )
    up_job = Job(ffn_share(lefts, up_grads))
    grad_low = tick(after(grad_low, up_job.started), up_job)
    grad_low = after(grad_low, up_job.started)
    out_job = Job(attn_share(grad_low, attended))
    down_next, after_attn = after((down_next, after_attn), out_job.started)
    mixed = (after_attn + down + down_next.astype(f32)).astype(bf16)
    mixed = shuffle_columns(mixed, absolute)
    mixed = tick(mixed, up_job, out_job)
    back_hats_own = after(back_hats_own, mixed, up_job.started, out_job.started)
    raw_grads, q_sum, k_sum = qkv_back(back_hats_own, raws, cosine, sine, gain_q, gain_k)
    q_job = Job(attn_share(normed_one, raw_grads, 0))
    raw_late = after(raw_grads, q_job.started)
    k_job = Job(attn_share(normed_one, raw_late, 1))
    raw_late = tick(after(raw_late, k_job.started), up_job, out_job, q_job)
    raw_late = after(raw_late, q_job.started, out_job.started)
    normed_one_grad = project_columns([raw_late], [qkv_tiles], seats, depth, f32)
    normed_one_grad = tick(normed_one_grad, out_job, q_job, k_job)
    normed_one_grad = after(normed_one_grad, q_job.started, k_job.started)
    attn_gain_part = jnp.sum(normed_one_grad * unit_one, axis=0)
    tokens_grad = (
        stream_grad + norm_back(normed_one_grad, unit_one, inverse_one, gain_one)
    ).astype(bf16)
    tokens_grad = shuffle_columns(tokens_grad, absolute)

    parts = jnp.concatenate(
        [
            attn_gain_part.reshape(m, block),
            ffn_gain_part.reshape(m, block),
            jnp.take(q_sum.reshape(m, small), relative, axis=0),
            jnp.take(k_sum.reshape(m, small), relative, axis=0),
        ],
        axis=1,
    )
    size = m
    while size > 1:
        size //= 2
        parts = parts[:size] + over("wide", parts[size:], order[size])
    step = 1
    while step < n:
        parts = parts + over("tp", parts, step)
        step *= 2
    sums = parts[0]
    gate_share, up_share = gate_job.finish(), up_job.finish()
    down_share, out_share = down_job.finish().T, out_job.finish().T
    q_share, k_share = q_job.finish(), k_job.finish()
    return (
        mixed,
        tokens_grad,
        sums[:block],
        q_share,
        k_share[:, : aw // 2],
        k_share[:, aw // 2 :],
        out_share,
        sums[2 * block : 2 * block + small],
        sums[2 * block + small :],
        sums[block : 2 * block],
        gate_share,
        up_share,
        down_share,
    )


def solution(mesh):
    both = P(("wide", "tp"), None)
    w, wt, tw = P("wide"), P("wide", "tp"), P("tp", "wide")
    return jax.shard_map(
        functools.partial(local, mesh.shape["wide"], mesh.shape["tp"]),
        mesh=mesh,
        in_specs=(both, both, w, w, w, w, wt, wt, wt, tw, w, w, w, wt, wt, tw),
        out_specs=(both, both, w, wt, wt, wt, tw, w, w, w, wt, wt, tw),
        check_vma=False,
    )
```

```python
import functools
import math

import jax
import jax.numpy as jnp
from jax import lax
from jax.experimental import pallas as pl
from jax.experimental.pallas import tpu as pltpu
from jax.sharding import PartitionSpec as P

HEAD_DIM = 128
TRUNK = 1152
BRANCH = 128
FORKS2 = 8
TREE_TOK = 2176
GROUP = 2

norm_eps = 1e-06
rope_base = 1000000.0
score_scale = HEAD_DIM ** (-0.5)
key_scale = score_scale * math.log2(math.e)
LN2 = math.log(2.0)
VMEM = 52 * 1024 * 1024
COST = 0.01
GAIN_ROWS = 16

f32 = jnp.float32
bf16 = jnp.bfloat16


def dot_nn(a, b):
    return lax.dot_general(a, b, (((1,), (0,)), ((), ())), preferred_element_type=f32)


def dot_nt(a, b):
    return lax.dot_general(a, b, (((1,), (1,)), ((), ())), preferred_element_type=f32)


def contract_rows(a, b):
    return lax.dot_general(a, b, (((0,), (0,)), ((), ())), preferred_element_type=f32)


def params():
    return pltpu.CompilerParams(vmem_limit_bytes=VMEM)


def cost(flops, nbytes):
    return pl.CostEstimate(flops=int(flops * COST), bytes_accessed=int(nbytes * COST), transcendentals=0)


def nbytes(arrays):
    return sum(a.size * a.dtype.itemsize for a in arrays)


class Tiles:
    def __init__(self, arrays, parts, base, width):
        self.list = list(arrays)
        self.quarters = sum(a.shape[0] for a in self.list)
        self.depth = self.list[0].shape[1]
        self.parts, self.base, self.width = parts, base, width
        self.steps = self.quarters * parts

    def arrays(self):
        return self.list

    def scratch(self):
        return [pltpu.VMEM((2, self.depth, self.width), bf16), pltpu.SemaphoreType.DMA((2,))]

    def fetch(self, refs, buf, sems, step):
        slot = lax.rem(step, 2)
        quarter = lax.div(step, self.parts)
        part = step - quarter * self.parts
        col = pl.multiple_of((self.base + part) * self.width, 128)

        def begin(ref, at):
            pltpu.make_async_copy(
                ref.at[at, :, pl.ds(col, self.width)], buf.at[slot], sems.at[slot]
            ).start()

        split = self.list[0].shape[0]
        if len(refs) == 1:
            begin(refs[0], quarter)
        else:

            @pl.when(quarter < split)
            def _():
                begin(refs[0], quarter)

            @pl.when(quarter >= split)
            def _():
                begin(refs[1], quarter - split)

    def wait(self, refs, buf, sems, step):
        slot = lax.rem(step, 2)
        pltpu.make_async_copy(
            refs[0].at[0, :, pl.ds(0, self.width)], buf.at[slot], sems.at[slot]
        ).wait()
        return slot


def tiled_call(body, sets, seats, ins, in_specs, out_shape, out_specs, scratch, flops):
    steps = sets[0].steps
    counts = [len(s.arrays()) for s in sets]
    n_in, n_out = len(ins), len(out_shape)

    def kernel(seat_ref, *refs):
        at = 0
        piece_refs = []
        for c in counts:
            piece_refs.append(refs[at : at + c])
            at += c
        in_refs = refs[at : at + n_in]
        at += n_in
        out_refs = refs[at : at + n_out]
        at += n_out
        bufs = [(refs[at + 2 * i], refs[at + 2 * i + 1]) for i in range(len(sets))]
        own = refs[at + 2 * len(sets) :]
        step = pl.program_id(0)

        @pl.when(step == 0)
        def _():
            for s, p, (buf, sems) in zip(sets, piece_refs, bufs):
                s.fetch(p, buf, sems, step)

        @pl.when(step + 1 < steps)
        def _():
            for s, p, (buf, sems) in zip(sets, piece_refs, bufs):
                s.fetch(p, buf, sems, step + 1)

        tiles = []
        for s, p, (buf, sems) in zip(sets, piece_refs, bufs):
            slot = s.wait(p, buf, sems, step)
            tiles.append(buf.at[slot])
        body(step, tiles, in_refs, out_refs, own)

    weights = [a for s in sets for a in s.arrays()]
    return pl.pallas_call(
        kernel,
        grid_spec=pltpu.PrefetchScalarGridSpec(
            num_scalar_prefetch=1,
            grid=(steps,),
            in_specs=[pl.BlockSpec(memory_space=pl.ANY)] * len(weights) + in_specs,
            out_specs=out_specs,
            scratch_shapes=[x for s in sets for x in s.scratch()] + scratch,
        ),
        out_shape=out_shape,
        compiler_params=params(),
        cost_estimate=cost(flops, nbytes(weights) + nbytes(ins) + nbytes(out_shape)),
    )(seats, *weights, *ins)


def whole(array):
    return pl.BlockSpec(array.shape, lambda t, s: (0,) * len(array.shape))


def seated(rows, width, parts):
    return pl.BlockSpec(
        (None, rows, width),
        lambda t, s: (s[lax.div(t, parts)], 0, lax.rem(t, parts)),
    )


def head_slices(width):
    return [slice(h * HEAD_DIM, (h + 1) * HEAD_DIM) for h in range(width // HEAD_DIM)]


def project_qkv(normed, tiles, seats, cosine, sine, q_gain, k_gain):
    rows, tw = normed.shape[0], tiles.width

    def body(step, weights, ins, outs, own):
        a, cos_ref, sin_ref, qg, kg = ins
        hat, raw = outs
        acc = dot_nn(a[...], weights[0][...])
        part = lax.rem(step, 2)

        def turned(x, gain):
            inverse = lax.rsqrt(jnp.mean(x * x, axis=-1, keepdims=True) + norm_eps)
            u = x * inverse * gain
            return u * cos_ref[...] + pltpu.roll(u, HEAD_DIM // 2, 1) * sin_ref[...]

        @pl.when(part == 0)
        def _():
            for cut in head_slices(tw):
                hat[:, cut] = turned(acc[:, cut], qg[...]).astype(bf16)
            raw[...] = acc.astype(bf16)

        @pl.when(part == 1)
        def _():
            for cut in head_slices(tw // 2):
                hat[:, cut] = (turned(acc[:, cut], kg[...]) * key_scale).astype(bf16)
            hat[:, tw // 2 :] = acc[:, tw // 2 :].astype(bf16)
            raw[...] = acc.astype(bf16)

    ins = [normed, cosine, sine, q_gain, k_gain]
    shape = jax.ShapeDtypeStruct((tiles.quarters, rows, 2 * tw), bf16)
    return tiled_call(
        body,
        [tiles],
        seats,
        ins,
        [whole(x) for x in ins],
        [shape, shape],
        [seated(rows, tw, 2)] * 2,
        [],
        4 * rows * normed.shape[1] * tw * tiles.quarters,
    )


def project_rows(a, tiles, seats):
    rows, tw = a.shape[0], tiles.width

    def body(step, weights, ins, outs, own):
        outs[0][...] = dot_nn(ins[0][...], weights[0][...]).astype(bf16)

    return tiled_call(
        body,
        [tiles],
        seats,
        [a],
        [whole(a)],
        [jax.ShapeDtypeStruct((tiles.quarters, rows, tiles.parts * tw), bf16)],
        [seated(rows, tw, tiles.parts)],
        [],
        2 * rows * a.shape[1] * tw * tiles.steps,
    )[0]


def project_columns(lefts, sets, seats, depth, out_dtype):
    rows, tw, steps = lefts[0].shape[1], sets[0].width, sets[0].steps

    def body(step, weights, ins, outs, own):
        acc = own[0]
        total = dot_nt(ins[0][...], weights[0][...])
        for left, weight in zip(ins[1:], weights[1:]):
            total = total + dot_nt(left[...], weight[...])

        @pl.when(step == 0)
        def _():
            acc[...] = total

        @pl.when(step > 0)
        def _():
            acc[...] += total

        @pl.when(step == steps - 1)
        def _():
            outs[0][...] = acc[...].astype(out_dtype)

    return tiled_call(
        body,
        sets,
        seats,
        list(lefts),
        [seated(rows, tw, s.parts) for s in sets],
        [jax.ShapeDtypeStruct((rows, depth), out_dtype)],
        [pl.BlockSpec((rows, depth), lambda t, s: (0, 0))],
        [pltpu.VMEM((rows, depth), f32)],
        2 * rows * depth * tw * steps * len(sets),
    )[0]


def feed_forward(normed, gate_tiles, up_tiles, seats):
    rows, tw = normed.shape[0], gate_tiles.width

    def body(step, weights, ins, outs, own):
        a = ins[0][...]
        gate = dot_nn(a, weights[0][...])
        up = dot_nn(a, weights[1][...])
        outs[0][...] = (gate * jax.nn.sigmoid(gate) * up).astype(bf16)
        outs[1][...] = gate.astype(bf16)
        outs[2][...] = up.astype(bf16)

    shape = jax.ShapeDtypeStruct((gate_tiles.quarters, rows, gate_tiles.parts * tw), bf16)
    return tiled_call(
        body,
        [gate_tiles, up_tiles],
        seats,
        [normed],
        [whole(normed)],
        [shape] * 3,
        [seated(rows, tw, gate_tiles.parts)] * 3,
        [],
        4 * rows * normed.shape[1] * tw * gate_tiles.steps,
    )


def feed_back(cotangent, gate, up, down_tiles, seats):
    rows, tw = cotangent.shape[0], down_tiles.width

    def body(step, weights, ins, outs, own):
        grad = dot_nn(ins[0][...], weights[0][...])
        g = ins[1][...].astype(f32)
        u = ins[2][...].astype(f32)
        s = jax.nn.sigmoid(g)
        outs[0][...] = (grad * u * s * (1.0 + g * (1.0 - s))).astype(bf16)
        outs[1][...] = (grad * (g * s)).astype(bf16)

    shape = jax.ShapeDtypeStruct(gate.shape, bf16)
    tile = seated(rows, tw, down_tiles.parts)
    return tiled_call(
        body,
        [down_tiles],
        seats,
        [cotangent, gate, up],
        [whole(cotangent), tile, tile],
        [shape] * 2,
        [tile] * 2,
        [],
        2 * rows * cotangent.shape[1] * tw * down_tiles.steps,
    )


def qkv_back(grad_hat, raw, cosine, sine, q_gain, k_gain):
    quarters, rows, width = grad_hat.shape
    tw = width // 2

    def kernel(g_ref, r_ref, cos_ref, sin_ref, qg, kg, out, qsum, ksum):
        @pl.when(pl.program_id(0) == 0)
        def _():
            qsum[...] = jnp.zeros_like(qsum)
            ksum[...] = jnp.zeros_like(ksum)

        def back(cut, gain, total):
            w = g_ref[:, cut].astype(f32)
            w = w * cos_ref[...] + pltpu.roll(w * sin_ref[...], HEAD_DIM // 2, 1)
            x = r_ref[:, cut].astype(f32)
            inverse = lax.rsqrt(jnp.mean(x * x, axis=-1, keepdims=True) + norm_eps)
            u = x * inverse
            wu = w * u
            scaled = w * gain
            out[:, cut] = (
                inverse * (scaled - u * jnp.mean(wu * gain, axis=-1, keepdims=True))
            ).astype(bf16)
            return total + jnp.sum(wu, axis=0, keepdims=True)

        total = jnp.zeros((1, HEAD_DIM), f32)
        cuts = head_slices(width)
        n_query, n_key = tw // HEAD_DIM, tw // HEAD_DIM // 2
        for cut in cuts[:n_query]:
            total = back(cut, qg[...], total)
        qsum[...] += total
        total = jnp.zeros((1, HEAD_DIM), f32)
        for cut in cuts[n_query : n_query + n_key]:
            total = back(cut, kg[...], total)
        ksum[...] += total
        out[:, tw + tw // 2 :] = g_ref[:, tw + tw // 2 :]

    ins = [grad_hat, raw, cosine, sine, q_gain, k_gain]
    gain_shape = jax.ShapeDtypeStruct((1, HEAD_DIM), f32)
    out_shape = [jax.ShapeDtypeStruct(grad_hat.shape, bf16), gain_shape, gain_shape]
    tile = pl.BlockSpec((None, rows, width), lambda e: (e, 0, 0))
    fixed = lambda x: pl.BlockSpec(x.shape, lambda e: (0, 0))
    return pl.pallas_call(
        kernel,
        grid=(quarters,),
        in_specs=[tile, tile] + [fixed(x) for x in ins[2:]],
        out_specs=[tile, fixed(gain_shape), fixed(gain_shape)],
        out_shape=out_shape,
        compiler_params=params(),
        cost_estimate=cost(40 * quarters * rows * width, nbytes(ins) + nbytes(out_shape)),
    )(*ins)


def attention_specs(kv):
    q = pl.BlockSpec((TREE_TOK, GROUP * HEAD_DIM), lambda n, s: (0, n))
    k = pl.BlockSpec((TREE_TOK, HEAD_DIM), lambda n, s: (0, GROUP * kv + n))
    v = pl.BlockSpec((TREE_TOK, HEAD_DIM), lambda n, s: (0, (GROUP + 1) * kv + n))
    return q, k, v


def stacked(ref, start):
    rows = pl.ds(start, BRANCH)
    return jnp.concatenate(
        [ref[rows, h * HEAD_DIM : (h + 1) * HEAD_DIM] for h in range(GROUP)], axis=0
    )


def causal():
    key = lax.broadcasted_iota(jnp.int32, (BRANCH, GROUP * BRANCH), 0)
    query = lax.rem(lax.broadcasted_iota(jnp.int32, (BRANCH, GROUP * BRANCH), 1), BRANCH)
    return key <= query


TRUNK_BLOCKS = TRUNK // BRANCH
BLOCKS = TREE_TOK // BRANCH


def attention_forward(qkv, parents, kv):
    def kernel(parent_ref, q_ref, k_ref, v_ref, out_ref, log_ref, vt):
        vt[...] = v_ref[...].T
        mask = causal()

        def part(q, start, size, rule):
            score = dot_nt(k_ref[pl.ds(start, size), :], q)
            weight = jnp.exp2(score)
            if rule is not None:
                weight = rule(weight)
            out = dot_nn(vt[:, pl.ds(start, size)], weight.astype(bf16))
            return out, jnp.sum(weight, axis=0, keepdims=True)

        def finish(block, start, pieces):
            out = sum(p[0] for p in pieces)
            total = sum(p[1] for p in pieces)
            out = (out / total).T.astype(bf16)
            for h in range(GROUP):
                out_ref[pl.ds(start, BRANCH), h * HEAD_DIM : (h + 1) * HEAD_DIM] = out[
                    h * BRANCH : (h + 1) * BRANCH
                ]
            log_ref[0, pl.ds(block, 1), :] = jnp.log2(total)

        diagonal = lambda w: jnp.where(mask, w, 0.0)
        for block in range(TRUNK_BLOCKS):
            q = stacked(q_ref, block * BRANCH)
            pieces = [part(q, block * BRANCH, BRANCH, diagonal)]
            if block > 0:
                pieces.append(part(q, 0, block * BRANCH, None))
            finish(block, block * BRANCH, pieces)

        def branch(i, carry):
            block = TRUNK_BLOCKS + i
            start = pl.multiple_of(block * BRANCH, BRANCH)
            q = stacked(q_ref, start)
            parent = parent_ref[i]
            has = (parent != block).astype(f32)
            pieces = [
                part(q, start, BRANCH, diagonal),
                part(q, pl.multiple_of(parent * BRANCH, BRANCH), BRANCH, lambda w: w * has),
                part(q, 0, TRUNK, None),
            ]
            finish(block, start, pieces)
            return carry

        lax.fori_loop(0, FORKS2, branch, 0)

    q, k, v = attention_specs(kv)
    out_shape = [
        jax.ShapeDtypeStruct((TREE_TOK, GROUP * kv * HEAD_DIM), bf16),
        jax.ShapeDtypeStruct((kv, BLOCKS, GROUP * BRANCH), f32),
    ]
    return pl.pallas_call(
        kernel,
        grid_spec=pltpu.PrefetchScalarGridSpec(
            num_scalar_prefetch=1,
            grid=(kv,),
            in_specs=[q, k, v],
            out_specs=[
                q,
                pl.BlockSpec((1, BLOCKS, GROUP * BRANCH), lambda n, s: (n, 0, 0)),
            ],
            scratch_shapes=[pltpu.VMEM((HEAD_DIM, TREE_TOK), bf16)],
        ),
        out_shape=out_shape,
        compiler_params=params(),
        cost_estimate=cost(kv * 2.2e6 * 2 * GROUP * 256 * 2, nbytes([qkv]) + nbytes(out_shape)),
    )(parents, qkv, qkv, qkv)


def attention_backward(qkv, attended, grads, logs, parents, kv):
    width = qkv.shape[1]

    def kernel(
        parent_ref, q_ref, k_ref, v_ref, o_ref, do_ref, log_ref, out_ref, kt, dk, dv, dq_ref
    ):
        kt[...] = k_ref[...].T
        dk[...] = jnp.zeros_like(dk)
        dv[...] = jnp.zeros_like(dv)
        mask = causal()

        def part(q, do, log, delta, start, size, rule):
            rows = pl.ds(start, size)
            prob = jnp.exp2(dot_nt(k_ref[rows, :], q) - log)
            if rule is not None:
                prob = rule(prob)
            grad = dot_nt(v_ref[rows, :], do)
            score_grad = (prob * (grad - delta)).astype(bf16)
            dk[rows, :] += dot_nn(score_grad, q)
            dv[rows, :] += dot_nn(prob.astype(bf16), do)
            return dot_nn(kt[:, rows], score_grad)

        def one(block, start, ranges):
            q = stacked(q_ref, start)
            do = stacked(do_ref, start)
            o = stacked(o_ref, start)
            delta = jnp.sum((do.astype(f32) * o.astype(f32)).T, axis=0, keepdims=True)
            log = log_ref[0, pl.ds(block, 1), :]
            total = sum(part(q, do, log, delta, *r) for r in ranges)
            out = (total * LN2).T.astype(bf16)
            for h in range(GROUP):
                dq_ref[pl.ds(start, BRANCH), h * HEAD_DIM : (h + 1) * HEAD_DIM] = out[
                    h * BRANCH : (h + 1) * BRANCH
                ]

        diagonal = lambda p: jnp.where(mask, p, 0.0)
        for block in range(TRUNK_BLOCKS):
            ranges = [(block * BRANCH, BRANCH, diagonal)]
            if block > 0:
                ranges.append((0, block * BRANCH, None))
            one(block, block * BRANCH, ranges)

        def branch(i, carry):
            block = TRUNK_BLOCKS + i
            start = pl.multiple_of(block * BRANCH, BRANCH)
            parent = parent_ref[i]
            has = (parent != block).astype(f32)
            one(
                block,
                start,
                [
                    (start, BRANCH, diagonal),
                    (pl.multiple_of(parent * BRANCH, BRANCH), BRANCH, lambda p: p * has),
                    (0, TRUNK, None),
                ],
            )
            return carry

        lax.fori_loop(0, FORKS2, branch, 0)
        for head in range(kv):

            @pl.when(pl.program_id(0) == head)
            def _(head=head):
                wide = GROUP * HEAD_DIM
                out_ref[:, head * wide : (head + 1) * wide] = dq_ref[...]
                at = kv * wide + head * HEAD_DIM
                out_ref[:, at : at + HEAD_DIM] = (dk[...] * score_scale).astype(bf16)
                at += kv * HEAD_DIM
                out_ref[:, at : at + HEAD_DIM] = dv[...].astype(bf16)

    q, k, v = attention_specs(kv)
    out_shape = jax.ShapeDtypeStruct((TREE_TOK, width), bf16)
    return pl.pallas_call(
        kernel,
        grid_spec=pltpu.PrefetchScalarGridSpec(
            num_scalar_prefetch=1,
            grid=(kv,),
            in_specs=[
                q,
                k,
                v,
                q,
                q,
                pl.BlockSpec((1, BLOCKS, GROUP * BRANCH), lambda n, s: (n, 0, 0)),
            ],
            out_specs=pl.BlockSpec((TREE_TOK, width), lambda n, s: (0, 0)),
            scratch_shapes=[
                pltpu.VMEM((HEAD_DIM, TREE_TOK), bf16),
                pltpu.VMEM((TREE_TOK, HEAD_DIM), f32),
                pltpu.VMEM((TREE_TOK, HEAD_DIM), f32),
                pltpu.VMEM((TREE_TOK, GROUP * HEAD_DIM), bf16),
            ],
        ),
        out_shape=out_shape,
        compiler_params=params(),
        cost_estimate=cost(
            kv * 2.2e6 * 2 * GROUP * 640 * 2, nbytes([qkv, attended, grads, qkv])
        ),
    )(parents, qkv, qkv, qkv, attended, grads, logs)


def weight_gradient(lefts, rights, half, cut=None):
    pairs = len(lefts)
    rows, depth = lefts[0].shape
    quarters, _, width = rights[0].shape
    size = depth // 2
    if cut is None:
        tw = width // 2 if width > 1024 else width
        parts, first = width // tw, 0
    else:
        width = tw = width // 2
        parts, first = 1, cut

    def kernel(*refs):
        left_refs, right_refs = refs[:pairs], refs[pairs : 2 * pairs]
        out_ref, left_s, right_s = refs[2 * pairs :]

        @pl.when(pl.program_id(0) == 0)
        def _():
            for i, ref in enumerate(left_refs):
                left_s[i * rows : (i + 1) * rows] = ref[...]

        for i, ref in enumerate(right_refs):
            right_s[i * rows : (i + 1) * rows] = ref[...]
        out_ref[...] = contract_rows(left_s[...], right_s[...]).astype(bf16)

    out_shape = jax.ShapeDtypeStruct((size, quarters * width), bf16)
    arrays = list(lefts) + list(rights)
    return pl.pallas_call(
        kernel,
        grid=(quarters * parts,),
        in_specs=[pl.BlockSpec((rows, size), lambda t: (0, half))] * pairs
        + [pl.BlockSpec((None, rows, tw), lambda t: (t // parts, 0, first + t % parts))] * pairs,
        out_specs=pl.BlockSpec((size, tw), lambda t: (0, t)),
        out_shape=out_shape,
        scratch_shapes=[
            pltpu.VMEM((pairs * rows, size), bf16),
            pltpu.VMEM((pairs * rows, tw), bf16),
        ],
        compiler_params=params(),
        cost_estimate=cost(
            2 * pairs * rows * size * quarters * width, nbytes(arrays) + nbytes([out_shape])
        ),
    )(*arrays)


def flipped(index, mask):
    bit = 1
    while bit <= mask:
        if mask & bit:
            index = index + bit * (1 - 2 * lax.rem(lax.div(index, bit), 2))
        bit *= 2
    return index


def transfer_call(
    program, m, n, ins, outs, scratch, count, locals_, number, vmem_ins=(), aliases=None
):
    n_in, n_out, n_scratch = len(ins), len(outs), len(scratch)

    class Mover:
        def __init__(self, send, recv, own):
            self.send, self.recv, self.own = send, recv, own
            self.made, self.local = [], []

        def start(self, source, target, axis, mask):
            k = len(self.made)
            place = flipped(lax.axis_index(axis), mask)
            copy = pltpu.make_async_remote_copy(
                src_ref=source,
                dst_ref=target,
                send_sem=self.send.at[k],
                recv_sem=self.recv.at[k],
                device_id={axis: place},
                device_id_type=pl.DeviceIdType.MESH,
            )
            copy.start()
            self.made.append(copy)
            return copy

        def keep(self, source, target):
            copy = pltpu.make_async_copy(source, target, self.own.at[len(self.local)])
            copy.start()
            self.local.append(copy)
            return copy

    def kernel(*refs):
        in_refs, out_refs = refs[:n_in], refs[n_in : n_in + n_out]
        rest = refs[n_in + n_out :]
        mover = Mover(*rest[n_scratch:])
        barrier = pltpu.get_barrier_semaphore()
        partners = [("wide", k) for k in range(1, m)] if m != 8 else [
            ("wide", k) for k in (1, 2, 4)
        ]
        partners += [("tp", e) for e in range(1, n)]
        for axis, mask in partners:
            pl.semaphore_signal(
                barrier,
                inc=1,
                device_id={axis: flipped(lax.axis_index(axis), mask)},
                device_id_type=pl.DeviceIdType.MESH,
            )
        pl.semaphore_wait(barrier, len(partners))
        program(mover, in_refs, out_refs, rest[:n_scratch])
        for copy in mover.made:
            copy.wait_send()

    return pl.pallas_call(
        kernel,
        in_specs=[
            pl.BlockSpec(memory_space=pltpu.VMEM if i in vmem_ins else pl.ANY) for i in range(n_in)
        ],
        out_specs=[pl.BlockSpec(memory_space=pl.ANY)] * n_out,
        out_shape=outs,
        scratch_shapes=list(scratch)
        + [
            pltpu.SemaphoreType.DMA((count,)),
            pltpu.SemaphoreType.DMA((count,)),
            pltpu.SemaphoreType.DMA((locals_,)),
        ],
        input_output_aliases=aliases or {},
        compiler_params=pltpu.CompilerParams(
            collective_id=number, has_side_effects=True, vmem_limit_bytes=VMEM
        ),
        cost_estimate=cost(0, 1e6),
    )(*ins)


def swap_own(source, target, mine, sems):
    seat = lax.axis_index("tp")
    return (
        pltpu.make_async_copy(source.at[seat], mine, sems.at[0]),
        pltpu.make_async_copy(mine, target.at[seat], sems.at[1]),
    )


def gradient_pair(lefts, rights, cut, number, ride=None):
    pairs = len(lefts)
    rows, depth = lefts[0].shape
    quarters, _, width = rights[0].shape
    size = depth // 2
    block = size // 4
    half = block // 2
    if cut is None:
        tw = width // 2 if width > 1024 else width
        parts, first = width // tw, 0
    else:
        width = tw = width // 2
        parts, first = 1, cut
    steps = quarters * parts
    n = ride.shape[0] if ride is not None else 1
    rides = [] if ride is None else [ride]

    def kernel(*refs):
        left_refs, right_refs = refs[:pairs], refs[pairs : 2 * pairs]
        at = 2 * pairs
        ride_in = refs[at : at + len(rides)]
        at += len(rides)
        own_ref, x_ref, y_ref, top_ref, low_ref = refs[at : at + 5]
        at += 5
        ride_out = refs[at : at + len(rides)]
        at += len(rides)
        left_s, right_s, sent, came, send_sems, recv_sems = refs[at : at + 6]
        extra = refs[at + 6 :]
        step = pl.program_id(0)
        other_core = {"wide": flipped(lax.axis_index("wide"), 1)}

        def copy(k):
            return pltpu.make_async_remote_copy(
                src_ref=sent.at[k],
                dst_ref=came.at[k],
                send_sem=send_sems.at[k],
                recv_sem=recv_sems.at[k],
                device_id=other_core,
                device_id_type=pl.DeviceIdType.MESH,
            )

        def ride_copies():
            mine, ride_send, ride_recv, own_sems = extra
            seat = lax.axis_index("tp")
            return [
                pltpu.make_async_remote_copy(
                    src_ref=ride_in[0].at[flipped(seat, e)],
                    dst_ref=ride_out[0].at[seat],
                    send_sem=ride_send.at[e - 1],
                    recv_sem=ride_recv.at[e - 1],
                    device_id={"tp": flipped(seat, e)},
                    device_id_type=pl.DeviceIdType.MESH,
                )
                for e in range(1, n)
            ], swap_own(ride_in[0], ride_out[0], mine, own_sems)

        @pl.when(step == 0)
        def _():
            barrier = pltpu.get_barrier_semaphore()
            partners = [other_core] + [
                {"tp": flipped(lax.axis_index("tp"), e)} for e in range(1, n)
            ]
            for partner in partners:
                pl.semaphore_signal(
                    barrier, inc=1, device_id=partner, device_id_type=pl.DeviceIdType.MESH
                )
            pl.semaphore_wait(barrier, len(partners))
            if rides:
                sends, (load, keep) = ride_copies()
                for c in sends:
                    c.start()
                load.start()
                load.wait()
                keep.start()

        @pl.when(lax.rem(step, steps) == 0)
        def _():
            for i, ref in enumerate(left_refs):
                left_s[i * rows : (i + 1) * rows] = ref[...]

        for i, ref in enumerate(right_refs):
            right_s[i * rows : (i + 1) * rows] = ref[...]
        product = contract_rows(left_s[...], right_s[...])

        @pl.when(step < steps)
        def _():
            sent[step] = product.astype(bf16)
            copy(step).start()

        @pl.when(step >= steps)
        def _():
            k = step - steps
            copy(k).wait_recv()
            total = (product + came[k].astype(f32)).astype(bf16)
            own_ref[...] = total[:block]
            x_ref[...] = total[block : 2 * block]
            y_ref[...] = total[2 * block : 3 * block]
            top_ref[...] = total[3 * block : 3 * block + half]
            low_ref[...] = total[3 * block + half :]

        @pl.when(step == 2 * steps - 1)
        def _():
            for k in range(steps):
                copy(k).wait_send()
            if rides:
                sends, (load, keep) = ride_copies()
                for c in sends:
                    c.wait_send()
                    c.wait_recv()
                keep.wait()

    columns = quarters * width
    heights = (block, block, block, half, half)
    out_shape = [struct(h, columns) for h in heights]
    arrays = list(lefts) + list(rights)
    late = lambda t: (0, jnp.maximum(t - steps, 0))
    ride_scratch = (
        []
        if ride is None
        else [
            pltpu.VMEM(ride.shape[1:], bf16),
            pltpu.SemaphoreType.DMA((n - 1,)),
            pltpu.SemaphoreType.DMA((n - 1,)),
            pltpu.SemaphoreType.DMA((2,)),
        ]
    )

    def right_map(t):
        t = lax.rem(t, steps)
        return (lax.div(t, parts), 0, first + lax.rem(t, parts))

    result = pl.pallas_call(
        kernel,
        grid=(2 * steps,),
        in_specs=[pl.BlockSpec((rows, size), lambda t: (0, 1 - lax.div(t, steps)))] * pairs
        + [pl.BlockSpec((None, rows, tw), right_map)] * pairs
        + [pl.BlockSpec(memory_space=pl.ANY)] * len(rides),
        out_specs=[pl.BlockSpec((h, tw), late) for h in heights]
        + [pl.BlockSpec(memory_space=pl.ANY)] * len(rides),
        out_shape=out_shape + [struct(*r.shape) for r in rides],
        scratch_shapes=[
            pltpu.VMEM((pairs * rows, size), bf16),
            pltpu.VMEM((pairs * rows, tw), bf16),
            pltpu.VMEM((steps, size, tw), bf16),
            pltpu.VMEM((steps, size, tw), bf16),
            pltpu.SemaphoreType.DMA((steps,)),
            pltpu.SemaphoreType.DMA((steps,)),
        ]
        + ride_scratch,
        compiler_params=pltpu.CompilerParams(
            collective_id=number, has_side_effects=True, vmem_limit_bytes=VMEM
        ),
        cost_estimate=cost(
            4 * pairs * rows * size * columns, nbytes(arrays) + nbytes(out_shape)
        ),
    )(*arrays, *rides)
    return (result[:5], result[5]) if rides else (result, None)


def struct(*shape):
    return jax.ShapeDtypeStruct(shape, bf16)


class Spread:
    def __init__(self, mover, m, source, target, block):
        self.mover, self.m, self.source, self.block = mover, m, source, block
        self.at = lambda start, size: target(pl.ds(start, size))

    def first(self):
        go, block, source = self.mover.start, self.block, self.source
        if self.m != 8:
            self.all = [
                go(source, self.at(k * block, block), "wide", k) for k in range(1, self.m)
            ]
            return
        self.x = go(source, self.at(block, block), "wide", 2)
        self.y = go(source, self.at(2 * block, block), "wide", 4)
        self.cores = [go(source, self.at(4 * block, block), "wide", 1)]

    def second(self):
        if self.m != 8:
            return
        go, block = self.mover.start, self.block
        half = block // 2
        self.x.wait_recv()
        low = self.at(block + half, half)
        self.low = go(low, self.at(3 * block + half, half), "wide", 4)
        self.cores.append(go(self.at(block, block), self.at(5 * block, block), "wide", 1))
        self.y.wait_recv()
        top = self.at(2 * block, half)
        self.top = go(top, self.at(3 * block, half), "wide", 2)
        self.cores.append(go(self.at(2 * block, block), self.at(6 * block, block), "wide", 1))

    def third(self):
        if self.m != 8:
            return
        go, block = self.mover.start, self.block
        self.low.wait_recv()
        self.top.wait_recv()
        self.cores.append(go(self.at(3 * block, block), self.at(7 * block, block), "wide", 1))

    def last(self):
        for copy in self.all if self.m != 8 else self.cores:
            copy.wait_recv()


def gather_front(m, n, qkv_block, in_block, down_block, gain_block):
    block, qw = qkv_block.shape
    fw, dw = in_block.shape[1], down_block.shape[1]
    depth = block * m
    pairs = n // 2

    def program(mover, ins, outs, _):
        qkv, inner, down, gain = ins
        weights, in_own, in_rest, down_rest, gains = outs
        rows = pl.ds(0, block)
        waves = [mover.start(qkv, weights.at[e, rows], "tp", e) for e in range(1, n)]
        kept = [
            mover.keep(qkv, weights.at[0, rows]),
            mover.keep(inner, in_own.at[0, rows]),
            mover.keep(gain, gains.at[pl.ds(0, GAIN_ROWS)]),
        ]
        spread_gains = Spread(mover, m, gain, lambda r: gains.at[r], GAIN_ROWS)
        spread_gains.first()
        spreads = [
            Spread(
                mover,
                m,
                qkv if q == 0 else weights.at[q, rows],
                lambda r, q=q: weights.at[q, r],
                block,
            )
            for q in range(n)
        ]
        spreads[0].first()
        spread_gains.second()
        spreads[0].second()
        spread_gains.third()
        spreads[0].third()
        for q in range(1, n):
            waves[q - 1].wait_recv()
            spreads[q].first()
        late = []
        for e in range(1, pairs):
            late.append(mover.start(inner, in_rest.at[e - 1, rows], "tp", 2 * e))
            late.append(mover.start(down, down_rest.at[e - 1, rows], "tp", 2 * e))
        for q in range(1, n):
            spreads[q].second()
        own = Spread(mover, m, inner, lambda r: in_own.at[0, r], block)
        own.first()
        for q in range(1, n):
            spreads[q].third()
        own.second()
        own.third()
        for spread in spreads:
            spread.last()
        own.last()
        spread_gains.last()
        for copy in late:
            copy.wait_recv()
        for copy in kept:
            copy.wait()

    per = 8 if m == 8 else m - 1
    return transfer_call(
        program,
        m,
        n,
        [qkv_block, in_block, down_block, gain_block],
        [
            struct(n, depth, qw),
            struct(1, depth, fw),
            struct(pairs - 1, depth, fw),
            struct(pairs - 1, depth, dw),
            jax.ShapeDtypeStruct((m * GAIN_ROWS, gain_block.shape[1]), f32),
        ],
        [],
        (n - 1) + per * (n + 2) + 2 * (pairs - 1),
        3,
        1,
        vmem_ins=(0, 1, 2, 3),
    )


def swap_heads(mover, n, mine, source, target):
    seat = lax.axis_index("tp")
    load = mover.keep(source.at[seat], mine)
    sends = [
        mover.start(source.at[flipped(seat, e)], target.at[seat], "tp", e) for e in range(1, n)
    ]
    load.wait()
    return sends, mover.keep(mine, target.at[seat])


def gather_middle(m, n, hats, in_rest, out_block, down_block):
    quarters, rows, width = hats.shape
    pairs, depth, fw = in_rest.shape
    block, ow = out_block.shape
    dw = down_block.shape[1]

    def program(mover, ins, outs, scratch):
        hat, _, out, down = ins
        heads, rest, weights, down_own = outs
        first = pl.ds(0, block)
        kept = [mover.keep(out, weights.at[0, first]), mover.keep(down, down_own.at[0, first])]
        waves = [mover.start(out, weights.at[e, first], "tp", e) for e in range(1, n)]
        spreads = [
            Spread(mover, m, rest.at[p, first], lambda r, p=p: rest.at[p, r], block)
            for p in range(pairs)
        ]
        for spread in spreads:
            spread.first()
        for copy in waves:
            copy.wait_recv()
        sends, own_row = swap_heads(mover, n, scratch[0], hat, heads)
        kept[0].wait()
        for spread in spreads:
            spread.second()
        quarter = Spread(mover, m, weights.at[:, first], lambda r: weights.at[:, r], block)
        quarter.first()
        for spread in spreads:
            spread.third()
        quarter.second()
        own = Spread(mover, m, down, lambda r: down_own.at[0, r], block)
        own.first()
        quarter.third()
        own.second()
        own.third()
        for spread in spreads + [own, quarter]:
            spread.last()
        for copy in sends:
            copy.wait_recv()
        kept[1].wait()
        own_row.wait()

    per = 8 if m == 8 else m - 1
    return transfer_call(
        program,
        m,
        n,
        [hats, in_rest, out_block, down_block],
        [
            struct(n, rows, width),
            struct(pairs, depth, fw),
            struct(n, depth, ow),
            struct(1, depth, dw),
        ],
        [pltpu.VMEM((rows, width), bf16)],
        2 * (n - 1) + per * (pairs + 2),
        4,
        2,
        vmem_ins=(2, 3),
        aliases={1: 1},
    )


def gather_late(m, n, heads, down_rest):
    quarters, rows, width = heads.shape
    pairs, depth, dw = down_rest.shape
    block = depth // m

    def program(mover, ins, outs, scratch):
        source, _ = ins
        target, rest = outs
        first = pl.ds(0, block)
        sends, own_row = swap_heads(mover, n, scratch[0], source, target)
        spreads = [
            Spread(mover, m, rest.at[p, first], lambda r, p=p: rest.at[p, r], block)
            for p in range(pairs)
        ]
        for stage in ("first", "second", "third", "last"):
            for spread in spreads:
                getattr(spread, stage)()
        for copy in sends:
            copy.wait_recv()
        own_row.wait()

    per = 8 if m == 8 else m - 1
    return transfer_call(
        program,
        m,
        n,
        [heads, down_rest],
        [struct(n, rows, width), struct(pairs, depth, dw)],
        [pltpu.VMEM((rows, width), bf16)],
        (n - 1) + per * pairs,
        2,
        3,
        aliases={1: 1},
    )


def shuffle_columns(a, order):
    rows, count = a.shape[0], order.shape[0]
    width = a.shape[1] // count

    def kernel(order_ref, in_ref, out_ref):
        out_ref[...] = in_ref[...]

    return pl.pallas_call(
        kernel,
        grid_spec=pltpu.PrefetchScalarGridSpec(
            num_scalar_prefetch=1,
            grid=(count,),
            in_specs=[pl.BlockSpec((rows, width), lambda k, s: (0, s[k]))],
            out_specs=pl.BlockSpec((rows, width), lambda k, s: (0, k)),
        ),
        out_shape=jax.ShapeDtypeStruct(a.shape, a.dtype),
        cost_estimate=cost(0, 2 * nbytes([a])),
    )(order, a)


def inverse_rms(values):
    return lax.rsqrt(jnp.mean(values * values, axis=-1, keepdims=True) + norm_eps)


def norm_back(grads, unit_values, inverse, gain):
    scaled = grads * gain
    return inverse * (scaled - unit_values * jnp.mean(scaled * unit_values, axis=-1, keepdims=True))


def after(values, *conditions):
    return lax.optimization_barrier((values, conditions))[0]


class Job:
    def __init__(self, stages):
        self.stages = stages
        self.result = None
        self.started, self.pending = next(stages)

    def advance(self, came):
        try:
            self.started, self.pending = self.stages.send(came)
        except StopIteration as stop:
            self.result = stop.value
            self.pending = None

    def finish(self):
        while self.result is None:
            self.advance(self.pending)
        return self.result


def tick(values, *jobs):
    jobs = [j for j in jobs if j.result is None]
    values, came = lax.optimization_barrier((values, [j.pending for j in jobs]))
    for j, c in zip(jobs, came):
        j.advance(c)
    return values


def local(
    m,
    n,
    tokens,
    out_grad,
    seg_ids,
    parent_table,
    path_pos,
    attn_gain,
    w_query,
    w_key,
    w_value,
    w_out,
    q_gain,
    k_gain,
    ffn_gain,
    w_gate,
    w_up,
    w_down,
):
    rows, depth = tokens.shape
    block = depth // m
    order = [0, 2, 4, 6, 1, 3, 5, 7] if m == 8 else list(range(m))
    where = lax.axis_index("wide").astype(jnp.int32)
    seat = lax.axis_index("tp").astype(jnp.int32)
    relative = jnp.asarray(order, jnp.int32) ^ where
    inverse_order = [order.index(k) for k in range(m)]
    absolute = jnp.take(jnp.asarray(inverse_order, jnp.int32), jnp.arange(m, dtype=jnp.int32) ^ where)
    seats = jnp.arange(n, dtype=jnp.int32) ^ seat
    plain = jnp.arange(n, dtype=jnp.int32)

    def over(axis, a, mask):
        size = m if axis == "wide" else n
        return lax.ppermute(a, axis, [(i, i ^ mask) for i in range(size)])

    def scatter(lefts, rights, cut, number, ride=None, rode=None):
        if m != 8:
            if ride is not None:
                rode.append(swap(ride))
            other = weight_gradient(lefts, rights, 1, cut)
            mine = weight_gradient(lefts, rights, 0, cut)
            both = jnp.concatenate([mine, other])
            got = yield both, [over("wide", both[k * block : (k + 1) * block], k) for k in range(1, m)]
            return sum((g.astype(f32) for g in got), both[:block].astype(f32))
        (own, x, y, top_sent, low_sent), came = gradient_pair(lefts, rights, cut, number, ride)
        if ride is not None:
            rode.append(came)
        half = block // 2
        top, low = yield (top_sent, low_sent), [over("wide", top_sent, 2), over("wide", low_sent, 4)]
        for_x = jnp.concatenate([x[:half], (x[half:].astype(f32) + low.astype(f32)).astype(bf16)])
        for_y = jnp.concatenate([(y[:half].astype(f32) + top.astype(f32)).astype(bf16), y[half:]])
        from_x, from_y = yield [for_x, for_y], [over("wide", for_x, 2), over("wide", for_y, 4)]
        return own.astype(f32) + from_x.astype(f32) + from_y.astype(f32)

    cotangent = shuffle_columns(out_grad, relative)

    def ffn_share(left, rights, number, ride=None, rode=None):
        total = yield from scatter(left, rights, None, number, ride, rode)
        parts = [total[:, e * fcols : (e + 1) * fcols].astype(bf16) for e in range(1, n // 2)]
        sent = yield parts, [over("tp", p, 2 * (e + 1)) for e, p in enumerate(parts)]
        return sum((x.astype(f32) for x in sent), total[:, :fcols])

    def swap(a):
        return lax.all_to_all(a, "tp", split_axis=0, concat_axis=0, tiled=True)

    def attn_share(left, right, cut, number):
        total = yield from scatter([left], [right], cut, number)
        parts = total.astype(bf16).reshape(block, n, -1).transpose(1, 0, 2)
        (came,) = yield parts, [swap(parts)]
        return jnp.sum(came.astype(f32), axis=0)

    qkv_block = jnp.concatenate([w_query, w_key, w_value], axis=1)
    out_block = w_out.T
    in_block = jnp.concatenate([w_gate, w_up], axis=1)
    down_block = w_down.T
    aw = w_query.shape[1]
    kv = w_key.shape[1] // HEAD_DIM
    fcols = w_gate.shape[1]
    fw = fcols // 3

    gain_row = jnp.concatenate([attn_gain, ffn_gain, q_gain, k_gain]).astype(f32)[None]
    gain_width = -(-gain_row.shape[1] // 128) * 128
    gain_block = jnp.pad(gain_row, ((0, GAIN_ROWS - 1), (0, gain_width - gain_row.shape[1])))
    qkv_all, in_own, in_rest, down_rest, gains = gather_front(
        m, n, qkv_block, in_block, down_block, gain_block
    )
    gains = gains[::GAIN_ROWS]
    small = q_gain.shape[0]
    gain_one = gains[:, :block].reshape(1, depth)
    gain_two = gains[:, block : 2 * block].reshape(1, depth)
    head_gains = jnp.take(gains[:, 2 * block :], absolute, axis=0)
    gain_q = head_gains[:, :small].reshape(1, HEAD_DIM)
    gain_k = head_gains[:, small : 2 * small].reshape(1, HEAD_DIM)

    base = where * parent_table.shape[0]
    block_segs = seg_ids[TRUNK::BRANCH] - base
    hit = block_segs[:, None] == jnp.arange(parent_table.shape[0], dtype=jnp.int32)[None, :]
    block_parents = jnp.sum(jnp.where(hit, parent_table[None, :] - base, 0), axis=1)
    match = block_parents[:, None] == block_segs[None, :]
    number = TRUNK_BLOCKS + jnp.arange(FORKS2, dtype=jnp.int32)
    parents = jnp.where(
        jnp.any(match, axis=1), jnp.sum(jnp.where(match, number[None, :], 0), axis=1), number
    ).astype(jnp.int32)

    own_pos = lax.dynamic_slice_in_dim(path_pos, seat * rows, rows, 0).astype(f32)
    frequency = rope_base ** (-(jnp.arange(HEAD_DIM // 2, dtype=f32) * 2.0) / HEAD_DIM)
    angles = own_pos[:, None] * frequency[None, :]
    cosine, sine = jnp.cos(angles), jnp.sin(angles)
    cosine = jnp.concatenate([cosine, cosine], axis=-1)
    sine = jnp.concatenate([-sine, sine], axis=-1)

    stream = shuffle_columns(tokens, relative).astype(f32)
    inverse_one = inverse_rms(stream)
    unit_one = stream * inverse_one
    normed_one = (unit_one * gain_one).astype(bf16)

    qkv_tiles = Tiles([qkv_all], 2, 0, aw)
    hats, raws = project_qkv(normed_one, qkv_tiles, seats, cosine, sine, gain_q, gain_k)
    qkv, in_rest, out_all, down_own = gather_middle(m, n, hats, in_rest, out_block, down_block)
    qkv = qkv.reshape(n * rows, -1)
    attended_heads, logs = attention_forward(qkv, parents, kv)
    attended, down_rest = gather_late(m, n, attended_heads.reshape(n, rows, -1), down_rest)
    out_tiles = Tiles([out_all], 1, 0, aw)
    after_attn = stream + project_columns([attended], [out_tiles], seats, depth, f32)

    inverse_two = inverse_rms(after_attn)
    unit_two = after_attn * inverse_two
    normed_two = (unit_two * gain_two).astype(bf16)
    normed_two_next = over("tp", normed_two, 1)

    gate_tiles = Tiles([in_own, in_rest], 3, 0, fw)
    up_tiles = Tiles([in_own, in_rest], 3, 3, fw)
    down_tiles = Tiles([down_own, down_rest], 3, 0, fw)

    hidden, gate, up = feed_forward(normed_two, gate_tiles, up_tiles, plain)
    down = project_columns([hidden], [down_tiles], plain, depth, f32)
    normed_two_next, cotangent_sent = after((normed_two_next, cotangent), (down, normed_two_next))
    cotangent_next = over("tp", cotangent_sent, 1)
    hidden_next, gate_next, up_next = feed_forward(normed_two_next, gate_tiles, up_tiles, plain)
    down_part = project_columns([hidden_next], [down_tiles], plain, depth, bf16)
    cotangent_next, hidden_late = after((cotangent_next, hidden), down_part)
    down_job = Job(ffn_share([cotangent, cotangent_next], [hidden_late, hidden_next], 4))
    cotangent_next = after(cotangent_next, down_job.started)
    gate_grad_next, up_grad_next = feed_back(
        cotangent_next, gate_next, up_next, down_tiles, plain
    )
    gate_late, up_late = tick((gate_grad_next, up_grad_next), down_job)
    gate_late, up_late = after((gate_late, up_late), down_job.started)
    back_part = project_columns([gate_late, up_late], [gate_tiles, up_tiles], plain, depth, bf16)
    back_next = over("tp", back_part, 1)
    own_grad = after(cotangent, back_part)
    gate_grad, up_grad = feed_back(own_grad, gate, up, down_tiles, plain)
    gate_job = Job(ffn_share([normed_two, normed_two_next], [gate_grad, gate_grad_next], 5))
    gate_late, up_late = after((gate_grad, up_grad), gate_job.started)
    gate_late, up_late = tick((gate_late, up_late), down_job)
    gate_late, up_late = after((gate_late, up_late), down_job.started)
    back = project_columns([gate_late, up_late], [gate_tiles, up_tiles], plain, depth, f32)
    back, back_next = after((back, back_next), back)
    back = tick(back, gate_job)
    back = after(back, gate_job.started)
    normed_two_grad = back + back_next.astype(f32)

    ffn_gain_part = jnp.sum(normed_two_grad * unit_two, axis=0)
    stream_grad = cotangent.astype(f32) + norm_back(
        normed_two_grad, unit_two, inverse_two, gain_two
    )
    grad_low = stream_grad.astype(bf16)
    attended_grad = tick(project_rows(grad_low, out_tiles, seats), down_job)
    lefts, up_grads = after(
        ([normed_two, normed_two_next], [up_grad, up_grad_next]), attended_grad
    )
    rode = []
    up_job = Job(ffn_share(lefts, up_grads, 6, attended_grad, rode))
    grad_heads = after(rode[0].reshape(n * rows, -1), up_job.started)
    grad_heads = tick(grad_heads, gate_job)
    grad_heads = after(grad_heads, gate_job.started)
    back_hats = attention_backward(qkv, attended_heads, grad_heads, logs, parents, kv)
    back_hats = tick(back_hats, gate_job, up_job)
    back_hats = after(back_hats, up_job.started)
    back_hats_own = swap(back_hats.reshape(n, rows, -1))
    grad_low, down_sent, after_attn = after((grad_low, down_part, after_attn), back_hats)
    out_job = Job(attn_share(grad_low, attended, None, 7))
    fence = tick(after(grad_low, out_job.started), up_job)
    back_hats_own = after(back_hats_own, fence, out_job.started)
    raw_grads, q_sum, k_sum = qkv_back(back_hats_own, raws, cosine, sine, gain_q, gain_k)
    raw_grads = tick(raw_grads, out_job)
    down_next = over("tp", after(down_sent, raw_grads), 1)
    q_job = Job(attn_share(normed_one, after(raw_grads, out_job.started), 0, 8))
    raw_late = after(raw_grads, q_job.started)
    k_job = Job(attn_share(normed_one, raw_late, 1, 9))
    raw_late = tick(after(raw_late, k_job.started), q_job, out_job, up_job)
    raw_late = after(raw_late, q_job.started, out_job.started, up_job.started)
    normed_one_grad = project_columns([raw_late], [qkv_tiles], seats, depth, f32)
    normed_one_grad, down_next = after((normed_one_grad, down_next), normed_one_grad)
    normed_one_grad = tick(normed_one_grad, q_job, k_job, up_job, out_job)
    normed_one_grad = after(normed_one_grad, q_job.started, k_job.started)
    mixed = (after_attn + down + down_next.astype(f32)).astype(bf16)
    mixed = shuffle_columns(mixed, absolute)
    attn_gain_part = jnp.sum(normed_one_grad * unit_one, axis=0)
    tokens_grad = (
        stream_grad + norm_back(normed_one_grad, unit_one, inverse_one, gain_one)
    ).astype(bf16)
    tokens_grad = shuffle_columns(tokens_grad, absolute)

    parts = jnp.concatenate(
        [
            attn_gain_part.reshape(m, block),
            ffn_gain_part.reshape(m, block),
            jnp.take(q_sum.reshape(m, small), relative, axis=0),
            jnp.take(k_sum.reshape(m, small), relative, axis=0),
        ],
        axis=1,
    )
    size = m
    while size > 1:
        size //= 2
        parts = parts[:size] + over("wide", parts[size:], order[size])
    step = 1
    while step < n:
        parts = parts + over("tp", parts, step)
        step *= 2
    sums = parts[0]
    gate_share, up_share = gate_job.finish(), up_job.finish()
    down_share, out_share = down_job.finish().T, out_job.finish().T
    q_share, k_share = q_job.finish(), k_job.finish()
    return (
        mixed,
        tokens_grad,
        sums[:block],
        q_share,
        k_share[:, : aw // 2],
        k_share[:, aw // 2 :],
        out_share,
        sums[2 * block : 2 * block + small],
        sums[2 * block + small :],
        sums[block : 2 * block],
        gate_share,
        up_share,
        down_share,
    )


def solution(mesh):
    both = P(("wide", "tp"), None)
    w, wt, tw = P("wide"), P("wide", "tp"), P("tp", "wide")
    return jax.shard_map(
        functools.partial(local, mesh.shape["wide"], mesh.shape["tp"]),
        mesh=mesh,
        in_specs=(both, both, w, w, w, w, wt, wt, wt, tw, w, w, w, wt, wt, tw),
        out_specs=(both, both, w, wt, wt, wt, tw, w, w, w, wt, wt, tw),
        check_vma=False,
    )
```

```python
import functools
import math

import jax
import jax.numpy as jnp
from jax import lax
from jax.experimental import pallas as pl
from jax.experimental.pallas import tpu as pltpu
from jax.sharding import PartitionSpec as P

HEAD_DIM = 128
TRUNK = 1152
BRANCH = 128
FORKS2 = 8
TREE_TOK = 2176
GROUP = 2

norm_eps = 1e-06
rope_base = 1000000.0
score_scale = HEAD_DIM ** (-0.5)
key_scale = score_scale * math.log2(math.e)
LN2 = math.log(2.0)
VMEM = 52 * 1024 * 1024
COST = 0.01
GAIN_ROWS = 16

f32 = jnp.float32
bf16 = jnp.bfloat16


def dot_nn(a, b):
    return lax.dot_general(a, b, (((1,), (0,)), ((), ())), preferred_element_type=f32)


def dot_nt(a, b):
    return lax.dot_general(a, b, (((1,), (1,)), ((), ())), preferred_element_type=f32)


def contract_rows(a, b):
    return lax.dot_general(a, b, (((0,), (0,)), ((), ())), preferred_element_type=f32)


def params():
    return pltpu.CompilerParams(vmem_limit_bytes=VMEM)


def cost(flops, nbytes):
    return pl.CostEstimate(flops=int(flops * COST), bytes_accessed=int(nbytes * COST), transcendentals=0)


def nbytes(arrays):
    return sum(a.size * a.dtype.itemsize for a in arrays)


class Tiles:
    def __init__(self, arrays, parts, base, width):
        self.list = list(arrays)
        self.quarters = sum(a.shape[0] for a in self.list)
        self.depth = self.list[0].shape[1]
        self.parts, self.base, self.width = parts, base, width
        self.steps = self.quarters * parts

    def arrays(self):
        return self.list

    def scratch(self):
        return [pltpu.VMEM((2, self.depth, self.width), bf16), pltpu.SemaphoreType.DMA((2,))]

    def fetch(self, refs, buf, sems, step):
        slot = lax.rem(step, 2)
        quarter = lax.div(step, self.parts)
        part = step - quarter * self.parts
        col = pl.multiple_of((self.base + part) * self.width, 128)

        def begin(ref, at):
            pltpu.make_async_copy(
                ref.at[at, :, pl.ds(col, self.width)], buf.at[slot], sems.at[slot]
            ).start()

        split = self.list[0].shape[0]
        if len(refs) == 1:
            begin(refs[0], quarter)
        else:

            @pl.when(quarter < split)
            def _():
                begin(refs[0], quarter)

            @pl.when(quarter >= split)
            def _():
                begin(refs[1], quarter - split)

    def wait(self, refs, buf, sems, step):
        slot = lax.rem(step, 2)
        pltpu.make_async_copy(
            refs[0].at[0, :, pl.ds(0, self.width)], buf.at[slot], sems.at[slot]
        ).wait()
        return slot


def tiled_call(body, sets, seats, ins, in_specs, out_shape, out_specs, scratch, flops):
    steps = sets[0].steps
    counts = [len(s.arrays()) for s in sets]
    n_in, n_out = len(ins), len(out_shape)

    def kernel(seat_ref, *refs):
        at = 0
        piece_refs = []
        for c in counts:
            piece_refs.append(refs[at : at + c])
            at += c
        in_refs = refs[at : at + n_in]
        at += n_in
        out_refs = refs[at : at + n_out]
        at += n_out
        bufs = [(refs[at + 2 * i], refs[at + 2 * i + 1]) for i in range(len(sets))]
        own = refs[at + 2 * len(sets) :]
        step = pl.program_id(0)

        @pl.when(step == 0)
        def _():
            for s, p, (buf, sems) in zip(sets, piece_refs, bufs):
                s.fetch(p, buf, sems, step)

        @pl.when(step + 1 < steps)
        def _():
            for s, p, (buf, sems) in zip(sets, piece_refs, bufs):
                s.fetch(p, buf, sems, step + 1)

        tiles = []
        for s, p, (buf, sems) in zip(sets, piece_refs, bufs):
            slot = s.wait(p, buf, sems, step)
            tiles.append(buf.at[slot])
        body(step, tiles, in_refs, out_refs, own)

    weights = [a for s in sets for a in s.arrays()]
    return pl.pallas_call(
        kernel,
        grid_spec=pltpu.PrefetchScalarGridSpec(
            num_scalar_prefetch=1,
            grid=(steps,),
            in_specs=[pl.BlockSpec(memory_space=pl.ANY)] * len(weights) + in_specs,
            out_specs=out_specs,
            scratch_shapes=[x for s in sets for x in s.scratch()] + scratch,
        ),
        out_shape=out_shape,
        compiler_params=params(),
        cost_estimate=cost(flops, nbytes(weights) + nbytes(ins) + nbytes(out_shape)),
    )(seats, *weights, *ins)


def whole(array):
    return pl.BlockSpec(array.shape, lambda t, s: (0,) * len(array.shape))


def seated(rows, width, parts):
    return pl.BlockSpec(
        (None, rows, width),
        lambda t, s: (s[lax.div(t, parts)], 0, lax.rem(t, parts)),
    )


def head_slices(width):
    return [slice(h * HEAD_DIM, (h + 1) * HEAD_DIM) for h in range(width // HEAD_DIM)]


def project_rows(a, tiles, seats):
    rows, tw = a.shape[0], tiles.width

    def body(step, weights, ins, outs, own):
        outs[0][...] = dot_nn(ins[0][...], weights[0][...]).astype(bf16)

    return tiled_call(
        body,
        [tiles],
        seats,
        [a],
        [whole(a)],
        [jax.ShapeDtypeStruct((tiles.quarters, rows, tiles.parts * tw), bf16)],
        [seated(rows, tw, tiles.parts)],
        [],
        2 * rows * a.shape[1] * tw * tiles.steps,
    )[0]


def project_columns(lefts, sets, seats, depth, out_dtype):
    rows, tw, steps = lefts[0].shape[1], sets[0].width, sets[0].steps

    def body(step, weights, ins, outs, own):
        acc = own[0]
        total = dot_nt(ins[0][...], weights[0][...])
        for left, weight in zip(ins[1:], weights[1:]):
            total = total + dot_nt(left[...], weight[...])

        @pl.when(step == 0)
        def _():
            acc[...] = total

        @pl.when(step > 0)
        def _():
            acc[...] += total

        @pl.when(step == steps - 1)
        def _():
            outs[0][...] = acc[...].astype(out_dtype)

    return tiled_call(
        body,
        sets,
        seats,
        list(lefts),
        [seated(rows, tw, s.parts) for s in sets],
        [jax.ShapeDtypeStruct((rows, depth), out_dtype)],
        [pl.BlockSpec((rows, depth), lambda t, s: (0, 0))],
        [pltpu.VMEM((rows, depth), f32)],
        2 * rows * depth * tw * steps * len(sets),
    )[0]


def feed_forward(normed, gate_tiles, up_tiles, seats):
    rows, tw = normed.shape[0], gate_tiles.width

    def body(step, weights, ins, outs, own):
        a = ins[0][...]
        gate = dot_nn(a, weights[0][...])
        up = dot_nn(a, weights[1][...])
        outs[0][...] = (gate * jax.nn.sigmoid(gate) * up).astype(bf16)
        outs[1][...] = gate.astype(bf16)
        outs[2][...] = up.astype(bf16)

    shape = jax.ShapeDtypeStruct((gate_tiles.quarters, rows, gate_tiles.parts * tw), bf16)
    return tiled_call(
        body,
        [gate_tiles, up_tiles],
        seats,
        [normed],
        [whole(normed)],
        [shape] * 3,
        [seated(rows, tw, gate_tiles.parts)] * 3,
        [],
        4 * rows * normed.shape[1] * tw * gate_tiles.steps,
    )


def feed_back(cotangent, gate, up, down_tiles, seats):
    rows, tw = cotangent.shape[0], down_tiles.width

    def body(step, weights, ins, outs, own):
        grad = dot_nn(ins[0][...], weights[0][...])
        g = ins[1][...].astype(f32)
        u = ins[2][...].astype(f32)
        s = jax.nn.sigmoid(g)
        outs[0][...] = (grad * u * s * (1.0 + g * (1.0 - s))).astype(bf16)
        outs[1][...] = (grad * (g * s)).astype(bf16)

    shape = jax.ShapeDtypeStruct(gate.shape, bf16)
    tile = seated(rows, tw, down_tiles.parts)
    return tiled_call(
        body,
        [down_tiles],
        seats,
        [cotangent, gate, up],
        [whole(cotangent), tile, tile],
        [shape] * 2,
        [tile] * 2,
        [],
        2 * rows * cotangent.shape[1] * tw * down_tiles.steps,
    )


def qkv_back(grad_hat, raw, cosine, sine, q_gain, k_gain):
    quarters, rows, width = grad_hat.shape
    tw = width // 2

    def kernel(g_ref, r_ref, cos_ref, sin_ref, qg, kg, out, qsum, ksum):
        @pl.when(pl.program_id(0) == 0)
        def _():
            qsum[...] = jnp.zeros_like(qsum)
            ksum[...] = jnp.zeros_like(ksum)

        def back(cut, gain, total):
            w = g_ref[:, cut].astype(f32)
            w = w * cos_ref[...] + pltpu.roll(w * sin_ref[...], HEAD_DIM // 2, 1)
            x = r_ref[:, cut].astype(f32)
            inverse = lax.rsqrt(jnp.mean(x * x, axis=-1, keepdims=True) + norm_eps)
            u = x * inverse
            wu = w * u
            scaled = w * gain
            out[:, cut] = (
                inverse * (scaled - u * jnp.mean(wu * gain, axis=-1, keepdims=True))
            ).astype(bf16)
            return total + jnp.sum(wu, axis=0, keepdims=True)

        total = jnp.zeros((1, HEAD_DIM), f32)
        cuts = head_slices(width)
        n_query, n_key = tw // HEAD_DIM, tw // HEAD_DIM // 2
        for cut in cuts[:n_query]:
            total = back(cut, qg[...], total)
        qsum[...] += total
        total = jnp.zeros((1, HEAD_DIM), f32)
        for cut in cuts[n_query : n_query + n_key]:
            total = back(cut, kg[...], total)
        ksum[...] += total
        out[:, tw + tw // 2 :] = g_ref[:, tw + tw // 2 :]

    ins = [grad_hat, raw, cosine, sine, q_gain, k_gain]
    gain_shape = jax.ShapeDtypeStruct((1, HEAD_DIM), f32)
    out_shape = [jax.ShapeDtypeStruct(grad_hat.shape, bf16), gain_shape, gain_shape]
    tile = pl.BlockSpec((None, rows, width), lambda e: (e, 0, 0))
    fixed = lambda x: pl.BlockSpec(x.shape, lambda e: (0, 0))
    return pl.pallas_call(
        kernel,
        grid=(quarters,),
        in_specs=[tile, tile] + [fixed(x) for x in ins[2:]],
        out_specs=[tile, fixed(gain_shape), fixed(gain_shape)],
        out_shape=out_shape,
        compiler_params=params(),
        cost_estimate=cost(40 * quarters * rows * width, nbytes(ins) + nbytes(out_shape)),
    )(*ins)


def attention_specs(kv):
    q = pl.BlockSpec((TREE_TOK, GROUP * HEAD_DIM), lambda n, s: (0, n))
    k = pl.BlockSpec((TREE_TOK, HEAD_DIM), lambda n, s: (0, GROUP * kv + n))
    v = pl.BlockSpec((TREE_TOK, HEAD_DIM), lambda n, s: (0, (GROUP + 1) * kv + n))
    return q, k, v


def stacked(ref, start):
    rows = pl.ds(start, BRANCH)
    return jnp.concatenate(
        [ref[rows, h * HEAD_DIM : (h + 1) * HEAD_DIM] for h in range(GROUP)], axis=0
    )


def causal():
    key = lax.broadcasted_iota(jnp.int32, (BRANCH, GROUP * BRANCH), 0)
    query = lax.rem(lax.broadcasted_iota(jnp.int32, (BRANCH, GROUP * BRANCH), 1), BRANCH)
    return key <= query


TRUNK_BLOCKS = TRUNK // BRANCH
BLOCKS = TREE_TOK // BRANCH


def attention_forward(qkv, parents, kv):
    def kernel(parent_ref, q_ref, k_ref, v_ref, out_ref, log_ref, vt):
        vt[...] = v_ref[...].T
        mask = causal()

        def part(q, start, size, rule):
            score = dot_nt(k_ref[pl.ds(start, size), :], q)
            weight = jnp.exp2(score)
            if rule is not None:
                weight = rule(weight)
            out = dot_nn(vt[:, pl.ds(start, size)], weight.astype(bf16))
            return out, jnp.sum(weight, axis=0, keepdims=True)

        def finish(block, start, pieces):
            out = sum(p[0] for p in pieces)
            total = sum(p[1] for p in pieces)
            out = (out / total).T.astype(bf16)
            for h in range(GROUP):
                out_ref[pl.ds(start, BRANCH), h * HEAD_DIM : (h + 1) * HEAD_DIM] = out[
                    h * BRANCH : (h + 1) * BRANCH
                ]
            log_ref[0, pl.ds(block, 1), :] = jnp.log2(total)

        diagonal = lambda w: jnp.where(mask, w, 0.0)
        for block in range(TRUNK_BLOCKS):
            q = stacked(q_ref, block * BRANCH)
            pieces = [part(q, block * BRANCH, BRANCH, diagonal)]
            if block > 0:
                pieces.append(part(q, 0, block * BRANCH, None))
            finish(block, block * BRANCH, pieces)

        def branch(i, carry):
            block = TRUNK_BLOCKS + i
            start = pl.multiple_of(block * BRANCH, BRANCH)
            q = stacked(q_ref, start)
            parent = parent_ref[i]
            has = (parent != block).astype(f32)
            pieces = [
                part(q, start, BRANCH, diagonal),
                part(q, pl.multiple_of(parent * BRANCH, BRANCH), BRANCH, lambda w: w * has),
                part(q, 0, TRUNK, None),
            ]
            finish(block, start, pieces)
            return carry

        lax.fori_loop(0, FORKS2, branch, 0)

    q, k, v = attention_specs(kv)
    out_shape = [
        jax.ShapeDtypeStruct((TREE_TOK, GROUP * kv * HEAD_DIM), bf16),
        jax.ShapeDtypeStruct((kv, BLOCKS, GROUP * BRANCH), f32),
    ]
    return pl.pallas_call(
        kernel,
        grid_spec=pltpu.PrefetchScalarGridSpec(
            num_scalar_prefetch=1,
            grid=(kv,),
            in_specs=[q, k, v],
            out_specs=[
                q,
                pl.BlockSpec((1, BLOCKS, GROUP * BRANCH), lambda n, s: (n, 0, 0)),
            ],
            scratch_shapes=[pltpu.VMEM((HEAD_DIM, TREE_TOK), bf16)],
        ),
        out_shape=out_shape,
        compiler_params=params(),
        cost_estimate=cost(kv * 2.2e6 * 2 * GROUP * 256 * 2, nbytes([qkv]) + nbytes(out_shape)),
    )(parents, qkv, qkv, qkv)


def attention_backward(qkv, attended, grads, logs, parents, kv):
    width = qkv.shape[1]

    def kernel(
        parent_ref, q_ref, k_ref, v_ref, o_ref, do_ref, log_ref, out_ref, kt, dk, dv, dq_ref
    ):
        kt[...] = k_ref[...].T
        dk[...] = jnp.zeros_like(dk)
        dv[...] = jnp.zeros_like(dv)
        mask = causal()

        def part(q, do, log, delta, start, size, rule):
            rows = pl.ds(start, size)
            prob = jnp.exp2(dot_nt(k_ref[rows, :], q) - log)
            if rule is not None:
                prob = rule(prob)
            grad = dot_nt(v_ref[rows, :], do)
            score_grad = (prob * (grad - delta)).astype(bf16)
            dk[rows, :] += dot_nn(score_grad, q)
            dv[rows, :] += dot_nn(prob.astype(bf16), do)
            return dot_nn(kt[:, rows], score_grad)

        def one(block, start, ranges):
            q = stacked(q_ref, start)
            do = stacked(do_ref, start)
            o = stacked(o_ref, start)
            delta = jnp.sum((do.astype(f32) * o.astype(f32)).T, axis=0, keepdims=True)
            log = log_ref[0, pl.ds(block, 1), :]
            total = sum(part(q, do, log, delta, *r) for r in ranges)
            out = (total * LN2).T.astype(bf16)
            for h in range(GROUP):
                dq_ref[pl.ds(start, BRANCH), h * HEAD_DIM : (h + 1) * HEAD_DIM] = out[
                    h * BRANCH : (h + 1) * BRANCH
                ]

        diagonal = lambda p: jnp.where(mask, p, 0.0)
        for block in range(TRUNK_BLOCKS):
            ranges = [(block * BRANCH, BRANCH, diagonal)]
            if block > 0:
                ranges.append((0, block * BRANCH, None))
            one(block, block * BRANCH, ranges)

        def branch(i, carry):
            block = TRUNK_BLOCKS + i
            start = pl.multiple_of(block * BRANCH, BRANCH)
            parent = parent_ref[i]
            has = (parent != block).astype(f32)
            one(
                block,
                start,
                [
                    (start, BRANCH, diagonal),
                    (pl.multiple_of(parent * BRANCH, BRANCH), BRANCH, lambda p: p * has),
                    (0, TRUNK, None),
                ],
            )
            return carry

        lax.fori_loop(0, FORKS2, branch, 0)
        for head in range(kv):

            @pl.when(pl.program_id(0) == head)
            def _(head=head):
                wide = GROUP * HEAD_DIM
                out_ref[:, head * wide : (head + 1) * wide] = dq_ref[...]
                at = kv * wide + head * HEAD_DIM
                out_ref[:, at : at + HEAD_DIM] = (dk[...] * score_scale).astype(bf16)
                at += kv * HEAD_DIM
                out_ref[:, at : at + HEAD_DIM] = dv[...].astype(bf16)

    q, k, v = attention_specs(kv)
    out_shape = jax.ShapeDtypeStruct((TREE_TOK, width), bf16)
    return pl.pallas_call(
        kernel,
        grid_spec=pltpu.PrefetchScalarGridSpec(
            num_scalar_prefetch=1,
            grid=(kv,),
            in_specs=[
                q,
                k,
                v,
                q,
                q,
                pl.BlockSpec((1, BLOCKS, GROUP * BRANCH), lambda n, s: (n, 0, 0)),
            ],
            out_specs=pl.BlockSpec((TREE_TOK, width), lambda n, s: (0, 0)),
            scratch_shapes=[
                pltpu.VMEM((HEAD_DIM, TREE_TOK), bf16),
                pltpu.VMEM((TREE_TOK, HEAD_DIM), f32),
                pltpu.VMEM((TREE_TOK, HEAD_DIM), f32),
                pltpu.VMEM((TREE_TOK, GROUP * HEAD_DIM), bf16),
            ],
        ),
        out_shape=out_shape,
        compiler_params=params(),
        cost_estimate=cost(
            kv * 2.2e6 * 2 * GROUP * 640 * 2, nbytes([qkv, attended, grads, qkv])
        ),
    )(parents, qkv, qkv, qkv, attended, grads, logs)


def weight_gradient(lefts, rights, half, cut=None):
    pairs = len(lefts)
    rows, depth = lefts[0].shape
    quarters, _, width = rights[0].shape
    size = depth // 2
    if cut is None:
        tw = width // 2 if width > 1024 else width
        parts, first = width // tw, 0
    else:
        width = tw = width // 2
        parts, first = 1, cut

    def kernel(*refs):
        left_refs, right_refs = refs[:pairs], refs[pairs : 2 * pairs]
        out_ref, left_s, right_s = refs[2 * pairs :]

        @pl.when(pl.program_id(0) == 0)
        def _():
            for i, ref in enumerate(left_refs):
                left_s[i * rows : (i + 1) * rows] = ref[...]

        for i, ref in enumerate(right_refs):
            right_s[i * rows : (i + 1) * rows] = ref[...]
        out_ref[...] = contract_rows(left_s[...], right_s[...]).astype(bf16)

    out_shape = jax.ShapeDtypeStruct((size, quarters * width), bf16)
    arrays = list(lefts) + list(rights)
    return pl.pallas_call(
        kernel,
        grid=(quarters * parts,),
        in_specs=[pl.BlockSpec((rows, size), lambda t: (0, half))] * pairs
        + [pl.BlockSpec((None, rows, tw), lambda t: (t // parts, 0, first + t % parts))] * pairs,
        out_specs=pl.BlockSpec((size, tw), lambda t: (0, t)),
        out_shape=out_shape,
        scratch_shapes=[
            pltpu.VMEM((pairs * rows, size), bf16),
            pltpu.VMEM((pairs * rows, tw), bf16),
        ],
        compiler_params=params(),
        cost_estimate=cost(
            2 * pairs * rows * size * quarters * width, nbytes(arrays) + nbytes([out_shape])
        ),
    )(*arrays)


def flipped(index, mask):
    bit = 1
    while bit <= mask:
        if mask & bit:
            index = index + bit * (1 - 2 * lax.rem(lax.div(index, bit), 2))
        bit *= 2
    return index


def transfer_call(
    program, m, n, ins, outs, scratch, count, locals_, number, vmem_ins=(), aliases=None
):
    n_in, n_out, n_scratch = len(ins), len(outs), len(scratch)

    class Mover:
        def __init__(self, send, recv, own):
            self.send, self.recv, self.own = send, recv, own
            self.made, self.local = [], []

        def start(self, source, target, axis, mask):
            k = len(self.made)
            place = flipped(lax.axis_index(axis), mask)
            copy = pltpu.make_async_remote_copy(
                src_ref=source,
                dst_ref=target,
                send_sem=self.send.at[k],
                recv_sem=self.recv.at[k],
                device_id={axis: place},
                device_id_type=pl.DeviceIdType.MESH,
            )
            copy.start()
            self.made.append(copy)
            return copy

        def keep(self, source, target):
            copy = pltpu.make_async_copy(source, target, self.own.at[len(self.local)])
            copy.start()
            self.local.append(copy)
            return copy

    def kernel(*refs):
        in_refs, out_refs = refs[:n_in], refs[n_in : n_in + n_out]
        rest = refs[n_in + n_out :]
        mover = Mover(*rest[n_scratch:])
        barrier = pltpu.get_barrier_semaphore()
        partners = [("wide", k) for k in range(1, m)] if m != 8 else [
            ("wide", k) for k in (1, 2, 4)
        ]
        partners += [("tp", e) for e in range(1, n)]
        for axis, mask in partners:
            pl.semaphore_signal(
                barrier,
                inc=1,
                device_id={axis: flipped(lax.axis_index(axis), mask)},
                device_id_type=pl.DeviceIdType.MESH,
            )
        pl.semaphore_wait(barrier, len(partners))
        program(mover, in_refs, out_refs, rest[:n_scratch])
        for copy in mover.made:
            copy.wait_send()

    return pl.pallas_call(
        kernel,
        in_specs=[
            pl.BlockSpec(memory_space=pltpu.VMEM if i in vmem_ins else pl.ANY) for i in range(n_in)
        ],
        out_specs=[pl.BlockSpec(memory_space=pl.ANY)] * n_out,
        out_shape=outs,
        scratch_shapes=list(scratch)
        + [
            pltpu.SemaphoreType.DMA((count,)),
            pltpu.SemaphoreType.DMA((count,)),
            pltpu.SemaphoreType.DMA((locals_,)),
        ],
        input_output_aliases=aliases or {},
        compiler_params=pltpu.CompilerParams(
            collective_id=number, has_side_effects=True, vmem_limit_bytes=VMEM
        ),
        cost_estimate=cost(0, 1e6),
    )(*ins)


def swap_own(source, target, mine, sems):
    seat = lax.axis_index("tp")
    return (
        pltpu.make_async_copy(source.at[seat], mine, sems.at[0]),
        pltpu.make_async_copy(mine, target.at[seat], sems.at[1]),
    )


def gradient_pair(lefts, rights, cut, number, ride=None):
    pairs = len(lefts)
    rows, depth = lefts[0].shape
    quarters, _, width = rights[0].shape
    size = depth // 2
    block = size // 4
    half = block // 2
    if cut is None:
        tw = width // 2 if width > 1024 else width
        parts, first = width // tw, 0
    else:
        width = tw = width // 2
        parts, first = 1, cut
    steps = quarters * parts
    n = ride.shape[0] if ride is not None else 1
    rides = [] if ride is None else [ride]

    def kernel(*refs):
        left_refs, right_refs = refs[:pairs], refs[pairs : 2 * pairs]
        at = 2 * pairs
        ride_in = refs[at : at + len(rides)]
        at += len(rides)
        own_ref, x_ref, y_ref, top_ref, low_ref = refs[at : at + 5]
        at += 5
        ride_out = refs[at : at + len(rides)]
        at += len(rides)
        left_s, right_s, sent, came, send_sems, recv_sems = refs[at : at + 6]
        extra = refs[at + 6 :]
        step = pl.program_id(0)
        other_core = {"wide": flipped(lax.axis_index("wide"), 1)}

        def copy(k):
            return pltpu.make_async_remote_copy(
                src_ref=sent.at[k],
                dst_ref=came.at[k],
                send_sem=send_sems.at[k],
                recv_sem=recv_sems.at[k],
                device_id=other_core,
                device_id_type=pl.DeviceIdType.MESH,
            )

        def ride_copies():
            mine, ride_send, ride_recv, own_sems = extra
            seat = lax.axis_index("tp")
            return [
                pltpu.make_async_remote_copy(
                    src_ref=ride_in[0].at[flipped(seat, e)],
                    dst_ref=ride_out[0].at[seat],
                    send_sem=ride_send.at[e - 1],
                    recv_sem=ride_recv.at[e - 1],
                    device_id={"tp": flipped(seat, e)},
                    device_id_type=pl.DeviceIdType.MESH,
                )
                for e in range(1, n)
            ], swap_own(ride_in[0], ride_out[0], mine, own_sems)

        @pl.when(step == 0)
        def _():
            barrier = pltpu.get_barrier_semaphore()
            partners = [other_core] + [
                {"tp": flipped(lax.axis_index("tp"), e)} for e in range(1, n)
            ]
            for partner in partners:
                pl.semaphore_signal(
                    barrier, inc=1, device_id=partner, device_id_type=pl.DeviceIdType.MESH
                )
            pl.semaphore_wait(barrier, len(partners))
            if rides:
                sends, (load, keep) = ride_copies()
                for c in sends:
                    c.start()
                load.start()
                load.wait()
                keep.start()

        @pl.when(lax.rem(step, steps) == 0)
        def _():
            for i, ref in enumerate(left_refs):
                left_s[i * rows : (i + 1) * rows] = ref[...]

        for i, ref in enumerate(right_refs):
            right_s[i * rows : (i + 1) * rows] = ref[...]
        product = contract_rows(left_s[...], right_s[...])

        @pl.when(step < steps)
        def _():
            sent[step] = product.astype(bf16)
            copy(step).start()

        @pl.when(step >= steps)
        def _():
            k = step - steps
            copy(k).wait_recv()
            total = (product + came[k].astype(f32)).astype(bf16)
            own_ref[...] = total[:block]
            x_ref[...] = total[block : 2 * block]
            y_ref[...] = total[2 * block : 3 * block]
            top_ref[...] = total[3 * block : 3 * block + half]
            low_ref[...] = total[3 * block + half :]

        @pl.when(step == 2 * steps - 1)
        def _():
            for k in range(steps):
                copy(k).wait_send()
            if rides:
                sends, own_row = ride_copies()
                for c in sends:
                    c.wait_send()
                    c.wait_recv()
                own_row[1].wait()

    columns = quarters * width
    heights = (block, block, block, half, half)
    out_shape = [struct(h, columns) for h in heights]
    arrays = list(lefts) + list(rights)
    late = lambda t: (0, jnp.maximum(t - steps, 0))
    ride_scratch = (
        []
        if ride is None
        else [
            pltpu.VMEM(ride.shape[1:], bf16),
            pltpu.SemaphoreType.DMA((n - 1,)),
            pltpu.SemaphoreType.DMA((n - 1,)),
            pltpu.SemaphoreType.DMA((2,)),
        ]
    )

    def right_map(t):
        t = lax.rem(t, steps)
        return (lax.div(t, parts), 0, first + lax.rem(t, parts))

    result = pl.pallas_call(
        kernel,
        grid=(2 * steps,),
        in_specs=[pl.BlockSpec((rows, size), lambda t: (0, 1 - lax.div(t, steps)))] * pairs
        + [pl.BlockSpec((None, rows, tw), right_map)] * pairs
        + [pl.BlockSpec(memory_space=pl.ANY)] * len(rides),
        out_specs=[pl.BlockSpec((h, tw), late) for h in heights]
        + [pl.BlockSpec(memory_space=pl.ANY)] * len(rides),
        out_shape=out_shape + [struct(*r.shape) for r in rides],
        scratch_shapes=[
            pltpu.VMEM((pairs * rows, size), bf16),
            pltpu.VMEM((pairs * rows, tw), bf16),
            pltpu.VMEM((steps, size, tw), bf16),
            pltpu.VMEM((steps, size, tw), bf16),
            pltpu.SemaphoreType.DMA((steps,)),
            pltpu.SemaphoreType.DMA((steps,)),
        ]
        + ride_scratch,
        compiler_params=pltpu.CompilerParams(
            collective_id=number, has_side_effects=True, vmem_limit_bytes=VMEM
        ),
        cost_estimate=cost(
            4 * pairs * rows * size * columns, nbytes(arrays) + nbytes(out_shape)
        ),
    )(*arrays, *rides)
    return (result[:5], result[5]) if rides else (result, None)


def waves_start(mover, n, source, target):
    if n != 4:
        return [mover.start(source, target(e), "tp", e) for e in range(1, n)]
    far = mover.start(source, target(2), "tp", 2)
    near = mover.start(source, target(1), "tp", 1)
    return [near, far]


def waves_forward(mover, n, waves, target):
    if n != 4:
        return waves
    waves[1].wait_recv()
    return waves + [mover.start(target(2), target(3), "tp", 1)]


def struct(*shape):
    return jax.ShapeDtypeStruct(shape, bf16)


class Spread:
    def __init__(self, mover, m, source, target, block):
        self.mover, self.m, self.source, self.block = mover, m, source, block
        self.at = lambda start, size: target(pl.ds(start, size))

    def first(self):
        go, block, source = self.mover.start, self.block, self.source
        if self.m != 8:
            self.all = [
                go(source, self.at(k * block, block), "wide", k) for k in range(1, self.m)
            ]
            return
        self.x = go(source, self.at(block, block), "wide", 2)
        self.y = go(source, self.at(2 * block, block), "wide", 4)
        self.cores = [go(source, self.at(4 * block, block), "wide", 1)]

    def second(self):
        if self.m != 8:
            return
        go, block = self.mover.start, self.block
        half = block // 2
        self.x.wait_recv()
        low = self.at(block + half, half)
        self.low = go(low, self.at(3 * block + half, half), "wide", 4)
        self.cores.append(go(self.at(block, block), self.at(5 * block, block), "wide", 1))
        self.y.wait_recv()
        top = self.at(2 * block, half)
        self.top = go(top, self.at(3 * block, half), "wide", 2)
        self.cores.append(go(self.at(2 * block, block), self.at(6 * block, block), "wide", 1))

    def third(self):
        if self.m != 8:
            return
        go, block = self.mover.start, self.block
        self.low.wait_recv()
        self.top.wait_recv()
        self.cores.append(go(self.at(3 * block, block), self.at(7 * block, block), "wide", 1))

    def last(self):
        for copy in self.all if self.m != 8 else self.cores:
            copy.wait_recv()


def exclusive_or(a, b, count):
    total, bit = 0, 1
    while bit < count:
        total = total + bit * lax.rem(lax.div(a, bit) + lax.div(b, bit), 2)
        bit *= 2
    return total


def gather_front(
    m, n, order, qkv_block, in_block, down_block, gain_block, tokens, out_grad, cosine, sine
):
    block, qw = qkv_block.shape
    fw, dw = in_block.shape[1], down_block.shape[1]
    depth = block * m
    pairs = n // 2
    rows_in = tokens.shape[0]
    tw = qw // 2
    gain_width = gain_block.shape[1]
    chunks = 2 if rows_in % 32 == 0 else 1
    chunk = rows_in // chunks

    def program(mover, ins, outs, scratch):
        qkv, inner, down, gain, x_ref, dy_ref, cos_ref, sin_ref = ins
        (
            weights, in_own, in_rest, down_rest, gains,
            x_out, dy_out, normed_out, hats, raws,
        ) = outs
        gain_s, normed_s, tile_s, hat_s, raw_s, tile_sems, hat_sems, raw_sems = scratch
        where, seat = lax.axis_index("wide"), lax.axis_index("tp")
        rows = pl.ds(0, block)
        place = lambda e: weights.at[e, rows]
        waves = waves_start(mover, n, qkv, place)
        spread_gains = Spread(mover, m, gain, lambda r: gains.at[r], GAIN_ROWS)
        spread_gains.first()
        spreads = [
            Spread(mover, m, qkv if q == 0 else place(q), lambda r, q=q: weights.at[q, r], block)
            for q in range(n)
        ]
        spreads[0].first()
        kept = [
            mover.keep(qkv, weights.at[0, rows]),
            mover.keep(inner, in_own.at[0, rows]),
        ]
        kept_gain = mover.keep(gain, gains.at[pl.ds(0, GAIN_ROWS)])
        spread_gains.second()
        spreads[0].second()
        spread_gains.third()
        spreads[0].third()
        columns = [
            pl.ds(pl.multiple_of(flipped(where, k) * block, 128), block) for k in order
        ]
        for k in range(m):
            cut = pl.ds(k * block, block)
            kept.append(mover.keep(x_ref.at[:, columns[k]], x_out.at[:, cut]))
            kept.append(mover.keep(dy_ref.at[:, columns[k]], dy_out.at[:, cut]))
        if n == 4:
            waves = waves_forward(mover, n, waves, place)
            spreads[2].first()
            waves[0].wait_recv()
            spreads[1].first()
            waves[2].wait_recv()
            spreads[3].first()
        else:
            for q in range(1, n):
                waves[q - 1].wait_recv()
                spreads[q].first()
        late = []
        for e in range(1, pairs):
            late.append(mover.start(inner, in_rest.at[e - 1, rows], "tp", 2 * e))
            late.append(mover.start(down, down_rest.at[e - 1, rows], "tp", 2 * e))

        spread_gains.last()
        kept_gain.wait()
        load = mover.keep(gains, gain_s)
        load.wait()

        def normalise(i, carry):
            part = pl.ds(pl.multiple_of(i * chunk, 16), chunk)
            x = x_ref[part, :].astype(f32)
            inverse = lax.rsqrt(jnp.mean(x * x, axis=-1, keepdims=True) + norm_eps)
            for k in range(m):
                piece = x_ref[part, columns[k]].astype(f32) * inverse
                scale = gain_s[k * GAIN_ROWS : k * GAIN_ROWS + 1, :block]
                normed_s[part, k * block : (k + 1) * block] = (piece * scale).astype(bf16)
            return carry

        lax.fori_loop(0, chunks, normalise, 0)
        kept.append(mover.keep(normed_s, normed_out))
        heads_at = 2 * block

        def head_gain(at):
            total = gain_s[0:1, at : at + HEAD_DIM]
            for k in range(1, m):
                total = total + gain_s[k * GAIN_ROWS : k * GAIN_ROWS + 1, at : at + HEAD_DIM]
            return total

        gain_q, gain_k = head_gain(heads_at), head_gain(heads_at + HEAD_DIM)

        turn = (2, 1, 3) if n == 4 else range(1, n)
        for q in turn:
            spreads[q].second()
        own = Spread(mover, m, inner, lambda r: in_own.at[0, r], block)
        own.first()
        for q in turn:
            spreads[q].third()
        for spread in spreads:
            spread.last()
        kept[0].wait()

        def fetch(q, part):
            return pltpu.make_async_copy(
                weights.at[q, :, pl.ds(part * tw, tw)], tile_s.at[part], tile_sems.at[part]
            )

        def leave(q, part):
            home = exclusive_or(seat, q, n)
            cut = pl.ds(part * tw, tw)
            return (
                pltpu.make_async_copy(
                    hat_s.at[part], hats.at[home, :, cut], hat_sems.at[part]
                ),
                pltpu.make_async_copy(
                    raw_s.at[part], raws.at[home, :, cut], raw_sems.at[part]
                ),
            )

        def turned(x, gain):
            inverse = lax.rsqrt(jnp.mean(x * x, axis=-1, keepdims=True) + norm_eps)
            u = x * inverse * gain
            return u * cos_ref[...] + pltpu.roll(u, HEAD_DIM // 2, 1) * sin_ref[...]

        def quarter(q, carry):
            for part in range(2):
                if part == 0:
                    fetch(q, 1).start()
                else:

                    @pl.when(q + 1 < n)
                    def _():
                        fetch(q + 1, 0).start()

                fetch(q, part).wait()

                @pl.when(q > 0)
                def _(part=part):
                    for c in leave(q, part):
                        c.wait()

                acc = dot_nn(normed_s[...], tile_s[part])
                raw_s[part] = acc.astype(bf16)
                if part == 0:
                    for cut in head_slices(tw):
                        hat_s[0, :, cut] = turned(acc[:, cut], gain_q).astype(bf16)
                else:
                    for cut in head_slices(tw // 2):
                        hat_s[1, :, cut] = (turned(acc[:, cut], gain_k) * key_scale).astype(bf16)
                    hat_s[1, :, tw // 2 :] = acc[:, tw // 2 :].astype(bf16)
                for c in leave(q, part):
                    c.start()
            return carry

        fetch(0, 0).start()
        lax.fori_loop(0, n // 2, quarter, 0)
        own.second()
        lax.fori_loop(n // 2, n, quarter, 0)
        own.third()
        for part in range(2):
            for c in leave(n - 1, part):
                c.wait()
        own.last()
        for copy in late:
            copy.wait_recv()
        for copy in kept[1:]:
            copy.wait()

    per = 8 if m == 8 else m - 1
    return transfer_call(
        program,
        m,
        n,
        [qkv_block, in_block, down_block, gain_block, tokens, out_grad, cosine, sine],
        [
            struct(n, depth, qw),
            struct(1, depth, fw),
            struct(pairs - 1, depth, fw),
            struct(pairs - 1, depth, dw),
            jax.ShapeDtypeStruct((m * GAIN_ROWS, gain_width), f32),
            struct(rows_in, depth),
            struct(rows_in, depth),
            struct(rows_in, depth),
            struct(n, rows_in, qw),
            struct(n, rows_in, qw),
        ],
        [
            pltpu.VMEM((m * GAIN_ROWS, gain_width), f32),
            pltpu.VMEM((rows_in, depth), bf16),
            pltpu.VMEM((2, depth, tw), bf16),
            pltpu.VMEM((2, rows_in, tw), bf16),
            pltpu.VMEM((2, rows_in, tw), bf16),
            pltpu.SemaphoreType.DMA((2,)),
            pltpu.SemaphoreType.DMA((2,)),
            pltpu.SemaphoreType.DMA((2,)),
        ],
        (n - 1) + per * (n + 2) + 2 * (pairs - 1),
        5 + 2 * m,
        1,
        vmem_ins=tuple(range(8)),
    )


def swap_heads(mover, n, mine, source, target):
    seat = lax.axis_index("tp")
    load = mover.keep(source.at[seat], mine)
    sends = [
        mover.start(source.at[flipped(seat, e)], target.at[seat], "tp", e) for e in range(1, n)
    ]
    load.wait()
    return sends, mover.keep(mine, target.at[seat])


def gather_middle(m, n, hats, in_rest, out_block, down_block):
    quarters, rows, width = hats.shape
    pairs, depth, fw = in_rest.shape
    block, ow = out_block.shape
    dw = down_block.shape[1]

    def program(mover, ins, outs, scratch):
        hat, _, out, down = ins
        heads, rest, weights, down_own = outs
        first = pl.ds(0, block)
        kept = [mover.keep(out, weights.at[0, first]), mover.keep(down, down_own.at[0, first])]
        place = lambda e: weights.at[e, first]
        waves = waves_start(mover, n, out, place)
        spreads = [
            Spread(mover, m, rest.at[p, first], lambda r, p=p: rest.at[p, r], block)
            for p in range(pairs)
        ]
        for spread in spreads:
            spread.first()
        waves = waves_forward(mover, n, waves, place)
        for copy in waves if n != 4 else (waves[0], waves[2]):
            copy.wait_recv()
        sends, own_row = swap_heads(mover, n, scratch[0], hat, heads)
        kept[0].wait()
        for spread in spreads:
            spread.second()
        quarter = Spread(mover, m, weights.at[:, first], lambda r: weights.at[:, r], block)
        quarter.first()
        for spread in spreads:
            spread.third()
        quarter.second()
        own = Spread(mover, m, down, lambda r: down_own.at[0, r], block)
        own.first()
        quarter.third()
        own.second()
        own.third()
        for spread in spreads + [own, quarter]:
            spread.last()
        for copy in sends:
            copy.wait_recv()
        kept[1].wait()
        own_row.wait()

    per = 8 if m == 8 else m - 1
    return transfer_call(
        program,
        m,
        n,
        [hats, in_rest, out_block, down_block],
        [
            struct(n, rows, width),
            struct(pairs, depth, fw),
            struct(n, depth, ow),
            struct(1, depth, dw),
        ],
        [pltpu.VMEM((rows, width), bf16)],
        2 * (n - 1) + per * (pairs + 2),
        4,
        2,
        vmem_ins=(2, 3),
        aliases={1: 1},
    )


def gather_late(m, n, heads, down_rest):
    quarters, rows, width = heads.shape
    pairs, depth, dw = down_rest.shape
    block = depth // m

    def program(mover, ins, outs, scratch):
        source, _ = ins
        target, rest = outs
        first = pl.ds(0, block)
        sends, own_row = swap_heads(mover, n, scratch[0], source, target)
        spreads = [
            Spread(mover, m, rest.at[p, first], lambda r, p=p: rest.at[p, r], block)
            for p in range(pairs)
        ]
        for stage in ("first", "second", "third", "last"):
            for spread in spreads:
                getattr(spread, stage)()
        for copy in sends:
            copy.wait_recv()
        own_row.wait()

    per = 8 if m == 8 else m - 1
    return transfer_call(
        program,
        m,
        n,
        [heads, down_rest],
        [struct(n, rows, width), struct(pairs, depth, dw)],
        [pltpu.VMEM((rows, width), bf16)],
        (n - 1) + per * pairs,
        2,
        3,
        aliases={1: 1},
    )


def shuffle_columns(a, order):
    rows, count = a.shape[0], order.shape[0]
    width = a.shape[1] // count

    def kernel(order_ref, in_ref, out_ref):
        out_ref[...] = in_ref[...]

    return pl.pallas_call(
        kernel,
        grid_spec=pltpu.PrefetchScalarGridSpec(
            num_scalar_prefetch=1,
            grid=(count,),
            in_specs=[pl.BlockSpec((rows, width), lambda k, s: (0, s[k]))],
            out_specs=pl.BlockSpec((rows, width), lambda k, s: (0, k)),
        ),
        out_shape=jax.ShapeDtypeStruct(a.shape, a.dtype),
        cost_estimate=cost(0, 2 * nbytes([a])),
    )(order, a)


def inverse_rms(values):
    return lax.rsqrt(jnp.mean(values * values, axis=-1, keepdims=True) + norm_eps)


def norm_back(grads, unit_values, inverse, gain):
    scaled = grads * gain
    return inverse * (scaled - unit_values * jnp.mean(scaled * unit_values, axis=-1, keepdims=True))


def after(values, *conditions):
    return lax.optimization_barrier((values, conditions))[0]


class Job:
    def __init__(self, stages):
        self.stages = stages
        self.result = None
        self.started, self.pending = next(stages)

    def advance(self, came):
        try:
            self.started, self.pending = self.stages.send(came)
        except StopIteration as stop:
            self.result = stop.value
            self.pending = None

    def finish(self):
        while self.result is None:
            self.advance(self.pending)
        return self.result


def tick(values, *jobs):
    jobs = [j for j in jobs if j.result is None]
    values, came = lax.optimization_barrier((values, [j.pending for j in jobs]))
    for j, c in zip(jobs, came):
        j.advance(c)
    return values


def local(
    m,
    n,
    tokens,
    out_grad,
    seg_ids,
    parent_table,
    path_pos,
    attn_gain,
    w_query,
    w_key,
    w_value,
    w_out,
    q_gain,
    k_gain,
    ffn_gain,
    w_gate,
    w_up,
    w_down,
):
    rows, depth = tokens.shape
    block = depth // m
    order = [0, 2, 4, 6, 1, 3, 5, 7] if m == 8 else list(range(m))
    where = lax.axis_index("wide").astype(jnp.int32)
    seat = lax.axis_index("tp").astype(jnp.int32)
    relative = jnp.asarray(order, jnp.int32) ^ where
    inverse_order = [order.index(k) for k in range(m)]
    absolute = jnp.take(jnp.asarray(inverse_order, jnp.int32), jnp.arange(m, dtype=jnp.int32) ^ where)
    seats = jnp.arange(n, dtype=jnp.int32) ^ seat
    plain = jnp.arange(n, dtype=jnp.int32)

    def over(axis, a, mask):
        size = m if axis == "wide" else n
        return lax.ppermute(a, axis, [(i, i ^ mask) for i in range(size)])

    def scatter(lefts, rights, cut, number, ride=None, rode=None):
        if m != 8:
            if ride is not None:
                rode.append(swap(ride))
            other = weight_gradient(lefts, rights, 1, cut)
            mine = weight_gradient(lefts, rights, 0, cut)
            both = jnp.concatenate([mine, other])
            got = yield both, [over("wide", both[k * block : (k + 1) * block], k) for k in range(1, m)]
            return sum((g.astype(f32) for g in got), both[:block].astype(f32))
        (own, x, y, top_sent, low_sent), came = gradient_pair(lefts, rights, cut, number, ride)
        if ride is not None:
            rode.append(came)
        half = block // 2
        top, low = yield (top_sent, low_sent), [over("wide", top_sent, 2), over("wide", low_sent, 4)]
        for_x = jnp.concatenate([x[:half], (x[half:].astype(f32) + low.astype(f32)).astype(bf16)])
        for_y = jnp.concatenate([(y[:half].astype(f32) + top.astype(f32)).astype(bf16), y[half:]])
        from_x, from_y = yield [for_x, for_y], [over("wide", for_x, 2), over("wide", for_y, 4)]
        return own.astype(f32) + from_x.astype(f32) + from_y.astype(f32)

    def ffn_share(left, rights, number, ride=None, rode=None):
        total = yield from scatter(left, rights, None, number, ride, rode)
        parts = [total[:, e * fcols : (e + 1) * fcols].astype(bf16) for e in range(1, n // 2)]
        sent = yield parts, [over("tp", p, 2 * (e + 1)) for e, p in enumerate(parts)]
        return sum((x.astype(f32) for x in sent), total[:, :fcols])

    def swap(a):
        return lax.all_to_all(a, "tp", split_axis=0, concat_axis=0, tiled=True)

    def attn_share(left, right, cut, number):
        total = yield from scatter([left], [right], cut, number)
        parts = total.astype(bf16).reshape(block, n, -1).transpose(1, 0, 2)
        (came,) = yield parts, [swap(parts)]
        return jnp.sum(came.astype(f32), axis=0)

    qkv_block = jnp.concatenate([w_query, w_key, w_value], axis=1)
    out_block = w_out.T
    in_block = jnp.concatenate([w_gate, w_up], axis=1)
    down_block = w_down.T
    aw = w_query.shape[1]
    kv = w_key.shape[1] // HEAD_DIM
    fcols = w_gate.shape[1]
    fw = fcols // 3

    small = q_gain.shape[0]
    head_row = lambda g: lax.dynamic_update_slice(
        jnp.zeros((HEAD_DIM,), f32), g.astype(f32), (where * small,)
    )
    gain_row = jnp.concatenate(
        [attn_gain.astype(f32), ffn_gain.astype(f32), head_row(q_gain), head_row(k_gain)]
    )[None]
    gain_block = jnp.pad(gain_row, ((0, GAIN_ROWS - 1), (0, 0)))
    base = where * parent_table.shape[0]
    block_segs = seg_ids[TRUNK::BRANCH] - base
    hit = block_segs[:, None] == jnp.arange(parent_table.shape[0], dtype=jnp.int32)[None, :]
    block_parents = jnp.sum(jnp.where(hit, parent_table[None, :] - base, 0), axis=1)
    match = block_parents[:, None] == block_segs[None, :]
    number = TRUNK_BLOCKS + jnp.arange(FORKS2, dtype=jnp.int32)
    parents = jnp.where(
        jnp.any(match, axis=1), jnp.sum(jnp.where(match, number[None, :], 0), axis=1), number
    ).astype(jnp.int32)

    own_pos = lax.dynamic_slice_in_dim(path_pos, seat * rows, rows, 0).astype(f32)
    frequency = rope_base ** (-(jnp.arange(HEAD_DIM // 2, dtype=f32) * 2.0) / HEAD_DIM)
    angles = own_pos[:, None] * frequency[None, :]
    cosine, sine = jnp.cos(angles), jnp.sin(angles)
    cosine = jnp.concatenate([cosine, cosine], axis=-1)
    sine = jnp.concatenate([-sine, sine], axis=-1)

    (
        qkv_all, in_own, in_rest, down_rest, gains, stream_low, cotangent, normed_one, hats, raws,
    ) = gather_front(
        m, n, order, qkv_block, in_block, down_block, gain_block, tokens, out_grad, cosine, sine
    )
    gains = gains[::GAIN_ROWS]
    gain_one = gains[:, :block].reshape(1, depth)
    gain_two = gains[:, block : 2 * block].reshape(1, depth)
    gain_q = jnp.sum(gains[:, 2 * block : 2 * block + HEAD_DIM], axis=0, keepdims=True)
    gain_k = jnp.sum(gains[:, 2 * block + HEAD_DIM :], axis=0, keepdims=True)
    qkv_tiles = Tiles([qkv_all], 2, 0, aw)
    qkv, in_rest, out_all, down_own = gather_middle(m, n, hats, in_rest, out_block, down_block)
    qkv = qkv.reshape(n * rows, -1)
    attended_heads, logs = attention_forward(qkv, parents, kv)
    attended, down_rest = gather_late(m, n, attended_heads.reshape(n, rows, -1), down_rest)
    out_tiles = Tiles([out_all], 1, 0, aw)
    stream = stream_low.astype(f32)
    after_attn = stream + project_columns([attended], [out_tiles], seats, depth, f32)

    inverse_two = inverse_rms(after_attn)
    unit_two = after_attn * inverse_two
    normed_two = (unit_two * gain_two).astype(bf16)
    normed_two_next = over("tp", normed_two, 1)

    gate_tiles = Tiles([in_own, in_rest], 3, 0, fw)
    up_tiles = Tiles([in_own, in_rest], 3, 3, fw)
    down_tiles = Tiles([down_own, down_rest], 3, 0, fw)

    hidden, gate, up = feed_forward(normed_two, gate_tiles, up_tiles, plain)
    down = project_columns([hidden], [down_tiles], plain, depth, f32)
    normed_two_next, cotangent_sent = after((normed_two_next, cotangent), (down, normed_two_next))
    cotangent_next = over("tp", cotangent_sent, 1)
    hidden_next, gate_next, up_next = feed_forward(normed_two_next, gate_tiles, up_tiles, plain)
    down_part = project_columns([hidden_next], [down_tiles], plain, depth, bf16)
    own_grad = after(cotangent, down_part)
    gate_grad, up_grad = feed_back(own_grad, gate, up, down_tiles, plain)
    cotangent_next, hidden_late = after((cotangent_next, hidden), gate_grad)
    down_job = Job(ffn_share([cotangent, cotangent_next], [hidden_late, hidden_next], 4))
    cotangent_next, down_sent = after((cotangent_next, down_part), down_job.started)
    down_next = over("tp", down_sent, 1)
    gate_grad_next, up_grad_next = feed_back(
        cotangent_next, gate_next, up_next, down_tiles, plain
    )
    gate_late, up_late = tick((gate_grad_next, up_grad_next), down_job)
    gate_late, up_late = after((gate_late, up_late), down_job.started)
    back_part = project_columns([gate_late, up_late], [gate_tiles, up_tiles], plain, depth, bf16)
    back_part, down_next = after((back_part, down_next), back_part)
    back_next = over("tp", back_part, 1)
    gate_grad, up_grad = after((gate_grad, up_grad), back_part)
    gate_job = Job(ffn_share([normed_two, normed_two_next], [gate_grad, gate_grad_next], 5))
    gate_late, up_late = after((gate_grad, up_grad), gate_job.started)
    gate_late, up_late = tick((gate_late, up_late), down_job)
    gate_late, up_late = after((gate_late, up_late), down_job.started)
    back = project_columns([gate_late, up_late], [gate_tiles, up_tiles], plain, depth, f32)
    back, back_next = after((back, back_next), back)
    back = tick(back, gate_job)
    back = after(back, gate_job.started)
    normed_two_grad = back + back_next.astype(f32)

    ffn_gain_part = jnp.sum(normed_two_grad * unit_two, axis=0)
    stream_grad = cotangent.astype(f32) + norm_back(
        normed_two_grad, unit_two, inverse_two, gain_two
    )
    grad_low = stream_grad.astype(bf16)
    attended_grad = tick(project_rows(grad_low, out_tiles, seats), down_job)
    lefts, up_grads = after(
        ([normed_two, normed_two_next], [up_grad, up_grad_next]), attended_grad
    )
    rode = []
    up_job = Job(ffn_share(lefts, up_grads, 6, attended_grad, rode))
    grad_heads = after(rode[0].reshape(n * rows, -1), up_job.started)
    grad_heads = tick(grad_heads, gate_job)
    grad_heads = after(grad_heads, gate_job.started)
    back_hats = attention_backward(qkv, attended_heads, grad_heads, logs, parents, kv)
    back_hats = tick(back_hats, gate_job, up_job)
    back_hats = after(back_hats, up_job.started)
    back_hats_own = swap(back_hats.reshape(n, rows, -1))
    grad_low, down_next, after_attn = after((grad_low, down_next, after_attn), back_hats)
    out_job = Job(attn_share(grad_low, attended, None, 7))
    fence = tick(after(grad_low, out_job.started), up_job)
    back_hats_own = after(back_hats_own, fence, out_job.started)
    raw_grads, q_sum, k_sum = qkv_back(back_hats_own, raws, cosine, sine, gain_q, gain_k)
    raw_grads = tick(raw_grads, out_job)
    q_job = Job(attn_share(normed_one, after(raw_grads, out_job.started), 0, 8))
    raw_late = after(raw_grads, q_job.started)
    k_job = Job(attn_share(normed_one, raw_late, 1, 9))
    raw_late = tick(after(raw_late, k_job.started), q_job, out_job, up_job)
    raw_late = after(raw_late, q_job.started)
    normed_one_grad = project_columns([raw_late], [qkv_tiles], seats, depth, f32)
    normed_one_grad = tick(normed_one_grad, q_job, k_job, up_job, out_job)
    normed_one_grad = after(normed_one_grad, q_job.started, k_job.started)
    mixed = (after_attn + down + down_next.astype(f32)).astype(bf16)
    mixed = shuffle_columns(mixed, absolute)
    stream = after(stream_low, normed_one_grad).astype(f32)
    inverse_one = inverse_rms(stream)
    unit_one = stream * inverse_one
    attn_gain_part = jnp.sum(normed_one_grad * unit_one, axis=0)
    tokens_grad = (
        stream_grad + norm_back(normed_one_grad, unit_one, inverse_one, gain_one)
    ).astype(bf16)
    tokens_grad = shuffle_columns(tokens_grad, absolute)

    parts = jnp.concatenate(
        [
            attn_gain_part.reshape(m, block),
            ffn_gain_part.reshape(m, block),
            jnp.take(q_sum.reshape(m, small), relative, axis=0),
            jnp.take(k_sum.reshape(m, small), relative, axis=0),
        ],
        axis=1,
    )
    size = m
    while size > 1:
        size //= 2
        parts = parts[:size] + over("wide", parts[size:], order[size])
    step = 1
    while step < n:
        parts = parts + over("tp", parts, step)
        step *= 2
    sums = parts[0]
    gate_share, up_share = gate_job.finish(), up_job.finish()
    down_share, out_share = down_job.finish().T, out_job.finish().T
    q_share, k_share = q_job.finish(), k_job.finish()
    return (
        mixed,
        tokens_grad,
        sums[:block],
        q_share,
        k_share[:, : aw // 2],
        k_share[:, aw // 2 :],
        out_share,
        sums[2 * block : 2 * block + small],
        sums[2 * block + small :],
        sums[block : 2 * block],
        gate_share,
        up_share,
        down_share,
    )


def solution(mesh):
    both = P(("wide", "tp"), None)
    w, wt, tw = P("wide"), P("wide", "tp"), P("tp", "wide")
    return jax.shard_map(
        functools.partial(local, mesh.shape["wide"], mesh.shape["tp"]),
        mesh=mesh,
        in_specs=(both, both, w, w, w, w, wt, wt, wt, tw, w, w, w, wt, wt, tw),
        out_specs=(both, both, w, wt, wt, wt, tw, w, w, w, wt, wt, tw),
        check_vma=False,
    )
```

```python
import functools
import math

import jax
import jax.numpy as jnp
from jax import lax
from jax.experimental import pallas as pl
from jax.experimental.pallas import tpu as pltpu
from jax.sharding import PartitionSpec as P

HEAD_DIM = 128
TRUNK = 1152
BRANCH = 128
FORKS2 = 8
TREE_TOK = 2176
GROUP = 2

norm_eps = 1e-06
rope_base = 1000000.0
score_scale = HEAD_DIM ** (-0.5)
key_scale = score_scale * math.log2(math.e)
LN2 = math.log(2.0)
VMEM = 52 * 1024 * 1024
COST = 0.01
GAIN_ROWS = 16

f32 = jnp.float32
bf16 = jnp.bfloat16


def dot_nn(a, b):
    return lax.dot_general(a, b, (((1,), (0,)), ((), ())), preferred_element_type=f32)


def dot_nt(a, b):
    return lax.dot_general(a, b, (((1,), (1,)), ((), ())), preferred_element_type=f32)


def contract_rows(a, b):
    return lax.dot_general(a, b, (((0,), (0,)), ((), ())), preferred_element_type=f32)


def params():
    return pltpu.CompilerParams(vmem_limit_bytes=VMEM)


def cost(flops, nbytes):
    return pl.CostEstimate(flops=int(flops * COST), bytes_accessed=int(nbytes * COST), transcendentals=0)


def nbytes(arrays):
    return sum(a.size * a.dtype.itemsize for a in arrays)


class Tiles:
    def __init__(self, arrays, parts, base, width):
        self.list = list(arrays)
        self.quarters = sum(a.shape[0] for a in self.list)
        self.depth = self.list[0].shape[1]
        self.parts, self.base, self.width = parts, base, width
        self.steps = self.quarters * parts

    def arrays(self):
        return self.list

    def scratch(self):
        return [pltpu.VMEM((2, self.depth, self.width), bf16), pltpu.SemaphoreType.DMA((2,))]

    def fetch(self, refs, buf, sems, step):
        slot = lax.rem(step, 2)
        quarter = lax.div(step, self.parts)
        part = step - quarter * self.parts
        col = pl.multiple_of((self.base + part) * self.width, 128)

        def begin(ref, at):
            pltpu.make_async_copy(
                ref.at[at, :, pl.ds(col, self.width)], buf.at[slot], sems.at[slot]
            ).start()

        split = self.list[0].shape[0]
        if len(refs) == 1:
            begin(refs[0], quarter)
        else:

            @pl.when(quarter < split)
            def _():
                begin(refs[0], quarter)

            @pl.when(quarter >= split)
            def _():
                begin(refs[1], quarter - split)

    def wait(self, refs, buf, sems, step):
        slot = lax.rem(step, 2)
        pltpu.make_async_copy(
            refs[0].at[0, :, pl.ds(0, self.width)], buf.at[slot], sems.at[slot]
        ).wait()
        return slot


def tiled_call(body, sets, seats, ins, in_specs, out_shape, out_specs, scratch, flops):
    steps = sets[0].steps
    counts = [len(s.arrays()) for s in sets]
    n_in, n_out = len(ins), len(out_shape)

    def kernel(seat_ref, *refs):
        at = 0
        piece_refs = []
        for c in counts:
            piece_refs.append(refs[at : at + c])
            at += c
        in_refs = refs[at : at + n_in]
        at += n_in
        out_refs = refs[at : at + n_out]
        at += n_out
        bufs = [(refs[at + 2 * i], refs[at + 2 * i + 1]) for i in range(len(sets))]
        own = refs[at + 2 * len(sets) :]
        step = pl.program_id(0)

        @pl.when(step == 0)
        def _():
            for s, p, (buf, sems) in zip(sets, piece_refs, bufs):
                s.fetch(p, buf, sems, step)

        @pl.when(step + 1 < steps)
        def _():
            for s, p, (buf, sems) in zip(sets, piece_refs, bufs):
                s.fetch(p, buf, sems, step + 1)

        tiles = []
        for s, p, (buf, sems) in zip(sets, piece_refs, bufs):
            slot = s.wait(p, buf, sems, step)
            tiles.append(buf.at[slot])
        body(step, tiles, in_refs, out_refs, own)

    weights = [a for s in sets for a in s.arrays()]
    return pl.pallas_call(
        kernel,
        grid_spec=pltpu.PrefetchScalarGridSpec(
            num_scalar_prefetch=1,
            grid=(steps,),
            in_specs=[pl.BlockSpec(memory_space=pl.ANY)] * len(weights) + in_specs,
            out_specs=out_specs,
            scratch_shapes=[x for s in sets for x in s.scratch()] + scratch,
        ),
        out_shape=out_shape,
        compiler_params=params(),
        cost_estimate=cost(flops, nbytes(weights) + nbytes(ins) + nbytes(out_shape)),
    )(seats, *weights, *ins)


def whole(array):
    return pl.BlockSpec(array.shape, lambda t, s: (0,) * len(array.shape))


def seated(rows, width, parts):
    return pl.BlockSpec(
        (None, rows, width),
        lambda t, s: (s[lax.div(t, parts)], 0, lax.rem(t, parts)),
    )


def head_slices(width):
    return [slice(h * HEAD_DIM, (h + 1) * HEAD_DIM) for h in range(width // HEAD_DIM)]


def project_rows(a, tiles, seats):
    rows, tw = a.shape[0], tiles.width

    def body(step, weights, ins, outs, own):
        outs[0][...] = dot_nn(ins[0][...], weights[0][...]).astype(bf16)

    return tiled_call(
        body,
        [tiles],
        seats,
        [a],
        [whole(a)],
        [jax.ShapeDtypeStruct((tiles.quarters, rows, tiles.parts * tw), bf16)],
        [seated(rows, tw, tiles.parts)],
        [],
        2 * rows * a.shape[1] * tw * tiles.steps,
    )[0]


def project_columns(lefts, sets, seats, depth, out_dtype):
    rows, tw, steps = lefts[0].shape[1], sets[0].width, sets[0].steps

    def body(step, weights, ins, outs, own):
        acc = own[0]
        total = dot_nt(ins[0][...], weights[0][...])
        for left, weight in zip(ins[1:], weights[1:]):
            total = total + dot_nt(left[...], weight[...])

        @pl.when(step == 0)
        def _():
            acc[...] = total

        @pl.when(step > 0)
        def _():
            acc[...] += total

        @pl.when(step == steps - 1)
        def _():
            outs[0][...] = acc[...].astype(out_dtype)

    return tiled_call(
        body,
        sets,
        seats,
        list(lefts),
        [seated(rows, tw, s.parts) for s in sets],
        [jax.ShapeDtypeStruct((rows, depth), out_dtype)],
        [pl.BlockSpec((rows, depth), lambda t, s: (0, 0))],
        [pltpu.VMEM((rows, depth), f32)],
        2 * rows * depth * tw * steps * len(sets),
    )[0]


def project_residual(left, tiles, seats, stream, gain):
    rows, depth = stream.shape
    tw, steps = tiles.width, tiles.steps

    def body(step, weights, ins, outs, own):
        acc = own[0]
        total = dot_nt(ins[0][...], weights[0][...])

        @pl.when(step == 0)
        def _():
            acc[...] = ins[1][...].astype(f32) + total

        @pl.when(step > 0)
        def _():
            acc[...] += total

        @pl.when(step == steps - 1)
        def _():
            value = acc[...]
            outs[0][...] = value
            inverse = lax.rsqrt(jnp.mean(value * value, axis=-1, keepdims=True) + norm_eps)
            outs[1][...] = (value * inverse * ins[2][...]).astype(bf16)

    return tiled_call(
        body,
        [tiles],
        seats,
        [left, stream, gain],
        [seated(rows, tw, tiles.parts), whole(stream), whole(gain)],
        [jax.ShapeDtypeStruct((rows, depth), f32), struct(rows, depth)],
        [pl.BlockSpec((rows, depth), lambda t, s: (0, 0))] * 2,
        [pltpu.VMEM((rows, depth), f32)],
        2 * rows * depth * tw * steps,
    )


def feed_forward(normed, gate_tiles, up_tiles, seats):
    rows, tw = normed.shape[0], gate_tiles.width

    def body(step, weights, ins, outs, own):
        a = ins[0][...]
        gate = dot_nn(a, weights[0][...])
        up = dot_nn(a, weights[1][...])
        outs[0][...] = (gate * jax.nn.sigmoid(gate) * up).astype(bf16)
        outs[1][...] = gate.astype(bf16)
        outs[2][...] = up.astype(bf16)

    shape = jax.ShapeDtypeStruct((gate_tiles.quarters, rows, gate_tiles.parts * tw), bf16)
    return tiled_call(
        body,
        [gate_tiles, up_tiles],
        seats,
        [normed],
        [whole(normed)],
        [shape] * 3,
        [seated(rows, tw, gate_tiles.parts)] * 3,
        [],
        4 * rows * normed.shape[1] * tw * gate_tiles.steps,
    )


def feed_back(cotangent, gate, up, down_tiles, seats):
    rows, tw = cotangent.shape[0], down_tiles.width

    def body(step, weights, ins, outs, own):
        grad = dot_nn(ins[0][...], weights[0][...])
        g = ins[1][...].astype(f32)
        u = ins[2][...].astype(f32)
        s = jax.nn.sigmoid(g)
        outs[0][...] = (grad * u * s * (1.0 + g * (1.0 - s))).astype(bf16)
        outs[1][...] = (grad * (g * s)).astype(bf16)

    shape = jax.ShapeDtypeStruct(gate.shape, bf16)
    tile = seated(rows, tw, down_tiles.parts)
    return tiled_call(
        body,
        [down_tiles],
        seats,
        [cotangent, gate, up],
        [whole(cotangent), tile, tile],
        [shape] * 2,
        [tile] * 2,
        [],
        2 * rows * cotangent.shape[1] * tw * down_tiles.steps,
    )


def qkv_back(grad_hat, raw, cosine, sine, q_gain, k_gain):
    quarters, rows, width = grad_hat.shape
    tw = width // 2

    def kernel(g_ref, r_ref, cos_ref, sin_ref, qg, kg, out, qsum, ksum):
        @pl.when(pl.program_id(0) == 0)
        def _():
            qsum[...] = jnp.zeros_like(qsum)
            ksum[...] = jnp.zeros_like(ksum)

        def back(cut, gain, total):
            w = g_ref[:, cut].astype(f32)
            w = w * cos_ref[...] + pltpu.roll(w * sin_ref[...], HEAD_DIM // 2, 1)
            x = r_ref[:, cut].astype(f32)
            inverse = lax.rsqrt(jnp.mean(x * x, axis=-1, keepdims=True) + norm_eps)
            u = x * inverse
            wu = w * u
            scaled = w * gain
            out[:, cut] = (
                inverse * (scaled - u * jnp.mean(wu * gain, axis=-1, keepdims=True))
            ).astype(bf16)
            return total + jnp.sum(wu, axis=0, keepdims=True)

        total = jnp.zeros((1, HEAD_DIM), f32)
        cuts = head_slices(width)
        n_query, n_key = tw // HEAD_DIM, tw // HEAD_DIM // 2
        for cut in cuts[:n_query]:
            total = back(cut, qg[...], total)
        qsum[...] += total
        total = jnp.zeros((1, HEAD_DIM), f32)
        for cut in cuts[n_query : n_query + n_key]:
            total = back(cut, kg[...], total)
        ksum[...] += total
        out[:, tw + tw // 2 :] = g_ref[:, tw + tw // 2 :]

    ins = [grad_hat, raw, cosine, sine, q_gain, k_gain]
    gain_shape = jax.ShapeDtypeStruct((1, HEAD_DIM), f32)
    out_shape = [jax.ShapeDtypeStruct(grad_hat.shape, bf16), gain_shape, gain_shape]
    tile = pl.BlockSpec((None, rows, width), lambda e: (e, 0, 0))
    fixed = lambda x: pl.BlockSpec(x.shape, lambda e: (0, 0))
    return pl.pallas_call(
        kernel,
        grid=(quarters,),
        in_specs=[tile, tile] + [fixed(x) for x in ins[2:]],
        out_specs=[tile, fixed(gain_shape), fixed(gain_shape)],
        out_shape=out_shape,
        compiler_params=params(),
        cost_estimate=cost(40 * quarters * rows * width, nbytes(ins) + nbytes(out_shape)),
    )(*ins)


def attention_specs(kv):
    q = pl.BlockSpec((TREE_TOK, GROUP * HEAD_DIM), lambda n, s: (0, n))
    k = pl.BlockSpec((TREE_TOK, HEAD_DIM), lambda n, s: (0, GROUP * kv + n))
    v = pl.BlockSpec((TREE_TOK, HEAD_DIM), lambda n, s: (0, (GROUP + 1) * kv + n))
    return q, k, v


def stacked(ref, start):
    rows = pl.ds(start, BRANCH)
    return jnp.concatenate(
        [ref[rows, h * HEAD_DIM : (h + 1) * HEAD_DIM] for h in range(GROUP)], axis=0
    )


def causal():
    key = lax.broadcasted_iota(jnp.int32, (BRANCH, GROUP * BRANCH), 0)
    query = lax.rem(lax.broadcasted_iota(jnp.int32, (BRANCH, GROUP * BRANCH), 1), BRANCH)
    return key <= query


TRUNK_BLOCKS = TRUNK // BRANCH
BLOCKS = TREE_TOK // BRANCH


def attention_forward(qkv, parents, kv):
    def kernel(parent_ref, q_ref, k_ref, v_ref, out_ref, log_ref, vt):
        vt[...] = v_ref[...].T
        mask = causal()

        def part(q, start, size, rule):
            score = dot_nt(k_ref[pl.ds(start, size), :], q)
            weight = jnp.exp2(score)
            if rule is not None:
                weight = rule(weight)
            out = dot_nn(vt[:, pl.ds(start, size)], weight.astype(bf16))
            return out, jnp.sum(weight, axis=0, keepdims=True)

        def finish(block, start, pieces):
            out = sum(p[0] for p in pieces)
            total = sum(p[1] for p in pieces)
            out = (out / total).T.astype(bf16)
            for h in range(GROUP):
                out_ref[pl.ds(start, BRANCH), h * HEAD_DIM : (h + 1) * HEAD_DIM] = out[
                    h * BRANCH : (h + 1) * BRANCH
                ]
            log_ref[0, pl.ds(block, 1), :] = jnp.log2(total)

        diagonal = lambda w: jnp.where(mask, w, 0.0)
        for block in range(TRUNK_BLOCKS):
            q = stacked(q_ref, block * BRANCH)
            pieces = [part(q, block * BRANCH, BRANCH, diagonal)]
            if block > 0:
                pieces.append(part(q, 0, block * BRANCH, None))
            finish(block, block * BRANCH, pieces)

        def branch(i, carry):
            block = TRUNK_BLOCKS + i
            start = pl.multiple_of(block * BRANCH, BRANCH)
            q = stacked(q_ref, start)
            parent = parent_ref[i]
            has = (parent != block).astype(f32)
            pieces = [
                part(q, start, BRANCH, diagonal),
                part(q, pl.multiple_of(parent * BRANCH, BRANCH), BRANCH, lambda w: w * has),
                part(q, 0, TRUNK, None),
            ]
            finish(block, start, pieces)
            return carry

        lax.fori_loop(0, FORKS2, branch, 0)

    q, k, v = attention_specs(kv)
    out_shape = [
        jax.ShapeDtypeStruct((TREE_TOK, GROUP * kv * HEAD_DIM), bf16),
        jax.ShapeDtypeStruct((kv, BLOCKS, GROUP * BRANCH), f32),
    ]
    return pl.pallas_call(
        kernel,
        grid_spec=pltpu.PrefetchScalarGridSpec(
            num_scalar_prefetch=1,
            grid=(kv,),
            in_specs=[q, k, v],
            out_specs=[
                q,
                pl.BlockSpec((1, BLOCKS, GROUP * BRANCH), lambda n, s: (n, 0, 0)),
            ],
            scratch_shapes=[pltpu.VMEM((HEAD_DIM, TREE_TOK), bf16)],
        ),
        out_shape=out_shape,
        compiler_params=params(),
        cost_estimate=cost(kv * 2.2e6 * 2 * GROUP * 256 * 2, nbytes([qkv]) + nbytes(out_shape)),
    )(parents, qkv, qkv, qkv)


def attention_backward(qkv, attended, grads, logs, parents, kv):
    width = qkv.shape[1]

    def kernel(
        parent_ref, q_ref, k_ref, v_ref, o_ref, do_ref, log_ref, out_ref, kt, dk, dv, dq_ref
    ):
        kt[...] = k_ref[...].T
        dk[...] = jnp.zeros_like(dk)
        dv[...] = jnp.zeros_like(dv)
        mask = causal()

        def part(q, do, log, delta, start, size, rule):
            rows = pl.ds(start, size)
            prob = jnp.exp2(dot_nt(k_ref[rows, :], q) - log)
            if rule is not None:
                prob = rule(prob)
            grad = dot_nt(v_ref[rows, :], do)
            score_grad = (prob * (grad - delta)).astype(bf16)
            dk[rows, :] += dot_nn(score_grad, q)
            dv[rows, :] += dot_nn(prob.astype(bf16), do)
            return dot_nn(kt[:, rows], score_grad)

        def one(block, start, ranges):
            q = stacked(q_ref, start)
            do = stacked(do_ref, start)
            o = stacked(o_ref, start)
            delta = jnp.sum((do.astype(f32) * o.astype(f32)).T, axis=0, keepdims=True)
            log = log_ref[0, pl.ds(block, 1), :]
            total = sum(part(q, do, log, delta, *r) for r in ranges)
            out = (total * LN2).T.astype(bf16)
            for h in range(GROUP):
                dq_ref[pl.ds(start, BRANCH), h * HEAD_DIM : (h + 1) * HEAD_DIM] = out[
                    h * BRANCH : (h + 1) * BRANCH
                ]

        diagonal = lambda p: jnp.where(mask, p, 0.0)
        for block in range(TRUNK_BLOCKS):
            ranges = [(block * BRANCH, BRANCH, diagonal)]
            if block > 0:
                ranges.append((0, block * BRANCH, None))
            one(block, block * BRANCH, ranges)

        def branch(i, carry):
            block = TRUNK_BLOCKS + i
            start = pl.multiple_of(block * BRANCH, BRANCH)
            parent = parent_ref[i]
            has = (parent != block).astype(f32)
            one(
                block,
                start,
                [
                    (start, BRANCH, diagonal),
                    (pl.multiple_of(parent * BRANCH, BRANCH), BRANCH, lambda p: p * has),
                    (0, TRUNK, None),
                ],
            )
            return carry

        lax.fori_loop(0, FORKS2, branch, 0)
        for head in range(kv):

            @pl.when(pl.program_id(0) == head)
            def _(head=head):
                wide = GROUP * HEAD_DIM
                out_ref[:, head * wide : (head + 1) * wide] = dq_ref[...]
                at = kv * wide + head * HEAD_DIM
                out_ref[:, at : at + HEAD_DIM] = (dk[...] * score_scale).astype(bf16)
                at += kv * HEAD_DIM
                out_ref[:, at : at + HEAD_DIM] = dv[...].astype(bf16)

    q, k, v = attention_specs(kv)
    out_shape = jax.ShapeDtypeStruct((TREE_TOK, width), bf16)
    return pl.pallas_call(
        kernel,
        grid_spec=pltpu.PrefetchScalarGridSpec(
            num_scalar_prefetch=1,
            grid=(kv,),
            in_specs=[
                q,
                k,
                v,
                q,
                q,
                pl.BlockSpec((1, BLOCKS, GROUP * BRANCH), lambda n, s: (n, 0, 0)),
            ],
            out_specs=pl.BlockSpec((TREE_TOK, width), lambda n, s: (0, 0)),
            scratch_shapes=[
                pltpu.VMEM((HEAD_DIM, TREE_TOK), bf16),
                pltpu.VMEM((TREE_TOK, HEAD_DIM), f32),
                pltpu.VMEM((TREE_TOK, HEAD_DIM), f32),
                pltpu.VMEM((TREE_TOK, GROUP * HEAD_DIM), bf16),
            ],
        ),
        out_shape=out_shape,
        compiler_params=params(),
        cost_estimate=cost(
            kv * 2.2e6 * 2 * GROUP * 640 * 2, nbytes([qkv, attended, grads, qkv])
        ),
    )(parents, qkv, qkv, qkv, attended, grads, logs)


def weight_gradient(lefts, rights, half, cut=None):
    pairs = len(lefts)
    rows, depth = lefts[0].shape
    quarters, _, width = rights[0].shape
    size = depth // 2
    if cut is None:
        tw = width // 2 if width > 1024 else width
        parts, first = width // tw, 0
    else:
        width = tw = width // 2
        parts, first = 1, cut

    def kernel(*refs):
        left_refs, right_refs = refs[:pairs], refs[pairs : 2 * pairs]
        out_ref, left_s, right_s = refs[2 * pairs :]

        @pl.when(pl.program_id(0) == 0)
        def _():
            for i, ref in enumerate(left_refs):
                left_s[i * rows : (i + 1) * rows] = ref[...]

        for i, ref in enumerate(right_refs):
            right_s[i * rows : (i + 1) * rows] = ref[...]
        out_ref[...] = contract_rows(left_s[...], right_s[...]).astype(bf16)

    out_shape = jax.ShapeDtypeStruct((size, quarters * width), bf16)
    arrays = list(lefts) + list(rights)
    return pl.pallas_call(
        kernel,
        grid=(quarters * parts,),
        in_specs=[pl.BlockSpec((rows, size), lambda t: (0, half))] * pairs
        + [pl.BlockSpec((None, rows, tw), lambda t: (t // parts, 0, first + t % parts))] * pairs,
        out_specs=pl.BlockSpec((size, tw), lambda t: (0, t)),
        out_shape=out_shape,
        scratch_shapes=[
            pltpu.VMEM((pairs * rows, size), bf16),
            pltpu.VMEM((pairs * rows, tw), bf16),
        ],
        compiler_params=params(),
        cost_estimate=cost(
            2 * pairs * rows * size * quarters * width, nbytes(arrays) + nbytes([out_shape])
        ),
    )(*arrays)


def flipped(index, mask):
    bit = 1
    while bit <= mask:
        if mask & bit:
            index = index + bit * (1 - 2 * lax.rem(lax.div(index, bit), 2))
        bit *= 2
    return index


def transfer_call(
    program, m, n, ins, outs, scratch, count, locals_, number, vmem_ins=(), aliases=None
):
    n_in, n_out, n_scratch = len(ins), len(outs), len(scratch)

    class Mover:
        def __init__(self, send, recv, own):
            self.send, self.recv, self.own = send, recv, own
            self.made, self.local = [], []

        def start(self, source, target, axis, mask):
            k = len(self.made)
            place = flipped(lax.axis_index(axis), mask)
            copy = pltpu.make_async_remote_copy(
                src_ref=source,
                dst_ref=target,
                send_sem=self.send.at[k],
                recv_sem=self.recv.at[k],
                device_id={axis: place},
                device_id_type=pl.DeviceIdType.MESH,
            )
            copy.start()
            self.made.append(copy)
            return copy

        def keep(self, source, target):
            copy = pltpu.make_async_copy(source, target, self.own.at[len(self.local)])
            copy.start()
            self.local.append(copy)
            return copy

    def kernel(*refs):
        in_refs, out_refs = refs[:n_in], refs[n_in : n_in + n_out]
        rest = refs[n_in + n_out :]
        mover = Mover(*rest[n_scratch:])
        barrier = pltpu.get_barrier_semaphore()
        partners = [("wide", k) for k in range(1, m)] if m != 8 else [
            ("wide", k) for k in (1, 2, 4)
        ]
        partners += [("tp", e) for e in range(1, n)]
        for axis, mask in partners:
            pl.semaphore_signal(
                barrier,
                inc=1,
                device_id={axis: flipped(lax.axis_index(axis), mask)},
                device_id_type=pl.DeviceIdType.MESH,
            )
        pl.semaphore_wait(barrier, len(partners))
        program(mover, in_refs, out_refs, rest[:n_scratch])
        for copy in mover.made:
            copy.wait_send()

    return pl.pallas_call(
        kernel,
        in_specs=[
            pl.BlockSpec(memory_space=pltpu.VMEM if i in vmem_ins else pl.ANY) for i in range(n_in)
        ],
        out_specs=[pl.BlockSpec(memory_space=pl.ANY)] * n_out,
        out_shape=outs,
        scratch_shapes=list(scratch)
        + [
            pltpu.SemaphoreType.DMA((count,)),
            pltpu.SemaphoreType.DMA((count,)),
            pltpu.SemaphoreType.DMA((locals_,)),
        ],
        input_output_aliases=aliases or {},
        compiler_params=pltpu.CompilerParams(
            collective_id=number, has_side_effects=True, vmem_limit_bytes=VMEM
        ),
        cost_estimate=cost(0, 1e6),
    )(*ins)


def swap_own(source, target, mine, sems):
    seat = lax.axis_index("tp")
    return (
        pltpu.make_async_copy(source.at[seat], mine, sems.at[0]),
        pltpu.make_async_copy(mine, target.at[seat], sems.at[1]),
    )


def gradient_pair(lefts, rights, cut, number, ride=None):
    pairs = len(lefts)
    rows, depth = lefts[0].shape
    quarters, _, width = rights[0].shape
    size = depth // 2
    block = size // 4
    half = block // 2
    if cut is None:
        tw = width // 2 if width > 1024 else width
        parts, first = width // tw, 0
    else:
        width = tw = width // 2
        parts, first = 1, cut
    steps = quarters * parts
    n = ride.shape[0] if ride is not None else 1
    rides = [] if ride is None else [ride]

    def kernel(*refs):
        left_refs, right_refs = refs[:pairs], refs[pairs : 2 * pairs]
        at = 2 * pairs
        ride_in = refs[at : at + len(rides)]
        at += len(rides)
        own_ref, x_ref, y_ref, top_ref, low_ref = refs[at : at + 5]
        at += 5
        ride_out = refs[at : at + len(rides)]
        at += len(rides)
        left_s, right_s, sent, came, send_sems, recv_sems = refs[at : at + 6]
        extra = refs[at + 6 :]
        step = pl.program_id(0)
        other_core = {"wide": flipped(lax.axis_index("wide"), 1)}

        def copy(k):
            return pltpu.make_async_remote_copy(
                src_ref=sent.at[k],
                dst_ref=came.at[k],
                send_sem=send_sems.at[k],
                recv_sem=recv_sems.at[k],
                device_id=other_core,
                device_id_type=pl.DeviceIdType.MESH,
            )

        def ride_copies():
            mine, ride_send, ride_recv, own_sems = extra
            seat = lax.axis_index("tp")
            return [
                pltpu.make_async_remote_copy(
                    src_ref=ride_in[0].at[flipped(seat, e)],
                    dst_ref=ride_out[0].at[seat],
                    send_sem=ride_send.at[e - 1],
                    recv_sem=ride_recv.at[e - 1],
                    device_id={"tp": flipped(seat, e)},
                    device_id_type=pl.DeviceIdType.MESH,
                )
                for e in range(1, n)
            ], swap_own(ride_in[0], ride_out[0], mine, own_sems)

        @pl.when(step == 0)
        def _():
            barrier = pltpu.get_barrier_semaphore()
            partners = [other_core] + [
                {"tp": flipped(lax.axis_index("tp"), e)} for e in range(1, n)
            ]
            for partner in partners:
                pl.semaphore_signal(
                    barrier, inc=1, device_id=partner, device_id_type=pl.DeviceIdType.MESH
                )
            pl.semaphore_wait(barrier, len(partners))
            if rides:
                sends, (load, keep) = ride_copies()
                for c in sends:
                    c.start()
                load.start()
                load.wait()
                keep.start()

        @pl.when(lax.rem(step, steps) == 0)
        def _():
            for i, ref in enumerate(left_refs):
                left_s[i * rows : (i + 1) * rows] = ref[...]

        for i, ref in enumerate(right_refs):
            right_s[i * rows : (i + 1) * rows] = ref[...]
        product = contract_rows(left_s[...], right_s[...])

        @pl.when(step < steps)
        def _():
            sent[step] = product.astype(bf16)
            copy(step).start()

        @pl.when(step >= steps)
        def _():
            k = step - steps
            copy(k).wait_recv()
            total = (product + came[k].astype(f32)).astype(bf16)
            own_ref[...] = total[:block]
            x_ref[...] = total[block : 2 * block]
            y_ref[...] = total[2 * block : 3 * block]
            top_ref[...] = total[3 * block : 3 * block + half]
            low_ref[...] = total[3 * block + half :]

        @pl.when(step == 2 * steps - 1)
        def _():
            for k in range(steps):
                copy(k).wait_send()
            if rides:
                sends, own_row = ride_copies()
                for c in sends:
                    c.wait_send()
                    c.wait_recv()
                own_row[1].wait()

    columns = quarters * width
    heights = (block, block, block, half, half)
    out_shape = [struct(h, columns) for h in heights]
    arrays = list(lefts) + list(rights)
    late = lambda t: (0, jnp.maximum(t - steps, 0))
    ride_scratch = (
        []
        if ride is None
        else [
            pltpu.VMEM(ride.shape[1:], bf16),
            pltpu.SemaphoreType.DMA((n - 1,)),
            pltpu.SemaphoreType.DMA((n - 1,)),
            pltpu.SemaphoreType.DMA((2,)),
        ]
    )

    def right_map(t):
        t = lax.rem(t, steps)
        return (lax.div(t, parts), 0, first + lax.rem(t, parts))

    result = pl.pallas_call(
        kernel,
        grid=(2 * steps,),
        in_specs=[pl.BlockSpec((rows, size), lambda t: (0, 1 - lax.div(t, steps)))] * pairs
        + [pl.BlockSpec((None, rows, tw), right_map)] * pairs
        + [pl.BlockSpec(memory_space=pl.ANY)] * len(rides),
        out_specs=[pl.BlockSpec((h, tw), late) for h in heights]
        + [pl.BlockSpec(memory_space=pl.ANY)] * len(rides),
        out_shape=out_shape + [struct(*r.shape) for r in rides],
        scratch_shapes=[
            pltpu.VMEM((pairs * rows, size), bf16),
            pltpu.VMEM((pairs * rows, tw), bf16),
            pltpu.VMEM((steps, size, tw), bf16),
            pltpu.VMEM((steps, size, tw), bf16),
            pltpu.SemaphoreType.DMA((steps,)),
            pltpu.SemaphoreType.DMA((steps,)),
        ]
        + ride_scratch,
        compiler_params=pltpu.CompilerParams(
            collective_id=number, has_side_effects=True, vmem_limit_bytes=VMEM
        ),
        cost_estimate=cost(
            4 * pairs * rows * size * columns, nbytes(arrays) + nbytes(out_shape)
        ),
    )(*arrays, *rides)
    return (result[:5], result[5]) if rides else (result, None)


def waves_start(mover, n, source, target):
    if n != 4:
        return [mover.start(source, target(e), "tp", e) for e in range(1, n)]
    far = mover.start(source, target(2), "tp", 2)
    near = mover.start(source, target(1), "tp", 1)
    return [near, far]


def waves_forward(mover, n, waves, target):
    if n != 4:
        return waves
    waves[1].wait_recv()
    return waves + [mover.start(target(2), target(3), "tp", 1)]


def struct(*shape):
    return jax.ShapeDtypeStruct(shape, bf16)


class Spread:
    def __init__(self, mover, m, source, target, block):
        self.mover, self.m, self.source, self.block = mover, m, source, block
        self.at = lambda start, size: target(pl.ds(start, size))

    def first(self):
        go, block, source = self.mover.start, self.block, self.source
        if self.m != 8:
            self.all = [
                go(source, self.at(k * block, block), "wide", k) for k in range(1, self.m)
            ]
            return
        self.x = go(source, self.at(block, block), "wide", 2)
        self.y = go(source, self.at(2 * block, block), "wide", 4)
        self.cores = [go(source, self.at(4 * block, block), "wide", 1)]

    def second(self):
        if self.m != 8:
            return
        go, block = self.mover.start, self.block
        half = block // 2
        self.x.wait_recv()
        low = self.at(block + half, half)
        self.low = go(low, self.at(3 * block + half, half), "wide", 4)
        self.cores.append(go(self.at(block, block), self.at(5 * block, block), "wide", 1))
        self.y.wait_recv()
        top = self.at(2 * block, half)
        self.top = go(top, self.at(3 * block, half), "wide", 2)
        self.cores.append(go(self.at(2 * block, block), self.at(6 * block, block), "wide", 1))

    def third(self):
        if self.m != 8:
            return
        go, block = self.mover.start, self.block
        self.low.wait_recv()
        self.top.wait_recv()
        self.cores.append(go(self.at(3 * block, block), self.at(7 * block, block), "wide", 1))

    def last(self):
        for copy in self.all if self.m != 8 else self.cores:
            copy.wait_recv()


def exclusive_or(a, b, count):
    total, bit = 0, 1
    while bit < count:
        total = total + bit * lax.rem(lax.div(a, bit) + lax.div(b, bit), 2)
        bit *= 2
    return total


def gather_front(
    m, n, order, qkv_block, in_block, down_block, gain_block, tokens, out_grad, cosine, sine
):
    block, qw = qkv_block.shape
    fw, dw = in_block.shape[1], down_block.shape[1]
    depth = block * m
    pairs = n // 2
    rows_in = tokens.shape[0]
    tw = qw // 2
    gain_width = gain_block.shape[1]
    chunks = 2 if rows_in % 32 == 0 else 1
    chunk = rows_in // chunks

    def program(mover, ins, outs, scratch):
        qkv, inner, down, gain, x_ref, dy_ref, cos_ref, sin_ref = ins
        (
            weights, in_own, in_rest, down_rest, gains,
            x_out, dy_out, normed_out, hats, raws,
        ) = outs
        gain_s, normed_s, tile_s, hat_s, raw_s, tile_sems, hat_sems, raw_sems = scratch
        where, seat = lax.axis_index("wide"), lax.axis_index("tp")
        rows = pl.ds(0, block)
        place = lambda e: weights.at[e, rows]
        waves = waves_start(mover, n, qkv, place)
        spread_gains = Spread(mover, m, gain, lambda r: gains.at[r], GAIN_ROWS)
        spread_gains.first()
        spreads = [
            Spread(mover, m, qkv if q == 0 else place(q), lambda r, q=q: weights.at[q, r], block)
            for q in range(n)
        ]
        spreads[0].first()
        kept = [
            mover.keep(qkv, weights.at[0, rows]),
            mover.keep(inner, in_own.at[0, rows]),
        ]
        kept_gain = mover.keep(gain, gains.at[pl.ds(0, GAIN_ROWS)])
        spread_gains.second()
        spreads[0].second()
        spread_gains.third()
        spreads[0].third()
        columns = [
            pl.ds(pl.multiple_of(flipped(where, k) * block, 128), block) for k in order
        ]
        for k in range(m):
            cut = pl.ds(k * block, block)
            kept.append(mover.keep(x_ref.at[:, columns[k]], x_out.at[:, cut]))
            kept.append(mover.keep(dy_ref.at[:, columns[k]], dy_out.at[:, cut]))
        if n == 4:
            waves = waves_forward(mover, n, waves, place)
            spreads[2].first()
            waves[0].wait_recv()
            spreads[1].first()
            waves[2].wait_recv()
            spreads[3].first()
        else:
            for q in range(1, n):
                waves[q - 1].wait_recv()
                spreads[q].first()
        late = []
        for e in range(1, pairs):
            late.append(mover.start(inner, in_rest.at[e - 1, rows], "tp", 2 * e))
            late.append(mover.start(down, down_rest.at[e - 1, rows], "tp", 2 * e))

        spread_gains.last()
        kept_gain.wait()
        load = mover.keep(gains, gain_s)
        load.wait()

        def normalise(i, carry):
            part = pl.ds(pl.multiple_of(i * chunk, 16), chunk)
            x = x_ref[part, :].astype(f32)
            inverse = lax.rsqrt(jnp.mean(x * x, axis=-1, keepdims=True) + norm_eps)
            for k in range(m):
                piece = x_ref[part, columns[k]].astype(f32) * inverse
                scale = gain_s[k * GAIN_ROWS : k * GAIN_ROWS + 1, :block]
                normed_s[part, k * block : (k + 1) * block] = (piece * scale).astype(bf16)
            return carry

        lax.fori_loop(0, chunks, normalise, 0)
        kept.append(mover.keep(normed_s, normed_out))
        heads_at = 2 * block

        def head_gain(at):
            total = gain_s[0:1, at : at + HEAD_DIM]
            for k in range(1, m):
                total = total + gain_s[k * GAIN_ROWS : k * GAIN_ROWS + 1, at : at + HEAD_DIM]
            return total

        gain_q, gain_k = head_gain(heads_at), head_gain(heads_at + HEAD_DIM)

        turn = (2, 1, 3) if n == 4 else range(1, n)
        for q in turn:
            spreads[q].second()
        own = Spread(mover, m, inner, lambda r: in_own.at[0, r], block)
        own.first()
        for q in turn:
            spreads[q].third()
        for spread in spreads:
            spread.last()
        kept[0].wait()

        def fetch(q, part):
            return pltpu.make_async_copy(
                weights.at[q, :, pl.ds(part * tw, tw)], tile_s.at[part], tile_sems.at[part]
            )

        def leave(q, part):
            home = exclusive_or(seat, q, n)
            cut = pl.ds(part * tw, tw)
            return (
                pltpu.make_async_copy(
                    hat_s.at[part], hats.at[home, :, cut], hat_sems.at[part]
                ),
                pltpu.make_async_copy(
                    raw_s.at[part], raws.at[home, :, cut], raw_sems.at[part]
                ),
            )

        def turned(x, gain):
            inverse = lax.rsqrt(jnp.mean(x * x, axis=-1, keepdims=True) + norm_eps)
            u = x * inverse * gain
            return u * cos_ref[...] + pltpu.roll(u, HEAD_DIM // 2, 1) * sin_ref[...]

        def quarter(q, carry):
            for part in range(2):
                if part == 0:
                    fetch(q, 1).start()
                else:

                    @pl.when(q + 1 < n)
                    def _():
                        fetch(q + 1, 0).start()

                fetch(q, part).wait()

                @pl.when(q > 0)
                def _(part=part):
                    for c in leave(q, part):
                        c.wait()

                acc = dot_nn(normed_s[...], tile_s[part])
                raw_s[part] = acc.astype(bf16)
                if part == 0:
                    for cut in head_slices(tw):
                        hat_s[0, :, cut] = turned(acc[:, cut], gain_q).astype(bf16)
                else:
                    for cut in head_slices(tw // 2):
                        hat_s[1, :, cut] = (turned(acc[:, cut], gain_k) * key_scale).astype(bf16)
                    hat_s[1, :, tw // 2 :] = acc[:, tw // 2 :].astype(bf16)
                for c in leave(q, part):
                    c.start()
            return carry

        fetch(0, 0).start()
        lax.fori_loop(0, n // 2, quarter, 0)
        own.second()
        lax.fori_loop(n // 2, n, quarter, 0)
        own.third()
        for part in range(2):
            for c in leave(n - 1, part):
                c.wait()
        own.last()
        for copy in late:
            copy.wait_recv()
        for copy in kept[1:]:
            copy.wait()

    per = 8 if m == 8 else m - 1
    return transfer_call(
        program,
        m,
        n,
        [qkv_block, in_block, down_block, gain_block, tokens, out_grad, cosine, sine],
        [
            struct(n, depth, qw),
            struct(1, depth, fw),
            struct(pairs - 1, depth, fw),
            struct(pairs - 1, depth, dw),
            jax.ShapeDtypeStruct((m * GAIN_ROWS, gain_width), f32),
            struct(rows_in, depth),
            struct(rows_in, depth),
            struct(rows_in, depth),
            struct(n, rows_in, qw),
            struct(n, rows_in, qw),
        ],
        [
            pltpu.VMEM((m * GAIN_ROWS, gain_width), f32),
            pltpu.VMEM((rows_in, depth), bf16),
            pltpu.VMEM((2, depth, tw), bf16),
            pltpu.VMEM((2, rows_in, tw), bf16),
            pltpu.VMEM((2, rows_in, tw), bf16),
            pltpu.SemaphoreType.DMA((2,)),
            pltpu.SemaphoreType.DMA((2,)),
            pltpu.SemaphoreType.DMA((2,)),
        ],
        (n - 1) + per * (n + 2) + 2 * (pairs - 1),
        5 + 2 * m,
        1,
        vmem_ins=tuple(range(8)),
    )


def swap_heads(mover, n, mine, source, target):
    seat = lax.axis_index("tp")
    load = mover.keep(source.at[seat], mine)
    sends = [
        mover.start(source.at[flipped(seat, e)], target.at[seat], "tp", e) for e in range(1, n)
    ]
    load.wait()
    return sends, mover.keep(mine, target.at[seat])


def gather_middle(m, n, hats, in_rest, out_block, down_block):
    quarters, rows, width = hats.shape
    pairs, depth, fw = in_rest.shape
    block, ow = out_block.shape
    dw = down_block.shape[1]

    def program(mover, ins, outs, scratch):
        hat, _, out, down = ins
        heads, rest, weights, down_own = outs
        first = pl.ds(0, block)
        kept = [mover.keep(out, weights.at[0, first]), mover.keep(down, down_own.at[0, first])]
        place = lambda e: weights.at[e, first]
        waves = waves_start(mover, n, out, place)
        spreads = [
            Spread(mover, m, rest.at[p, first], lambda r, p=p: rest.at[p, r], block)
            for p in range(pairs)
        ]
        for spread in spreads:
            spread.first()
        waves = waves_forward(mover, n, waves, place)
        for copy in waves if n != 4 else (waves[0], waves[2]):
            copy.wait_recv()
        sends, own_row = swap_heads(mover, n, scratch[0], hat, heads)
        kept[0].wait()
        for spread in spreads:
            spread.second()
        quarter = Spread(mover, m, weights.at[:, first], lambda r: weights.at[:, r], block)
        quarter.first()
        for spread in spreads:
            spread.third()
        quarter.second()
        own = Spread(mover, m, down, lambda r: down_own.at[0, r], block)
        own.first()
        quarter.third()
        own.second()
        own.third()
        for spread in spreads + [own, quarter]:
            spread.last()
        for copy in sends:
            copy.wait_recv()
        kept[1].wait()
        own_row.wait()

    per = 8 if m == 8 else m - 1
    return transfer_call(
        program,
        m,
        n,
        [hats, in_rest, out_block, down_block],
        [
            struct(n, rows, width),
            struct(pairs, depth, fw),
            struct(n, depth, ow),
            struct(1, depth, dw),
        ],
        [pltpu.VMEM((rows, width), bf16)],
        2 * (n - 1) + per * (pairs + 2),
        4,
        2,
        vmem_ins=(2, 3),
        aliases={1: 1},
    )


def gather_late(m, n, heads, down_rest):
    quarters, rows, width = heads.shape
    pairs, depth, dw = down_rest.shape
    block = depth // m

    def program(mover, ins, outs, scratch):
        source, _ = ins
        target, rest = outs
        first = pl.ds(0, block)
        sends, own_row = swap_heads(mover, n, scratch[0], source, target)
        spreads = [
            Spread(mover, m, rest.at[p, first], lambda r, p=p: rest.at[p, r], block)
            for p in range(pairs)
        ]
        for stage in ("first", "second", "third", "last"):
            for spread in spreads:
                getattr(spread, stage)()
        for copy in sends:
            copy.wait_recv()
        own_row.wait()

    per = 8 if m == 8 else m - 1
    return transfer_call(
        program,
        m,
        n,
        [heads, down_rest],
        [struct(n, rows, width), struct(pairs, depth, dw)],
        [pltpu.VMEM((rows, width), bf16)],
        (n - 1) + per * pairs,
        2,
        3,
        aliases={1: 1},
    )


def shuffle_columns(a, order):
    rows, count = a.shape[0], order.shape[0]
    width = a.shape[1] // count

    def kernel(order_ref, in_ref, out_ref):
        out_ref[...] = in_ref[...]

    return pl.pallas_call(
        kernel,
        grid_spec=pltpu.PrefetchScalarGridSpec(
            num_scalar_prefetch=1,
            grid=(count,),
            in_specs=[pl.BlockSpec((rows, width), lambda k, s: (0, s[k]))],
            out_specs=pl.BlockSpec((rows, width), lambda k, s: (0, k)),
        ),
        out_shape=jax.ShapeDtypeStruct(a.shape, a.dtype),
        cost_estimate=cost(0, 2 * nbytes([a])),
    )(order, a)


def inverse_rms(values):
    return lax.rsqrt(jnp.mean(values * values, axis=-1, keepdims=True) + norm_eps)


def norm_back(grads, unit_values, inverse, gain):
    scaled = grads * gain
    return inverse * (scaled - unit_values * jnp.mean(scaled * unit_values, axis=-1, keepdims=True))


def after(values, *conditions):
    return lax.optimization_barrier((values, conditions))[0]


class Job:
    def __init__(self, stages):
        self.stages = stages
        self.result = None
        self.started, self.pending = next(stages)

    def advance(self, came):
        try:
            self.started, self.pending = self.stages.send(came)
        except StopIteration as stop:
            self.result = stop.value
            self.pending = None

    def finish(self):
        while self.result is None:
            self.advance(self.pending)
        return self.result


def tick(values, *jobs):
    jobs = [j for j in jobs if j.result is None]
    values, came = lax.optimization_barrier((values, [j.pending for j in jobs]))
    for j, c in zip(jobs, came):
        j.advance(c)
    return values


def local(
    m,
    n,
    tokens,
    out_grad,
    seg_ids,
    parent_table,
    path_pos,
    attn_gain,
    w_query,
    w_key,
    w_value,
    w_out,
    q_gain,
    k_gain,
    ffn_gain,
    w_gate,
    w_up,
    w_down,
):
    rows, depth = tokens.shape
    block = depth // m
    order = [0, 2, 4, 6, 1, 3, 5, 7] if m == 8 else list(range(m))
    where = lax.axis_index("wide").astype(jnp.int32)
    seat = lax.axis_index("tp").astype(jnp.int32)
    relative = jnp.asarray(order, jnp.int32) ^ where
    inverse_order = [order.index(k) for k in range(m)]
    absolute = jnp.take(jnp.asarray(inverse_order, jnp.int32), jnp.arange(m, dtype=jnp.int32) ^ where)
    seats = jnp.arange(n, dtype=jnp.int32) ^ seat
    plain = jnp.arange(n, dtype=jnp.int32)

    def over(axis, a, mask):
        size = m if axis == "wide" else n
        return lax.ppermute(a, axis, [(i, i ^ mask) for i in range(size)])

    def scatter(lefts, rights, cut, number, ride=None, rode=None):
        if m != 8:
            if ride is not None:
                rode.append(swap(ride))
            other = weight_gradient(lefts, rights, 1, cut)
            mine = weight_gradient(lefts, rights, 0, cut)
            both = jnp.concatenate([mine, other])
            got = yield both, [over("wide", both[k * block : (k + 1) * block], k) for k in range(1, m)]
            return sum((g.astype(f32) for g in got), both[:block].astype(f32))
        (own, x, y, top_sent, low_sent), came = gradient_pair(lefts, rights, cut, number, ride)
        if ride is not None:
            rode.append(came)
        half = block // 2
        top, low = yield (top_sent, low_sent), [over("wide", top_sent, 2), over("wide", low_sent, 4)]
        for_x = jnp.concatenate([x[:half], (x[half:].astype(f32) + low.astype(f32)).astype(bf16)])
        for_y = jnp.concatenate([(y[:half].astype(f32) + top.astype(f32)).astype(bf16), y[half:]])
        from_x, from_y = yield [for_x, for_y], [over("wide", for_x, 2), over("wide", for_y, 4)]
        return own.astype(f32) + from_x.astype(f32) + from_y.astype(f32)

    def ffn_share(left, rights, number, ride=None, rode=None):
        total = yield from scatter(left, rights, None, number, ride, rode)
        parts = [total[:, e * fcols : (e + 1) * fcols].astype(bf16) for e in range(1, n // 2)]
        sent = yield parts, [over("tp", p, 2 * (e + 1)) for e, p in enumerate(parts)]
        return sum((x.astype(f32) for x in sent), total[:, :fcols])

    def swap(a):
        return lax.all_to_all(a, "tp", split_axis=0, concat_axis=0, tiled=True)

    def attn_share(left, right, cut, number):
        total = yield from scatter([left], [right], cut, number)
        parts = total.astype(bf16).reshape(block, n, -1).transpose(1, 0, 2)
        (came,) = yield parts, [swap(parts)]
        return jnp.sum(came.astype(f32), axis=0)

    qkv_block = jnp.concatenate([w_query, w_key, w_value], axis=1)
    out_block = w_out.T
    in_block = jnp.concatenate([w_gate, w_up], axis=1)
    down_block = w_down.T
    aw = w_query.shape[1]
    kv = w_key.shape[1] // HEAD_DIM
    fcols = w_gate.shape[1]
    fw = fcols // 3

    small = q_gain.shape[0]
    head_row = lambda g: lax.dynamic_update_slice(
        jnp.zeros((HEAD_DIM,), f32), g.astype(f32), (where * small,)
    )
    gain_row = jnp.concatenate(
        [attn_gain.astype(f32), ffn_gain.astype(f32), head_row(q_gain), head_row(k_gain)]
    )[None]
    gain_block = jnp.pad(gain_row, ((0, GAIN_ROWS - 1), (0, 0)))
    base = where * parent_table.shape[0]
    block_segs = seg_ids[TRUNK::BRANCH] - base
    hit = block_segs[:, None] == jnp.arange(parent_table.shape[0], dtype=jnp.int32)[None, :]
    block_parents = jnp.sum(jnp.where(hit, parent_table[None, :] - base, 0), axis=1)
    match = block_parents[:, None] == block_segs[None, :]
    number = TRUNK_BLOCKS + jnp.arange(FORKS2, dtype=jnp.int32)
    parents = jnp.where(
        jnp.any(match, axis=1), jnp.sum(jnp.where(match, number[None, :], 0), axis=1), number
    ).astype(jnp.int32)

    own_pos = lax.dynamic_slice_in_dim(path_pos, seat * rows, rows, 0).astype(f32)
    frequency = rope_base ** (-(jnp.arange(HEAD_DIM // 2, dtype=f32) * 2.0) / HEAD_DIM)
    angles = own_pos[:, None] * frequency[None, :]
    cosine, sine = jnp.cos(angles), jnp.sin(angles)
    cosine = jnp.concatenate([cosine, cosine], axis=-1)
    sine = jnp.concatenate([-sine, sine], axis=-1)

    (
        qkv_all, in_own, in_rest, down_rest, gains, stream_low, cotangent, normed_one, hats, raws,
    ) = gather_front(
        m, n, order, qkv_block, in_block, down_block, gain_block, tokens, out_grad, cosine, sine
    )
    gains = gains[::GAIN_ROWS]
    gain_one = gains[:, :block].reshape(1, depth)
    gain_two = gains[:, block : 2 * block].reshape(1, depth)
    gain_q = jnp.sum(gains[:, 2 * block : 2 * block + HEAD_DIM], axis=0, keepdims=True)
    gain_k = jnp.sum(gains[:, 2 * block + HEAD_DIM :], axis=0, keepdims=True)
    qkv_tiles = Tiles([qkv_all], 2, 0, aw)
    qkv, in_rest, out_all, down_own = gather_middle(m, n, hats, in_rest, out_block, down_block)
    qkv = qkv.reshape(n * rows, -1)
    attended_heads, logs = attention_forward(qkv, parents, kv)
    attended, down_rest = gather_late(m, n, attended_heads.reshape(n, rows, -1), down_rest)
    out_tiles = Tiles([out_all], 1, 0, aw)
    after_attn, normed_two = project_residual(attended, out_tiles, seats, stream_low, gain_two)

    normed_two_next = over("tp", normed_two, 1)

    gate_tiles = Tiles([in_own, in_rest], 3, 0, fw)
    up_tiles = Tiles([in_own, in_rest], 3, 3, fw)
    down_tiles = Tiles([down_own, down_rest], 3, 0, fw)

    hidden, gate, up = feed_forward(normed_two, gate_tiles, up_tiles, plain)
    down = project_columns([hidden], [down_tiles], plain, depth, f32)
    normed_two_next, cotangent_sent = after((normed_two_next, cotangent), (down, normed_two_next))
    cotangent_next = over("tp", cotangent_sent, 1)
    hidden_next, gate_next, up_next = feed_forward(normed_two_next, gate_tiles, up_tiles, plain)
    down_part = project_columns([hidden_next], [down_tiles], plain, depth, bf16)
    own_grad = after(cotangent, down_part)
    gate_grad, up_grad = feed_back(own_grad, gate, up, down_tiles, plain)
    cotangent_next, hidden_late = after((cotangent_next, hidden), gate_grad)
    down_job = Job(ffn_share([cotangent, cotangent_next], [hidden_late, hidden_next], 4))
    cotangent_next, down_sent = after((cotangent_next, down_part), down_job.started)
    down_next = over("tp", down_sent, 1)
    gate_grad_next, up_grad_next = feed_back(
        cotangent_next, gate_next, up_next, down_tiles, plain
    )
    gate_late, up_late = tick((gate_grad_next, up_grad_next), down_job)
    gate_late, up_late = after((gate_late, up_late), down_job.started)
    back_part = project_columns([gate_late, up_late], [gate_tiles, up_tiles], plain, depth, bf16)
    back_part, down_next = after((back_part, down_next), back_part)
    back_next = over("tp", back_part, 1)
    gate_grad, up_grad = after((gate_grad, up_grad), back_part)
    gate_job = Job(ffn_share([normed_two, normed_two_next], [gate_grad, gate_grad_next], 5))
    gate_late, up_late = after((gate_grad, up_grad), gate_job.started)
    gate_late, up_late = tick((gate_late, up_late), down_job)
    gate_late, up_late = after((gate_late, up_late), down_job.started)
    back = project_columns([gate_late, up_late], [gate_tiles, up_tiles], plain, depth, f32)
    back, back_next = after((back, back_next), back)
    back = tick(back, gate_job)
    back = after(back, gate_job.started)
    normed_two_grad = back + back_next.astype(f32)
    inverse_two = inverse_rms(after(after_attn, normed_two_next))
    unit_two = after_attn * inverse_two

    ffn_gain_part = jnp.sum(normed_two_grad * unit_two, axis=0)
    stream_grad = cotangent.astype(f32) + norm_back(
        normed_two_grad, unit_two, inverse_two, gain_two
    )
    grad_low = stream_grad.astype(bf16)
    attended_grad = tick(project_rows(grad_low, out_tiles, seats), down_job)
    lefts, up_grads = after(
        ([normed_two, normed_two_next], [up_grad, up_grad_next]), attended_grad
    )
    rode = []
    up_job = Job(ffn_share(lefts, up_grads, 6, attended_grad, rode))
    grad_heads = after(rode[0].reshape(n * rows, -1), up_job.started)
    grad_heads = tick(grad_heads, gate_job)
    grad_heads = after(grad_heads, gate_job.started)
    back_hats = attention_backward(qkv, attended_heads, grad_heads, logs, parents, kv)
    back_hats = tick(back_hats, gate_job, up_job)
    back_hats = after(back_hats, up_job.started)
    back_hats_own = swap(back_hats.reshape(n, rows, -1))
    grad_low, down_next, after_attn = after((grad_low, down_next, after_attn), back_hats)
    out_job = Job(attn_share(grad_low, attended, None, 7))
    fence = tick(after(grad_low, out_job.started), up_job)
    mixed = (after_attn + down + down_next.astype(f32)).astype(bf16)
    mixed = shuffle_columns(mixed, absolute)
    inverse_one = inverse_rms(after(stream_low, back_hats).astype(f32))
    back_hats_own, inverse_one, mixed = after(
        (back_hats_own, inverse_one, mixed), fence, out_job.started
    )
    raw_grads, q_sum, k_sum = qkv_back(back_hats_own, raws, cosine, sine, gain_q, gain_k)
    raw_grads = tick(raw_grads, out_job)
    q_job = Job(attn_share(normed_one, after(raw_grads, out_job.started), 0, 8))
    raw_late = after(raw_grads, q_job.started)
    k_job = Job(attn_share(normed_one, raw_late, 1, 9))
    raw_late = tick(after(raw_late, k_job.started), q_job, out_job, up_job)
    raw_late = after(raw_late, q_job.started)
    normed_one_grad = project_columns([raw_late], [qkv_tiles], seats, depth, f32)
    normed_one_grad = tick(normed_one_grad, q_job, k_job, up_job, out_job)
    normed_one_grad = after(normed_one_grad, q_job.started, k_job.started)
    unit_one = stream_low.astype(f32) * inverse_one
    attn_gain_part = jnp.sum(normed_one_grad * unit_one, axis=0)
    tokens_grad = (
        stream_grad + norm_back(normed_one_grad, unit_one, inverse_one, gain_one)
    ).astype(bf16)
    tokens_grad = shuffle_columns(tokens_grad, absolute)

    parts = jnp.concatenate(
        [
            attn_gain_part.reshape(m, block),
            ffn_gain_part.reshape(m, block),
            jnp.take(q_sum.reshape(m, small), relative, axis=0),
            jnp.take(k_sum.reshape(m, small), relative, axis=0),
        ],
        axis=1,
    )
    size = m
    while size > 1:
        size //= 2
        parts = parts[:size] + over("wide", parts[size:], order[size])
    step = 1
    while step < n:
        parts = parts + over("tp", parts, step)
        step *= 2
    sums = parts[0]
    gate_share, up_share = gate_job.finish(), up_job.finish()
    down_share, out_share = down_job.finish().T, out_job.finish().T
    q_share, k_share = q_job.finish(), k_job.finish()
    return (
        mixed,
        tokens_grad,
        sums[:block],
        q_share,
        k_share[:, : aw // 2],
        k_share[:, aw // 2 :],
        out_share,
        sums[2 * block : 2 * block + small],
        sums[2 * block + small :],
        sums[block : 2 * block],
        gate_share,
        up_share,
        down_share,
    )


def solution(mesh):
    both = P(("wide", "tp"), None)
    w, wt, tw = P("wide"), P("wide", "tp"), P("tp", "wide")
    return jax.shard_map(
        functools.partial(local, mesh.shape["wide"], mesh.shape["tp"]),
        mesh=mesh,
        in_specs=(both, both, w, w, w, w, wt, wt, wt, tw, w, w, w, wt, wt, tw),
        out_specs=(both, both, w, wt, wt, wt, tw, w, w, w, wt, wt, tw),
        check_vma=False,
    )
```

```python
import functools
import math

import jax
import jax.numpy as jnp
from jax import lax
from jax.experimental import pallas as pl
from jax.experimental.pallas import tpu as pltpu
from jax.sharding import PartitionSpec as P

HEAD_DIM = 128
TRUNK = 1152
BRANCH = 128
FORKS2 = 8
TREE_TOK = 2176
GROUP = 2

norm_eps = 1e-06
rope_base = 1000000.0
score_scale = HEAD_DIM ** (-0.5)
key_scale = score_scale * math.log2(math.e)
LN2 = math.log(2.0)
VMEM = 52 * 1024 * 1024
COST = 0.01
GAIN_ROWS = 16

f32 = jnp.float32
bf16 = jnp.bfloat16


def dot_nn(a, b):
    return lax.dot_general(a, b, (((1,), (0,)), ((), ())), preferred_element_type=f32)


def dot_nt(a, b):
    return lax.dot_general(a, b, (((1,), (1,)), ((), ())), preferred_element_type=f32)


def contract_rows(a, b):
    return lax.dot_general(a, b, (((0,), (0,)), ((), ())), preferred_element_type=f32)


def params():
    return pltpu.CompilerParams(vmem_limit_bytes=VMEM)


def cost(flops, nbytes):
    return pl.CostEstimate(flops=int(flops * COST), bytes_accessed=int(nbytes * COST), transcendentals=0)


def nbytes(arrays):
    return sum(a.size * a.dtype.itemsize for a in arrays)


class Tiles:
    def __init__(self, arrays, parts, base, width):
        self.list = list(arrays)
        self.quarters = sum(a.shape[0] for a in self.list)
        self.depth = self.list[0].shape[1]
        self.parts, self.base, self.width = parts, base, width
        self.steps = self.quarters * parts

    def arrays(self):
        return self.list

    def scratch(self):
        return [pltpu.VMEM((2, self.depth, self.width), bf16), pltpu.SemaphoreType.DMA((2,))]

    def fetch(self, refs, buf, sems, step):
        slot = lax.rem(step, 2)
        quarter = lax.div(step, self.parts)
        part = step - quarter * self.parts
        col = pl.multiple_of((self.base + part) * self.width, 128)

        def begin(ref, at):
            pltpu.make_async_copy(
                ref.at[at, :, pl.ds(col, self.width)], buf.at[slot], sems.at[slot]
            ).start()

        split = self.list[0].shape[0]
        if len(refs) == 1:
            begin(refs[0], quarter)
        else:

            @pl.when(quarter < split)
            def _():
                begin(refs[0], quarter)

            @pl.when(quarter >= split)
            def _():
                begin(refs[1], quarter - split)

    def wait(self, refs, buf, sems, step):
        slot = lax.rem(step, 2)
        pltpu.make_async_copy(
            refs[0].at[0, :, pl.ds(0, self.width)], buf.at[slot], sems.at[slot]
        ).wait()
        return slot


def tiled_call(body, sets, seats, ins, in_specs, out_shape, out_specs, scratch, flops):
    steps = sets[0].steps
    counts = [len(s.arrays()) for s in sets]
    n_in, n_out = len(ins), len(out_shape)

    def kernel(seat_ref, *refs):
        at = 0
        piece_refs = []
        for c in counts:
            piece_refs.append(refs[at : at + c])
            at += c
        in_refs = refs[at : at + n_in]
        at += n_in
        out_refs = refs[at : at + n_out]
        at += n_out
        bufs = [(refs[at + 2 * i], refs[at + 2 * i + 1]) for i in range(len(sets))]
        own = refs[at + 2 * len(sets) :]
        step = pl.program_id(0)

        @pl.when(step == 0)
        def _():
            for s, p, (buf, sems) in zip(sets, piece_refs, bufs):
                s.fetch(p, buf, sems, step)

        @pl.when(step + 1 < steps)
        def _():
            for s, p, (buf, sems) in zip(sets, piece_refs, bufs):
                s.fetch(p, buf, sems, step + 1)

        tiles = []
        for s, p, (buf, sems) in zip(sets, piece_refs, bufs):
            slot = s.wait(p, buf, sems, step)
            tiles.append(buf.at[slot])
        body(step, tiles, in_refs, out_refs, own)

    weights = [a for s in sets for a in s.arrays()]
    return pl.pallas_call(
        kernel,
        grid_spec=pltpu.PrefetchScalarGridSpec(
            num_scalar_prefetch=1,
            grid=(steps,),
            in_specs=[pl.BlockSpec(memory_space=pl.ANY)] * len(weights) + in_specs,
            out_specs=out_specs,
            scratch_shapes=[x for s in sets for x in s.scratch()] + scratch,
        ),
        out_shape=out_shape,
        compiler_params=params(),
        cost_estimate=cost(flops, nbytes(weights) + nbytes(ins) + nbytes(out_shape)),
    )(seats, *weights, *ins)


def whole(array):
    return pl.BlockSpec(array.shape, lambda t, s: (0,) * len(array.shape))


def seated(rows, width, parts):
    return pl.BlockSpec(
        (None, rows, width),
        lambda t, s: (s[lax.div(t, parts)], 0, lax.rem(t, parts)),
    )


def head_slices(width):
    return [slice(h * HEAD_DIM, (h + 1) * HEAD_DIM) for h in range(width // HEAD_DIM)]


def project_rows(a, tiles, seats):
    rows, tw = a.shape[0], tiles.width

    def body(step, weights, ins, outs, own):
        outs[0][...] = dot_nn(ins[0][...], weights[0][...]).astype(bf16)

    return tiled_call(
        body,
        [tiles],
        seats,
        [a],
        [whole(a)],
        [jax.ShapeDtypeStruct((tiles.quarters, rows, tiles.parts * tw), bf16)],
        [seated(rows, tw, tiles.parts)],
        [],
        2 * rows * a.shape[1] * tw * tiles.steps,
    )[0]


def project_columns(lefts, sets, seats, depth, out_dtype):
    rows, tw, steps = lefts[0].shape[1], sets[0].width, sets[0].steps

    def body(step, weights, ins, outs, own):
        acc = own[0]
        total = dot_nt(ins[0][...], weights[0][...])
        for left, weight in zip(ins[1:], weights[1:]):
            total = total + dot_nt(left[...], weight[...])

        @pl.when(step == 0)
        def _():
            acc[...] = total

        @pl.when(step > 0)
        def _():
            acc[...] += total

        @pl.when(step == steps - 1)
        def _():
            outs[0][...] = acc[...].astype(out_dtype)

    return tiled_call(
        body,
        sets,
        seats,
        list(lefts),
        [seated(rows, tw, s.parts) for s in sets],
        [jax.ShapeDtypeStruct((rows, depth), out_dtype)],
        [pl.BlockSpec((rows, depth), lambda t, s: (0, 0))],
        [pltpu.VMEM((rows, depth), f32)],
        2 * rows * depth * tw * steps * len(sets),
    )[0]


def project_residual(left, tiles, seats, stream, gain):
    rows, depth = stream.shape
    tw, steps = tiles.width, tiles.steps

    def body(step, weights, ins, outs, own):
        acc = own[0]
        total = dot_nt(ins[0][...], weights[0][...])

        @pl.when(step == 0)
        def _():
            acc[...] = ins[1][...].astype(f32) + total

        @pl.when(step > 0)
        def _():
            acc[...] += total

        @pl.when(step == steps - 1)
        def _():
            value = acc[...]
            outs[0][...] = value
            inverse = lax.rsqrt(jnp.mean(value * value, axis=-1, keepdims=True) + norm_eps)
            outs[1][...] = (value * inverse * ins[2][...]).astype(bf16)

    return tiled_call(
        body,
        [tiles],
        seats,
        [left, stream, gain],
        [seated(rows, tw, tiles.parts), whole(stream), whole(gain)],
        [jax.ShapeDtypeStruct((rows, depth), f32), struct(rows, depth)],
        [pl.BlockSpec((rows, depth), lambda t, s: (0, 0))] * 2,
        [pltpu.VMEM((rows, depth), f32)],
        2 * rows * depth * tw * steps,
    )


def feed_forward(normed, gate_tiles, up_tiles, seats):
    rows, tw = normed.shape[0], gate_tiles.width

    def body(step, weights, ins, outs, own):
        a = ins[0][...]
        gate = dot_nn(a, weights[0][...])
        up = dot_nn(a, weights[1][...])
        outs[0][...] = (gate * jax.nn.sigmoid(gate) * up).astype(bf16)
        outs[1][...] = gate.astype(bf16)
        outs[2][...] = up.astype(bf16)

    shape = jax.ShapeDtypeStruct((gate_tiles.quarters, rows, gate_tiles.parts * tw), bf16)
    return tiled_call(
        body,
        [gate_tiles, up_tiles],
        seats,
        [normed],
        [whole(normed)],
        [shape] * 3,
        [seated(rows, tw, gate_tiles.parts)] * 3,
        [],
        4 * rows * normed.shape[1] * tw * gate_tiles.steps,
    )


def feed_back(cotangent, gate, up, down_tiles, seats):
    rows, tw = cotangent.shape[0], down_tiles.width

    def body(step, weights, ins, outs, own):
        grad = dot_nn(ins[0][...], weights[0][...])
        g = ins[1][...].astype(f32)
        u = ins[2][...].astype(f32)
        s = jax.nn.sigmoid(g)
        outs[0][...] = (grad * u * s * (1.0 + g * (1.0 - s))).astype(bf16)
        outs[1][...] = (grad * (g * s)).astype(bf16)

    shape = jax.ShapeDtypeStruct(gate.shape, bf16)
    tile = seated(rows, tw, down_tiles.parts)
    return tiled_call(
        body,
        [down_tiles],
        seats,
        [cotangent, gate, up],
        [whole(cotangent), tile, tile],
        [shape] * 2,
        [tile] * 2,
        [],
        2 * rows * cotangent.shape[1] * tw * down_tiles.steps,
    )


def qkv_back(grad_hat, raw, cosine, sine, q_gain, k_gain):
    quarters, rows, width = grad_hat.shape
    tw = width // 2

    def kernel(g_ref, r_ref, cos_ref, sin_ref, qg, kg, out, qsum, ksum):
        @pl.when(pl.program_id(0) == 0)
        def _():
            qsum[...] = jnp.zeros_like(qsum)
            ksum[...] = jnp.zeros_like(ksum)

        def back(cut, gain, total):
            w = g_ref[:, cut].astype(f32)
            w = w * cos_ref[...] + pltpu.roll(w * sin_ref[...], HEAD_DIM // 2, 1)
            x = r_ref[:, cut].astype(f32)
            inverse = lax.rsqrt(jnp.mean(x * x, axis=-1, keepdims=True) + norm_eps)
            u = x * inverse
            wu = w * u
            scaled = w * gain
            out[:, cut] = (
                inverse * (scaled - u * jnp.mean(wu * gain, axis=-1, keepdims=True))
            ).astype(bf16)
            return total + jnp.sum(wu, axis=0, keepdims=True)

        total = jnp.zeros((1, HEAD_DIM), f32)
        cuts = head_slices(width)
        n_query, n_key = tw // HEAD_DIM, tw // HEAD_DIM // 2
        for cut in cuts[:n_query]:
            total = back(cut, qg[...], total)
        qsum[...] += total
        total = jnp.zeros((1, HEAD_DIM), f32)
        for cut in cuts[n_query : n_query + n_key]:
            total = back(cut, kg[...], total)
        ksum[...] += total
        out[:, tw + tw // 2 :] = g_ref[:, tw + tw // 2 :]

    ins = [grad_hat, raw, cosine, sine, q_gain, k_gain]
    gain_shape = jax.ShapeDtypeStruct((1, HEAD_DIM), f32)
    out_shape = [jax.ShapeDtypeStruct(grad_hat.shape, bf16), gain_shape, gain_shape]
    tile = pl.BlockSpec((None, rows, width), lambda e: (e, 0, 0))
    fixed = lambda x: pl.BlockSpec(x.shape, lambda e: (0, 0))
    return pl.pallas_call(
        kernel,
        grid=(quarters,),
        in_specs=[tile, tile] + [fixed(x) for x in ins[2:]],
        out_specs=[tile, fixed(gain_shape), fixed(gain_shape)],
        out_shape=out_shape,
        compiler_params=params(),
        cost_estimate=cost(40 * quarters * rows * width, nbytes(ins) + nbytes(out_shape)),
    )(*ins)


def attention_specs(kv):
    q = pl.BlockSpec((TREE_TOK, GROUP * HEAD_DIM), lambda n, s: (0, n))
    k = pl.BlockSpec((TREE_TOK, HEAD_DIM), lambda n, s: (0, GROUP * kv + n))
    v = pl.BlockSpec((TREE_TOK, HEAD_DIM), lambda n, s: (0, (GROUP + 1) * kv + n))
    return q, k, v


def stacked(ref, start):
    rows = pl.ds(start, BRANCH)
    return jnp.concatenate(
        [ref[rows, h * HEAD_DIM : (h + 1) * HEAD_DIM] for h in range(GROUP)], axis=0
    )


def causal():
    key = lax.broadcasted_iota(jnp.int32, (BRANCH, GROUP * BRANCH), 0)
    query = lax.rem(lax.broadcasted_iota(jnp.int32, (BRANCH, GROUP * BRANCH), 1), BRANCH)
    return key <= query


TRUNK_BLOCKS = TRUNK // BRANCH
BLOCKS = TREE_TOK // BRANCH


def attention_forward(qkv, parents, kv):
    def kernel(parent_ref, q_ref, k_ref, v_ref, out_ref, log_ref, vt):
        vt[...] = v_ref[...].T
        mask = causal()

        def part(q, start, size, rule):
            score = dot_nt(k_ref[pl.ds(start, size), :], q)
            weight = jnp.exp2(score)
            if rule is not None:
                weight = rule(weight)
            out = dot_nn(vt[:, pl.ds(start, size)], weight.astype(bf16))
            return out, jnp.sum(weight, axis=0, keepdims=True)

        def finish(block, start, pieces):
            out = sum(p[0] for p in pieces)
            total = sum(p[1] for p in pieces)
            out = (out / total).T.astype(bf16)
            for h in range(GROUP):
                out_ref[pl.ds(start, BRANCH), h * HEAD_DIM : (h + 1) * HEAD_DIM] = out[
                    h * BRANCH : (h + 1) * BRANCH
                ]
            log_ref[0, pl.ds(block, 1), :] = jnp.log2(total)

        diagonal = lambda w: jnp.where(mask, w, 0.0)
        for block in range(TRUNK_BLOCKS):
            q = stacked(q_ref, block * BRANCH)
            pieces = [part(q, block * BRANCH, BRANCH, diagonal)]
            if block > 0:
                pieces.append(part(q, 0, block * BRANCH, None))
            finish(block, block * BRANCH, pieces)

        def branch(i, carry):
            block = TRUNK_BLOCKS + i
            start = pl.multiple_of(block * BRANCH, BRANCH)
            q = stacked(q_ref, start)
            parent = parent_ref[i]
            has = (parent != block).astype(f32)
            pieces = [
                part(q, start, BRANCH, diagonal),
                part(q, pl.multiple_of(parent * BRANCH, BRANCH), BRANCH, lambda w: w * has),
                part(q, 0, TRUNK, None),
            ]
            finish(block, start, pieces)
            return carry

        lax.fori_loop(0, FORKS2, branch, 0)

    q, k, v = attention_specs(kv)
    out_shape = [
        jax.ShapeDtypeStruct((TREE_TOK, GROUP * kv * HEAD_DIM), bf16),
        jax.ShapeDtypeStruct((kv, BLOCKS, GROUP * BRANCH), f32),
    ]
    return pl.pallas_call(
        kernel,
        grid_spec=pltpu.PrefetchScalarGridSpec(
            num_scalar_prefetch=1,
            grid=(kv,),
            in_specs=[q, k, v],
            out_specs=[
                q,
                pl.BlockSpec((1, BLOCKS, GROUP * BRANCH), lambda n, s: (n, 0, 0)),
            ],
            scratch_shapes=[pltpu.VMEM((HEAD_DIM, TREE_TOK), bf16)],
        ),
        out_shape=out_shape,
        compiler_params=params(),
        cost_estimate=cost(kv * 2.2e6 * 2 * GROUP * 256 * 2, nbytes([qkv]) + nbytes(out_shape)),
    )(parents, qkv, qkv, qkv)


def attention_backward(qkv, attended, grads, logs, parents, kv):
    width = qkv.shape[1]

    def kernel(
        parent_ref, q_ref, k_ref, v_ref, o_ref, do_ref, log_ref, out_ref, kt, dk, dv, dq_ref
    ):
        kt[...] = k_ref[...].T
        dk[...] = jnp.zeros_like(dk)
        dv[...] = jnp.zeros_like(dv)
        mask = causal()

        def part(q, do, log, delta, start, size, rule):
            rows = pl.ds(start, size)
            prob = jnp.exp2(dot_nt(k_ref[rows, :], q) - log)
            if rule is not None:
                prob = rule(prob)
            grad = dot_nt(v_ref[rows, :], do)
            score_grad = (prob * (grad - delta)).astype(bf16)
            dk[rows, :] += dot_nn(score_grad, q)
            dv[rows, :] += dot_nn(prob.astype(bf16), do)
            return dot_nn(kt[:, rows], score_grad)

        def one(block, start, ranges):
            q = stacked(q_ref, start)
            do = stacked(do_ref, start)
            o = stacked(o_ref, start)
            delta = jnp.sum((do.astype(f32) * o.astype(f32)).T, axis=0, keepdims=True)
            log = log_ref[0, pl.ds(block, 1), :]
            total = sum(part(q, do, log, delta, *r) for r in ranges)
            out = (total * LN2).T.astype(bf16)
            for h in range(GROUP):
                dq_ref[pl.ds(start, BRANCH), h * HEAD_DIM : (h + 1) * HEAD_DIM] = out[
                    h * BRANCH : (h + 1) * BRANCH
                ]

        diagonal = lambda p: jnp.where(mask, p, 0.0)
        for block in range(TRUNK_BLOCKS):
            ranges = [(block * BRANCH, BRANCH, diagonal)]
            if block > 0:
                ranges.append((0, block * BRANCH, None))
            one(block, block * BRANCH, ranges)

        def branch(i, carry):
            block = TRUNK_BLOCKS + i
            start = pl.multiple_of(block * BRANCH, BRANCH)
            parent = parent_ref[i]
            has = (parent != block).astype(f32)
            one(
                block,
                start,
                [
                    (start, BRANCH, diagonal),
                    (pl.multiple_of(parent * BRANCH, BRANCH), BRANCH, lambda p: p * has),
                    (0, TRUNK, None),
                ],
            )
            return carry

        lax.fori_loop(0, FORKS2, branch, 0)
        for head in range(kv):

            @pl.when(pl.program_id(0) == head)
            def _(head=head):
                wide = GROUP * HEAD_DIM
                out_ref[:, head * wide : (head + 1) * wide] = dq_ref[...]
                at = kv * wide + head * HEAD_DIM
                out_ref[:, at : at + HEAD_DIM] = (dk[...] * score_scale).astype(bf16)
                at += kv * HEAD_DIM
                out_ref[:, at : at + HEAD_DIM] = dv[...].astype(bf16)

    q, k, v = attention_specs(kv)
    out_shape = jax.ShapeDtypeStruct((TREE_TOK, width), bf16)
    return pl.pallas_call(
        kernel,
        grid_spec=pltpu.PrefetchScalarGridSpec(
            num_scalar_prefetch=1,
            grid=(kv,),
            in_specs=[
                q,
                k,
                v,
                q,
                q,
                pl.BlockSpec((1, BLOCKS, GROUP * BRANCH), lambda n, s: (n, 0, 0)),
            ],
            out_specs=pl.BlockSpec((TREE_TOK, width), lambda n, s: (0, 0)),
            scratch_shapes=[
                pltpu.VMEM((HEAD_DIM, TREE_TOK), bf16),
                pltpu.VMEM((TREE_TOK, HEAD_DIM), f32),
                pltpu.VMEM((TREE_TOK, HEAD_DIM), f32),
                pltpu.VMEM((TREE_TOK, GROUP * HEAD_DIM), bf16),
            ],
        ),
        out_shape=out_shape,
        compiler_params=params(),
        cost_estimate=cost(
            kv * 2.2e6 * 2 * GROUP * 640 * 2, nbytes([qkv, attended, grads, qkv])
        ),
    )(parents, qkv, qkv, qkv, attended, grads, logs)


def weight_gradient(lefts, rights, half, cut=None):
    pairs = len(lefts)
    rows, depth = lefts[0].shape
    quarters, _, width = rights[0].shape
    size = depth // 2
    if cut is None:
        tw = width // 2 if width > 1024 else width
        parts, first = width // tw, 0
    else:
        width = tw = width // 2
        parts, first = 1, cut

    def kernel(*refs):
        left_refs, right_refs = refs[:pairs], refs[pairs : 2 * pairs]
        out_ref, left_s, right_s = refs[2 * pairs :]

        @pl.when(pl.program_id(0) == 0)
        def _():
            for i, ref in enumerate(left_refs):
                left_s[i * rows : (i + 1) * rows] = ref[...]

        for i, ref in enumerate(right_refs):
            right_s[i * rows : (i + 1) * rows] = ref[...]
        out_ref[...] = contract_rows(left_s[...], right_s[...]).astype(bf16)

    out_shape = jax.ShapeDtypeStruct((size, quarters * width), bf16)
    arrays = list(lefts) + list(rights)
    return pl.pallas_call(
        kernel,
        grid=(quarters * parts,),
        in_specs=[pl.BlockSpec((rows, size), lambda t: (0, half))] * pairs
        + [pl.BlockSpec((None, rows, tw), lambda t: (t // parts, 0, first + t % parts))] * pairs,
        out_specs=pl.BlockSpec((size, tw), lambda t: (0, t)),
        out_shape=out_shape,
        scratch_shapes=[
            pltpu.VMEM((pairs * rows, size), bf16),
            pltpu.VMEM((pairs * rows, tw), bf16),
        ],
        compiler_params=params(),
        cost_estimate=cost(
            2 * pairs * rows * size * quarters * width, nbytes(arrays) + nbytes([out_shape])
        ),
    )(*arrays)


def flipped(index, mask):
    bit = 1
    while bit <= mask:
        if mask & bit:
            index = index + bit * (1 - 2 * lax.rem(lax.div(index, bit), 2))
        bit *= 2
    return index


def transfer_call(
    program, m, n, ins, outs, scratch, count, locals_, number, vmem_ins=(), aliases=None
):
    n_in, n_out, n_scratch = len(ins), len(outs), len(scratch)

    class Mover:
        def __init__(self, send, recv, own):
            self.send, self.recv, self.own = send, recv, own
            self.made, self.local = [], []

        def start(self, source, target, axis, mask):
            k = len(self.made)
            place = flipped(lax.axis_index(axis), mask)
            copy = pltpu.make_async_remote_copy(
                src_ref=source,
                dst_ref=target,
                send_sem=self.send.at[k],
                recv_sem=self.recv.at[k],
                device_id={axis: place},
                device_id_type=pl.DeviceIdType.MESH,
            )
            copy.start()
            self.made.append(copy)
            return copy

        def keep(self, source, target):
            copy = pltpu.make_async_copy(source, target, self.own.at[len(self.local)])
            copy.start()
            self.local.append(copy)
            return copy

    def kernel(*refs):
        in_refs, out_refs = refs[:n_in], refs[n_in : n_in + n_out]
        rest = refs[n_in + n_out :]
        mover = Mover(*rest[n_scratch:])
        barrier = pltpu.get_barrier_semaphore()
        partners = [("wide", k) for k in range(1, m)] if m != 8 else [
            ("wide", k) for k in (1, 2, 4)
        ]
        partners += [("tp", e) for e in range(1, n)]
        for axis, mask in partners:
            pl.semaphore_signal(
                barrier,
                inc=1,
                device_id={axis: flipped(lax.axis_index(axis), mask)},
                device_id_type=pl.DeviceIdType.MESH,
            )
        pl.semaphore_wait(barrier, len(partners))
        program(mover, in_refs, out_refs, rest[:n_scratch])
        for copy in mover.made:
            copy.wait_send()

    return pl.pallas_call(
        kernel,
        in_specs=[
            pl.BlockSpec(memory_space=pltpu.VMEM if i in vmem_ins else pl.ANY) for i in range(n_in)
        ],
        out_specs=[pl.BlockSpec(memory_space=pl.ANY)] * n_out,
        out_shape=outs,
        scratch_shapes=list(scratch)
        + [
            pltpu.SemaphoreType.DMA((count,)),
            pltpu.SemaphoreType.DMA((count,)),
            pltpu.SemaphoreType.DMA((locals_,)),
        ],
        input_output_aliases=aliases or {},
        compiler_params=pltpu.CompilerParams(
            collective_id=number, has_side_effects=True, vmem_limit_bytes=VMEM
        ),
        cost_estimate=cost(0, 1e6),
    )(*ins)


def swap_own(source, target, mine, sems):
    seat = lax.axis_index("tp")
    return (
        pltpu.make_async_copy(source.at[seat], mine, sems.at[0]),
        pltpu.make_async_copy(mine, target.at[seat], sems.at[1]),
    )


def gradient_pair(lefts, rights, cut, number, ride=None):
    pairs = len(lefts)
    rows, depth = lefts[0].shape
    quarters, _, width = rights[0].shape
    size = depth // 2
    block = size // 4
    half = block // 2
    if cut is None:
        tw = width // 2 if width > 1024 else width
        parts, first = width // tw, 0
    else:
        width = tw = width // 2
        parts, first = 1, cut
    steps = quarters * parts
    n = ride.shape[0] if ride is not None else 1
    rides = [] if ride is None else [ride]

    def kernel(*refs):
        left_refs, right_refs = refs[:pairs], refs[pairs : 2 * pairs]
        at = 2 * pairs
        ride_in = refs[at : at + len(rides)]
        at += len(rides)
        own_ref, x_ref, y_ref, top_ref, low_ref = refs[at : at + 5]
        at += 5
        ride_out = refs[at : at + len(rides)]
        at += len(rides)
        left_s, right_s, sent, came, send_sems, recv_sems = refs[at : at + 6]
        extra = refs[at + 6 :]
        step = pl.program_id(0)
        other_core = {"wide": flipped(lax.axis_index("wide"), 1)}

        def copy(k):
            return pltpu.make_async_remote_copy(
                src_ref=sent.at[k],
                dst_ref=came.at[k],
                send_sem=send_sems.at[k],
                recv_sem=recv_sems.at[k],
                device_id=other_core,
                device_id_type=pl.DeviceIdType.MESH,
            )

        def ride_copies():
            mine, ride_send, ride_recv, own_sems = extra
            seat = lax.axis_index("tp")
            return [
                pltpu.make_async_remote_copy(
                    src_ref=ride_in[0].at[flipped(seat, e)],
                    dst_ref=ride_out[0].at[seat],
                    send_sem=ride_send.at[e - 1],
                    recv_sem=ride_recv.at[e - 1],
                    device_id={"tp": flipped(seat, e)},
                    device_id_type=pl.DeviceIdType.MESH,
                )
                for e in range(1, n)
            ], swap_own(ride_in[0], ride_out[0], mine, own_sems)

        @pl.when(step == 0)
        def _():
            barrier = pltpu.get_barrier_semaphore()
            partners = [other_core] + [
                {"tp": flipped(lax.axis_index("tp"), e)} for e in range(1, n)
            ]
            for partner in partners:
                pl.semaphore_signal(
                    barrier, inc=1, device_id=partner, device_id_type=pl.DeviceIdType.MESH
                )
            pl.semaphore_wait(barrier, len(partners))
            if rides:
                sends, (load, keep) = ride_copies()
                for c in sends:
                    c.start()
                load.start()
                load.wait()
                keep.start()

        @pl.when(lax.rem(step, steps) == 0)
        def _():
            for i, ref in enumerate(left_refs):
                left_s[i * rows : (i + 1) * rows] = ref[...]

        for i, ref in enumerate(right_refs):
            right_s[i * rows : (i + 1) * rows] = ref[...]
        product = contract_rows(left_s[...], right_s[...])

        @pl.when(step < steps)
        def _():
            sent[step] = product.astype(bf16)
            copy(step).start()

        @pl.when(step >= steps)
        def _():
            k = step - steps
            copy(k).wait_recv()
            total = (product + came[k].astype(f32)).astype(bf16)
            own_ref[...] = total[:block]
            x_ref[...] = total[block : 2 * block]
            y_ref[...] = total[2 * block : 3 * block]
            top_ref[...] = total[3 * block : 3 * block + half]
            low_ref[...] = total[3 * block + half :]

        @pl.when(step == 2 * steps - 1)
        def _():
            for k in range(steps):
                copy(k).wait_send()
            if rides:
                sends, own_row = ride_copies()
                for c in sends:
                    c.wait_send()
                    c.wait_recv()
                own_row[1].wait()

    columns = quarters * width
    heights = (block, block, block, half, half)
    out_shape = [struct(h, columns) for h in heights]
    arrays = list(lefts) + list(rights)
    late = lambda t: (0, jnp.maximum(t - steps, 0))
    ride_scratch = (
        []
        if ride is None
        else [
            pltpu.VMEM(ride.shape[1:], bf16),
            pltpu.SemaphoreType.DMA((n - 1,)),
            pltpu.SemaphoreType.DMA((n - 1,)),
            pltpu.SemaphoreType.DMA((2,)),
        ]
    )

    def right_map(t):
        t = lax.rem(t, steps)
        return (lax.div(t, parts), 0, first + lax.rem(t, parts))

    result = pl.pallas_call(
        kernel,
        grid=(2 * steps,),
        in_specs=[pl.BlockSpec((rows, size), lambda t: (0, 1 - lax.div(t, steps)))] * pairs
        + [pl.BlockSpec((None, rows, tw), right_map)] * pairs
        + [pl.BlockSpec(memory_space=pl.ANY)] * len(rides),
        out_specs=[pl.BlockSpec((h, tw), late) for h in heights]
        + [pl.BlockSpec(memory_space=pl.ANY)] * len(rides),
        out_shape=out_shape + [struct(*r.shape) for r in rides],
        scratch_shapes=[
            pltpu.VMEM((pairs * rows, size), bf16),
            pltpu.VMEM((pairs * rows, tw), bf16),
            pltpu.VMEM((steps, size, tw), bf16),
            pltpu.VMEM((steps, size, tw), bf16),
            pltpu.SemaphoreType.DMA((steps,)),
            pltpu.SemaphoreType.DMA((steps,)),
        ]
        + ride_scratch,
        compiler_params=pltpu.CompilerParams(
            collective_id=number, has_side_effects=True, vmem_limit_bytes=VMEM
        ),
        cost_estimate=cost(
            4 * pairs * rows * size * columns, nbytes(arrays) + nbytes(out_shape)
        ),
    )(*arrays, *rides)
    return (result[:5], result[5]) if rides else (result, None)


def waves_start(mover, n, source, target):
    if n != 4:
        return [mover.start(source, target(e), "tp", e) for e in range(1, n)]
    far = mover.start(source, target(2), "tp", 2)
    near = mover.start(source, target(1), "tp", 1)
    return [near, far]


def waves_forward(mover, n, waves, target):
    if n != 4:
        return waves
    waves[1].wait_recv()
    return waves + [mover.start(target(2), target(3), "tp", 1)]


def struct(*shape):
    return jax.ShapeDtypeStruct(shape, bf16)


class Spread:
    def __init__(self, mover, m, source, target, block):
        self.mover, self.m, self.source, self.block = mover, m, source, block
        self.at = lambda start, size: target(pl.ds(start, size))

    def first(self):
        go, block, source = self.mover.start, self.block, self.source
        if self.m != 8:
            self.all = [
                go(source, self.at(k * block, block), "wide", k) for k in range(1, self.m)
            ]
            return
        self.x = go(source, self.at(block, block), "wide", 2)
        self.y = go(source, self.at(2 * block, block), "wide", 4)
        self.cores = [go(source, self.at(4 * block, block), "wide", 1)]

    def second(self):
        if self.m != 8:
            return
        go, block = self.mover.start, self.block
        half = block // 2
        self.x.wait_recv()
        low = self.at(block + half, half)
        self.low = go(low, self.at(3 * block + half, half), "wide", 4)
        self.cores.append(go(self.at(block, block), self.at(5 * block, block), "wide", 1))
        self.y.wait_recv()
        top = self.at(2 * block, half)
        self.top = go(top, self.at(3 * block, half), "wide", 2)
        self.cores.append(go(self.at(2 * block, block), self.at(6 * block, block), "wide", 1))

    def third(self):
        if self.m != 8:
            return
        go, block = self.mover.start, self.block
        self.low.wait_recv()
        self.top.wait_recv()
        self.cores.append(go(self.at(3 * block, block), self.at(7 * block, block), "wide", 1))

    def last(self):
        for copy in self.all if self.m != 8 else self.cores:
            copy.wait_recv()


def exclusive_or(a, b, count):
    total, bit = 0, 1
    while bit < count:
        total = total + bit * lax.rem(lax.div(a, bit) + lax.div(b, bit), 2)
        bit *= 2
    return total


def gather_front(
    m, n, order, qkv_block, in_block, down_block, gain_block, tokens, out_grad, cosine, sine
):
    block, qw = qkv_block.shape
    fw, dw = in_block.shape[1], down_block.shape[1]
    depth = block * m
    pairs = n // 2
    rows_in = tokens.shape[0]
    tw = qw // 2
    gain_width = gain_block.shape[1]
    chunks = 2 if rows_in % 32 == 0 else 1
    chunk = rows_in // chunks

    def program(mover, ins, outs, scratch):
        qkv, inner, down, gain, x_ref, dy_ref, cos_ref, sin_ref = ins
        (
            weights, in_own, in_rest, down_rest, gains,
            x_out, dy_out, normed_out, hats, raws,
        ) = outs
        gain_s, normed_s, tile_s, hat_s, raw_s, tile_sems, hat_sems, raw_sems = scratch
        where, seat = lax.axis_index("wide"), lax.axis_index("tp")
        rows = pl.ds(0, block)
        place = lambda e: weights.at[e, rows]
        waves = waves_start(mover, n, qkv, place)
        spread_gains = Spread(mover, m, gain, lambda r: gains.at[r], GAIN_ROWS)
        spread_gains.first()
        spreads = [
            Spread(mover, m, qkv if q == 0 else place(q), lambda r, q=q: weights.at[q, r], block)
            for q in range(n)
        ]
        spreads[0].first()
        kept = [
            mover.keep(qkv, weights.at[0, rows]),
            mover.keep(inner, in_own.at[0, rows]),
        ]
        kept_gain = mover.keep(gain, gains.at[pl.ds(0, GAIN_ROWS)])
        spread_gains.second()
        spreads[0].second()
        spread_gains.third()
        spreads[0].third()
        columns = [
            pl.ds(pl.multiple_of(flipped(where, k) * block, 128), block) for k in order
        ]
        for k in range(m):
            cut = pl.ds(k * block, block)
            kept.append(mover.keep(x_ref.at[:, columns[k]], x_out.at[:, cut]))
            kept.append(mover.keep(dy_ref.at[:, columns[k]], dy_out.at[:, cut]))
        if n == 4:
            waves = waves_forward(mover, n, waves, place)
            spreads[2].first()
            waves[0].wait_recv()
            spreads[1].first()
            waves[2].wait_recv()
            spreads[3].first()
        else:
            for q in range(1, n):
                waves[q - 1].wait_recv()
                spreads[q].first()
        late = []
        for e in range(1, pairs):
            late.append(mover.start(inner, in_rest.at[e - 1, rows], "tp", 2 * e))
            late.append(mover.start(down, down_rest.at[e - 1, rows], "tp", 2 * e))

        spread_gains.last()
        kept_gain.wait()
        load = mover.keep(gains, gain_s)
        load.wait()

        def normalise(i, carry):
            part = pl.ds(pl.multiple_of(i * chunk, 16), chunk)
            x = x_ref[part, :].astype(f32)
            inverse = lax.rsqrt(jnp.mean(x * x, axis=-1, keepdims=True) + norm_eps)
            for k in range(m):
                piece = x_ref[part, columns[k]].astype(f32) * inverse
                scale = gain_s[k * GAIN_ROWS : k * GAIN_ROWS + 1, :block]
                normed_s[part, k * block : (k + 1) * block] = (piece * scale).astype(bf16)
            return carry

        lax.fori_loop(0, chunks, normalise, 0)
        kept.append(mover.keep(normed_s, normed_out))
        heads_at = 2 * block

        def head_gain(at):
            total = gain_s[0:1, at : at + HEAD_DIM]
            for k in range(1, m):
                total = total + gain_s[k * GAIN_ROWS : k * GAIN_ROWS + 1, at : at + HEAD_DIM]
            return total

        gain_q, gain_k = head_gain(heads_at), head_gain(heads_at + HEAD_DIM)

        turn = (2, 1, 3) if n == 4 else range(1, n)
        for q in turn:
            spreads[q].second()
        own = Spread(mover, m, inner, lambda r: in_own.at[0, r], block)
        own.first()
        for q in turn:
            spreads[q].third()
        for spread in spreads:
            spread.last()
        kept[0].wait()

        def fetch(q, part):
            return pltpu.make_async_copy(
                weights.at[q, :, pl.ds(part * tw, tw)], tile_s.at[part], tile_sems.at[part]
            )

        def leave(q, part):
            home = exclusive_or(seat, q, n)
            cut = pl.ds(part * tw, tw)
            return (
                pltpu.make_async_copy(
                    hat_s.at[part], hats.at[home, :, cut], hat_sems.at[part]
                ),
                pltpu.make_async_copy(
                    raw_s.at[part], raws.at[home, :, cut], raw_sems.at[part]
                ),
            )

        def turned(x, gain):
            inverse = lax.rsqrt(jnp.mean(x * x, axis=-1, keepdims=True) + norm_eps)
            u = x * inverse * gain
            return u * cos_ref[...] + pltpu.roll(u, HEAD_DIM // 2, 1) * sin_ref[...]

        def quarter(q, carry):
            for part in range(2):
                if part == 0:
                    fetch(q, 1).start()
                else:

                    @pl.when(q + 1 < n)
                    def _():
                        fetch(q + 1, 0).start()

                fetch(q, part).wait()

                @pl.when(q > 0)
                def _(part=part):
                    for c in leave(q, part):
                        c.wait()

                acc = dot_nn(normed_s[...], tile_s[part])
                raw_s[part] = acc.astype(bf16)
                if part == 0:
                    for cut in head_slices(tw):
                        hat_s[0, :, cut] = turned(acc[:, cut], gain_q).astype(bf16)
                else:
                    for cut in head_slices(tw // 2):
                        hat_s[1, :, cut] = (turned(acc[:, cut], gain_k) * key_scale).astype(bf16)
                    hat_s[1, :, tw // 2 :] = acc[:, tw // 2 :].astype(bf16)
                for c in leave(q, part):
                    c.start()
            return carry

        fetch(0, 0).start()
        lax.fori_loop(0, n // 2, quarter, 0)
        own.second()
        lax.fori_loop(n // 2, n, quarter, 0)
        own.third()
        for part in range(2):
            for c in leave(n - 1, part):
                c.wait()
        own.last()
        for copy in late:
            copy.wait_recv()
        for copy in kept[1:]:
            copy.wait()

    per = 8 if m == 8 else m - 1
    return transfer_call(
        program,
        m,
        n,
        [qkv_block, in_block, down_block, gain_block, tokens, out_grad, cosine, sine],
        [
            struct(n, depth, qw),
            struct(1, depth, fw),
            struct(pairs - 1, depth, fw),
            struct(pairs - 1, depth, dw),
            jax.ShapeDtypeStruct((m * GAIN_ROWS, gain_width), f32),
            struct(rows_in, depth),
            struct(rows_in, depth),
            struct(rows_in, depth),
            struct(n, rows_in, qw),
            struct(n, rows_in, qw),
        ],
        [
            pltpu.VMEM((m * GAIN_ROWS, gain_width), f32),
            pltpu.VMEM((rows_in, depth), bf16),
            pltpu.VMEM((2, depth, tw), bf16),
            pltpu.VMEM((2, rows_in, tw), bf16),
            pltpu.VMEM((2, rows_in, tw), bf16),
            pltpu.SemaphoreType.DMA((2,)),
            pltpu.SemaphoreType.DMA((2,)),
            pltpu.SemaphoreType.DMA((2,)),
        ],
        (n - 1) + per * (n + 2) + 2 * (pairs - 1),
        5 + 2 * m,
        1,
        vmem_ins=tuple(range(8)),
    )


def swap_heads(mover, n, mine, source, target):
    seat = lax.axis_index("tp")
    load = mover.keep(source.at[seat], mine)
    sends = [
        mover.start(source.at[flipped(seat, e)], target.at[seat], "tp", e) for e in range(1, n)
    ]
    load.wait()
    return sends, mover.keep(mine, target.at[seat])


def gather_middle(m, n, hats, in_rest, out_block, down_block):
    quarters, rows, width = hats.shape
    pairs, depth, fw = in_rest.shape
    block, ow = out_block.shape
    dw = down_block.shape[1]

    def program(mover, ins, outs, scratch):
        hat, _, out, down = ins
        heads, rest, weights, down_own = outs
        first = pl.ds(0, block)
        kept = [mover.keep(out, weights.at[0, first]), mover.keep(down, down_own.at[0, first])]
        place = lambda e: weights.at[e, first]
        waves = waves_start(mover, n, out, place)
        spreads = [
            Spread(mover, m, rest.at[p, first], lambda r, p=p: rest.at[p, r], block)
            for p in range(pairs)
        ]
        for spread in spreads:
            spread.first()
        waves = waves_forward(mover, n, waves, place)
        for copy in waves if n != 4 else (waves[0], waves[2]):
            copy.wait_recv()
        sends, own_row = swap_heads(mover, n, scratch[0], hat, heads)
        kept[0].wait()
        for spread in spreads:
            spread.second()
        quarter = Spread(mover, m, weights.at[:, first], lambda r: weights.at[:, r], block)
        quarter.first()
        for spread in spreads:
            spread.third()
        quarter.second()
        own = Spread(mover, m, down, lambda r: down_own.at[0, r], block)
        own.first()
        quarter.third()
        own.second()
        own.third()
        for spread in spreads + [own, quarter]:
            spread.last()
        for copy in sends:
            copy.wait_recv()
        kept[1].wait()
        own_row.wait()

    per = 8 if m == 8 else m - 1
    return transfer_call(
        program,
        m,
        n,
        [hats, in_rest, out_block, down_block],
        [
            struct(n, rows, width),
            struct(pairs, depth, fw),
            struct(n, depth, ow),
            struct(1, depth, dw),
        ],
        [pltpu.VMEM((rows, width), bf16)],
        2 * (n - 1) + per * (pairs + 2),
        4,
        2,
        vmem_ins=(2, 3),
        aliases={1: 1},
    )


def gather_late(m, n, heads, down_rest):
    quarters, rows, width = heads.shape
    pairs, depth, dw = down_rest.shape
    block = depth // m

    def program(mover, ins, outs, scratch):
        source, _ = ins
        target, rest = outs
        first = pl.ds(0, block)
        sends, own_row = swap_heads(mover, n, scratch[0], source, target)
        spreads = [
            Spread(mover, m, rest.at[p, first], lambda r, p=p: rest.at[p, r], block)
            for p in range(pairs)
        ]
        for stage in ("first", "second", "third", "last"):
            for spread in spreads:
                getattr(spread, stage)()
        for copy in sends:
            copy.wait_recv()
        own_row.wait()

    per = 8 if m == 8 else m - 1
    return transfer_call(
        program,
        m,
        n,
        [heads, down_rest],
        [struct(n, rows, width), struct(pairs, depth, dw)],
        [pltpu.VMEM((rows, width), bf16)],
        (n - 1) + per * pairs,
        2,
        3,
        aliases={1: 1},
    )


def shuffle_columns(a, order):
    rows, count = a.shape[0], order.shape[0]
    width = a.shape[1] // count

    def kernel(order_ref, in_ref, out_ref):
        out_ref[...] = in_ref[...]

    return pl.pallas_call(
        kernel,
        grid_spec=pltpu.PrefetchScalarGridSpec(
            num_scalar_prefetch=1,
            grid=(count,),
            in_specs=[pl.BlockSpec((rows, width), lambda k, s: (0, s[k]))],
            out_specs=pl.BlockSpec((rows, width), lambda k, s: (0, k)),
        ),
        out_shape=jax.ShapeDtypeStruct(a.shape, a.dtype),
        cost_estimate=cost(0, 2 * nbytes([a])),
    )(order, a)


def inverse_rms(values):
    return lax.rsqrt(jnp.mean(values * values, axis=-1, keepdims=True) + norm_eps)


def norm_back(grads, unit_values, inverse, gain):
    scaled = grads * gain
    return inverse * (scaled - unit_values * jnp.mean(scaled * unit_values, axis=-1, keepdims=True))


def after(values, *conditions):
    return lax.optimization_barrier((values, conditions))[0]


class Job:
    def __init__(self, stages):
        self.stages = stages
        self.result = None
        self.started, self.pending = next(stages)

    def advance(self, came):
        try:
            self.started, self.pending = self.stages.send(came)
        except StopIteration as stop:
            self.result = stop.value
            self.pending = None

    def finish(self):
        while self.result is None:
            self.advance(self.pending)
        return self.result


def tick(values, *jobs):
    jobs = [j for j in jobs if j.result is None]
    values, came = lax.optimization_barrier((values, [j.pending for j in jobs]))
    for j, c in zip(jobs, came):
        j.advance(c)
    return values


def local(
    m,
    n,
    tokens,
    out_grad,
    seg_ids,
    parent_table,
    path_pos,
    attn_gain,
    w_query,
    w_key,
    w_value,
    w_out,
    q_gain,
    k_gain,
    ffn_gain,
    w_gate,
    w_up,
    w_down,
):
    rows, depth = tokens.shape
    block = depth // m
    order = [0, 2, 4, 6, 1, 3, 5, 7] if m == 8 else list(range(m))
    where = lax.axis_index("wide").astype(jnp.int32)
    seat = lax.axis_index("tp").astype(jnp.int32)
    relative = jnp.asarray(order, jnp.int32) ^ where
    inverse_order = [order.index(k) for k in range(m)]
    absolute = jnp.take(jnp.asarray(inverse_order, jnp.int32), jnp.arange(m, dtype=jnp.int32) ^ where)
    seats = jnp.arange(n, dtype=jnp.int32) ^ seat
    plain = jnp.arange(n, dtype=jnp.int32)

    def over(axis, a, mask):
        size = m if axis == "wide" else n
        return lax.ppermute(a, axis, [(i, i ^ mask) for i in range(size)])

    def scatter(lefts, rights, cut, number, ride=None, rode=None):
        if m != 8:
            if ride is not None:
                rode.append(swap(ride))
            other = weight_gradient(lefts, rights, 1, cut)
            mine = weight_gradient(lefts, rights, 0, cut)
            both = jnp.concatenate([mine, other])
            got = yield both, [over("wide", both[k * block : (k + 1) * block], k) for k in range(1, m)]
            return sum((g.astype(f32) for g in got), both[:block].astype(f32))
        (own, x, y, top_sent, low_sent), came = gradient_pair(lefts, rights, cut, number, ride)
        if ride is not None:
            rode.append(came)
        half = block // 2
        top, low = yield (top_sent, low_sent), [over("wide", top_sent, 2), over("wide", low_sent, 4)]
        for_x = jnp.concatenate([x[:half], (x[half:].astype(f32) + low.astype(f32)).astype(bf16)])
        for_y = jnp.concatenate([(y[:half].astype(f32) + top.astype(f32)).astype(bf16), y[half:]])
        from_x, from_y = yield [for_x, for_y], [over("wide", for_x, 2), over("wide", for_y, 4)]
        return own.astype(f32) + from_x.astype(f32) + from_y.astype(f32)

    def ffn_share(left, rights, number, ride=None, rode=None):
        total = yield from scatter(left, rights, None, number, ride, rode)
        parts = [total[:, e * fcols : (e + 1) * fcols].astype(bf16) for e in range(1, n // 2)]
        sent = yield parts, [over("tp", p, 2 * (e + 1)) for e, p in enumerate(parts)]
        return sum((x.astype(f32) for x in sent), total[:, :fcols])

    def swap(a):
        return lax.all_to_all(a, "tp", split_axis=0, concat_axis=0, tiled=True)

    def attn_share(left, right, cut, number):
        total = yield from scatter([left], [right], cut, number)
        parts = total.astype(bf16).reshape(block, n, -1).transpose(1, 0, 2)
        (came,) = yield parts, [swap(parts)]
        return jnp.sum(came.astype(f32), axis=0)

    qkv_block = jnp.concatenate([w_query, w_key, w_value], axis=1)
    out_block = w_out.T
    in_block = jnp.concatenate([w_gate, w_up], axis=1)
    down_block = w_down.T
    aw = w_query.shape[1]
    kv = w_key.shape[1] // HEAD_DIM
    fcols = w_gate.shape[1]
    fw = fcols // 3

    small = q_gain.shape[0]
    head_row = lambda g: lax.dynamic_update_slice(
        jnp.zeros((HEAD_DIM,), f32), g.astype(f32), (where * small,)
    )
    gain_row = jnp.concatenate(
        [attn_gain.astype(f32), ffn_gain.astype(f32), head_row(q_gain), head_row(k_gain)]
    )[None]
    gain_block = jnp.pad(gain_row, ((0, GAIN_ROWS - 1), (0, 0)))
    base = where * parent_table.shape[0]
    block_segs = seg_ids[TRUNK::BRANCH] - base
    hit = block_segs[:, None] == jnp.arange(parent_table.shape[0], dtype=jnp.int32)[None, :]
    block_parents = jnp.sum(jnp.where(hit, parent_table[None, :] - base, 0), axis=1)
    match = block_parents[:, None] == block_segs[None, :]
    number = TRUNK_BLOCKS + jnp.arange(FORKS2, dtype=jnp.int32)
    parents = jnp.where(
        jnp.any(match, axis=1), jnp.sum(jnp.where(match, number[None, :], 0), axis=1), number
    ).astype(jnp.int32)

    own_pos = lax.dynamic_slice_in_dim(path_pos, seat * rows, rows, 0).astype(f32)
    frequency = rope_base ** (-(jnp.arange(HEAD_DIM // 2, dtype=f32) * 2.0) / HEAD_DIM)
    angles = own_pos[:, None] * frequency[None, :]
    cosine, sine = jnp.cos(angles), jnp.sin(angles)
    cosine = jnp.concatenate([cosine, cosine], axis=-1)
    sine = jnp.concatenate([-sine, sine], axis=-1)

    (
        qkv_all, in_own, in_rest, down_rest, gains, stream_low, cotangent, normed_one, hats, raws,
    ) = gather_front(
        m, n, order, qkv_block, in_block, down_block, gain_block, tokens, out_grad, cosine, sine
    )
    gains = gains[::GAIN_ROWS]
    gain_one = gains[:, :block].reshape(1, depth)
    gain_two = gains[:, block : 2 * block].reshape(1, depth)
    gain_q = jnp.sum(gains[:, 2 * block : 2 * block + HEAD_DIM], axis=0, keepdims=True)
    gain_k = jnp.sum(gains[:, 2 * block + HEAD_DIM :], axis=0, keepdims=True)
    qkv_tiles = Tiles([qkv_all], 2, 0, aw)
    qkv, in_rest, out_all, down_own = gather_middle(m, n, hats, in_rest, out_block, down_block)
    qkv = qkv.reshape(n * rows, -1)
    attended_heads, logs = attention_forward(qkv, parents, kv)
    attended, down_rest = gather_late(m, n, attended_heads.reshape(n, rows, -1), down_rest)
    out_tiles = Tiles([out_all], 1, 0, aw)
    after_attn, normed_two = project_residual(attended, out_tiles, seats, stream_low, gain_two)

    normed_two_next = over("tp", normed_two, 1)

    gate_tiles = Tiles([in_own, in_rest], 3, 0, fw)
    up_tiles = Tiles([in_own, in_rest], 3, 3, fw)
    down_tiles = Tiles([down_own, down_rest], 3, 0, fw)

    hidden, gate, up = feed_forward(normed_two, gate_tiles, up_tiles, plain)
    down = project_columns([hidden], [down_tiles], plain, depth, f32)
    normed_two_next, cotangent_sent = after((normed_two_next, cotangent), (down, normed_two_next))
    cotangent_next = over("tp", cotangent_sent, 1)
    hidden_next, gate_next, up_next = feed_forward(normed_two_next, gate_tiles, up_tiles, plain)
    down_part = project_columns([hidden_next], [down_tiles], plain, depth, bf16)
    own_grad = after(cotangent, down_part)
    gate_grad, up_grad = feed_back(own_grad, gate, up, down_tiles, plain)
    cotangent_next, hidden_late = after((cotangent_next, hidden), gate_grad)
    down_job = Job(ffn_share([cotangent, cotangent_next], [hidden_late, hidden_next], 4))
    cotangent_next, down_sent = after((cotangent_next, down_part), down_job.started)
    down_next = over("tp", down_sent, 1)
    gate_grad_next, up_grad_next = feed_back(
        cotangent_next, gate_next, up_next, down_tiles, plain
    )
    gate_late, up_late = tick((gate_grad_next, up_grad_next), down_job)
    gate_late, up_late = after((gate_late, up_late), down_job.started)
    back_part = project_columns([gate_late, up_late], [gate_tiles, up_tiles], plain, depth, bf16)
    back_part, down_next = after((back_part, down_next), back_part)
    back_next = over("tp", back_part, 1)
    gate_grad, up_grad = after((gate_grad, up_grad), back_part)
    gate_job = Job(ffn_share([normed_two, normed_two_next], [gate_grad, gate_grad_next], 5))
    gate_late, up_late = after((gate_grad, up_grad), gate_job.started)
    gate_late, up_late = tick((gate_late, up_late), down_job)
    gate_late, up_late = after((gate_late, up_late), down_job.started)
    back = project_columns([gate_late, up_late], [gate_tiles, up_tiles], plain, depth, f32)
    back, back_next = after((back, back_next), back)
    back = tick(back, gate_job)
    back = after(back, gate_job.started)
    normed_two_grad = back + back_next.astype(f32)
    inverse_two = inverse_rms(after(after_attn, normed_two_next))
    unit_two = after_attn * inverse_two

    ffn_gain_part = jnp.sum(normed_two_grad * unit_two, axis=0)
    stream_grad = cotangent.astype(f32) + norm_back(
        normed_two_grad, unit_two, inverse_two, gain_two
    )
    grad_low = stream_grad.astype(bf16)
    attended_grad = tick(project_rows(grad_low, out_tiles, seats), down_job)
    lefts, up_grads = after(
        ([normed_two, normed_two_next], [up_grad, up_grad_next]), attended_grad
    )
    rode = []
    up_job = Job(ffn_share(lefts, up_grads, 6, attended_grad, rode))
    grad_heads = after(rode[0].reshape(n * rows, -1), up_job.started)
    grad_heads = tick(grad_heads, gate_job)
    grad_heads = after(grad_heads, gate_job.started)
    back_hats = attention_backward(qkv, attended_heads, grad_heads, logs, parents, kv)
    back_hats = tick(back_hats, gate_job, up_job)
    back_hats = after(back_hats, up_job.started)
    back_hats_own = swap(back_hats.reshape(n, rows, -1))
    grad_low, down_next, after_attn = after((grad_low, down_next, after_attn), back_hats)
    out_job = Job(attn_share(grad_low, attended, None, 7))
    fence = tick(after(grad_low, out_job.started), up_job)
    mixed = (after_attn + down + down_next.astype(f32)).astype(bf16)
    mixed = shuffle_columns(mixed, absolute)
    inverse_one = inverse_rms(after(stream_low, back_hats).astype(f32))
    back_hats_own, inverse_one, mixed = after(
        (back_hats_own, inverse_one, mixed), fence, out_job.started
    )
    raw_grads, q_sum, k_sum = qkv_back(back_hats_own, raws, cosine, sine, gain_q, gain_k)
    raw_grads = tick(raw_grads, out_job)
    q_job = Job(attn_share(normed_one, after(raw_grads, out_job.started), 0, 8))
    raw_late = after(raw_grads, q_job.started)
    k_job = Job(attn_share(normed_one, raw_late, 1, 9))
    raw_late = tick(after(raw_late, k_job.started), q_job, out_job, up_job)
    raw_late = after(raw_late, q_job.started)
    normed_one_grad = project_columns([raw_late], [qkv_tiles], seats, depth, f32)
    normed_one_grad = tick(normed_one_grad, q_job, k_job, up_job, out_job)
    normed_one_grad = after(normed_one_grad, q_job.started, k_job.started)
    unit_one = stream_low.astype(f32) * inverse_one
    attn_gain_part = jnp.sum(normed_one_grad * unit_one, axis=0)
    tokens_grad = (
        stream_grad + norm_back(normed_one_grad, unit_one, inverse_one, gain_one)
    ).astype(bf16)
    tokens_grad = shuffle_columns(tokens_grad, absolute)

    parts = jnp.concatenate(
        [
            attn_gain_part.reshape(m, block),
            ffn_gain_part.reshape(m, block),
            jnp.take(q_sum.reshape(m, small), relative, axis=0),
            jnp.take(k_sum.reshape(m, small), relative, axis=0),
        ],
        axis=1,
    )
    size = m
    while size > 1:
        size //= 2
        parts = parts[:size] + over("wide", parts[size:], order[size])
    parts = after(parts, tokens_grad)
    step = 1
    while step < n:
        parts = parts + over("tp", parts, step)
        step *= 2
    sums = parts[0]
    gate_share, up_share = gate_job.finish(), up_job.finish()
    down_share, out_share = down_job.finish().T, out_job.finish().T
    q_share, k_share = q_job.finish(), k_job.finish()
    return (
        mixed,
        tokens_grad,
        sums[:block],
        q_share,
        k_share[:, : aw // 2],
        k_share[:, aw // 2 :],
        out_share,
        sums[2 * block : 2 * block + small],
        sums[2 * block + small :],
        sums[block : 2 * block],
        gate_share,
        up_share,
        down_share,
    )


def solution(mesh):
    both = P(("wide", "tp"), None)
    w, wt, tw = P("wide"), P("wide", "tp"), P("tp", "wide")
    return jax.shard_map(
        functools.partial(local, mesh.shape["wide"], mesh.shape["tp"]),
        mesh=mesh,
        in_specs=(both, both, w, w, w, w, wt, wt, wt, tw, w, w, w, wt, wt, tw),
        out_specs=(both, both, w, wt, wt, wt, tw, w, w, w, wt, wt, tw),
        check_vma=False,
    )
```
